512 devices in a mesh: gx: 16 (over y, x_hi, core), gy: 32 (over x_lo, z).
Axes of the slice: x: 4 (x_hi: 2, x_lo: 2; x = x_hi * 2 + x_lo), y: 4, z: 16, core: 2. Of those that a mesh axis runs over, the one named last changes fastest.
Arguments:
- basis: bfloat16 [32, 256, 256, 128], P(None, 'gx', 'gy'), may hold values from -6 to 6
- phase_ids: int32 [256, 256, 128], P('gx', 'gy'), may hold values from 0 to 7
- phase_stiffness: bfloat16 [8], replicated, may hold values from 0.099609375 to 10
- owner_map: int32 [16, 32], P('gx'), may hold values from 0 to 31, as said below
Outputs:
- owned_diagonal: float32 [16, 96, 32, 32], P('gx', 'gy')
- owned_coupling: float32 [16, 96, 8, 32, 32], P('gx', 'gy')
The draws below stay inside these ranges and needn't reach their ends.
Inputs may be any that keep to these rules, and one draw needn't show every extreme that they name: `owner_map`: in each grid row no owner holds more than 3 subdomains, and one owner holds exactly 3.
All inputs are finite; a program needn't handle non-finite values.
Results may differ from the reference program's by a relative error of at most 0.0003.
Values may be sent and summed in bfloat16 or wider, within the bound.
A program may use at most 64 MiB of HBM per device.

```python
import math
import jax
import jax.numpy as jnp
from jax import lax

K = 32
CX = 16
CY = 8
PHASES = 8
CAP = 3
SX = 16
SY = 32
NX = 256
NY = 256
NZ = 128


def draw_owner_map(key, part):
    key = jax.random.fold_in(key, 11)

    def line(row):
        sub = jax.random.fold_in(key, row)
        order = jax.random.permutation(jax.random.fold_in(sub, 1), SY)
        owners = jax.random.permutation(jax.random.fold_in(sub, 2), SY).astype(jnp.int32)
        steps = jnp.arange(SY, dtype=jnp.int32)
        later = jnp.minimum(1 + (steps - CAP) // 2, SY - 1)
        target = jnp.where(steps < CAP, owners[0], owners[jnp.clip(later, 0, SY - 1)])
        return jnp.zeros((SY,), jnp.int32).at[order].set(target)
    return jax.vmap(line)(jnp.arange(SX, dtype=jnp.int32))


def set_ends(drawn, own_key, low, largest):
    extent = drawn.shape
    index_at = [jax.random.randint(jax.random.fold_in(own_key, axis), (), 0, extent[axis]) for axis in range(len(extent))]
    drawn = drawn.at[tuple(index_at)].set(low)
    longest = extent.index(max(extent))
    index_at[longest] = (index_at[longest] + 1) % extent[longest]
    return drawn.at[tuple(index_at)].set(largest)


def level_of(key, extent, split, smallest, high):
    factor_of = 1.0
    for axis_at, shards_of in split:
        draws = jax.random.uniform(jax.random.fold_in(jax.random.fold_in(key, 6), axis_at), (shards_of,), jnp.float32, smallest / len(split), high / len(split))
        factor_of = factor_of * jnp.repeat(jnp.exp(draws), extent[axis_at] // shards_of).reshape((-1,) + (1,) * (len(extent) - 1 - axis_at))
    return factor_of


def gaussian(stream_key, extent, width, limit, pieces=(), kind=jnp.bfloat16):
    array = jax.random.normal(stream_key, extent, jnp.float32) * width
    if len(pieces) > 0:
        array = level_of(stream_key, extent, pieces, -0.22, 0.18) * array
    return jnp.clip(array, min=-limit, max=limit).astype(kind)


def setup_inputs(seed: int = 0) -> dict:
    arg_keys = jax.random.split(jax.random.key(seed), 5)
    return {
        "basis": gaussian(arg_keys[0], (K, NX, NY, NZ), 1.0, 6.0, ((1, 16), (2, 32))),
        "phase_ids": set_ends(jax.random.randint(arg_keys[1], (NX, NY, NZ), 0, PHASES), jax.random.fold_in(arg_keys[1], 1), 0, PHASES - 1).astype(jnp.int32),
        "phase_stiffness": jnp.clip(jnp.exp(jax.random.uniform(arg_keys[2], (PHASES,), jnp.float32, math.log(0.099609375), math.log(10.0))), 0.099609375, 10.0).astype(jnp.bfloat16),
        "owner_map": draw_owner_map(jax.random.fold_in(arg_keys[4], 71), 0),
    }


REACT = 0.1
REGIONS = ((-1, -1), (-1, 0), (-1, 1), (0, -1), (0, 1), (1, -1), (1, 0), (1, 1))


def region_block(padb, padk, sx, sy):
    wx = padb.shape[1]
    wy = padb.shape[2]
    depth = padb.shape[3] - 2
    inner_x = wx - 2
    inner_y = wy - 2
    x_lo = inner_x - 1 if sx == 1 else 0
    x_hi = 1 if sx == -1 else inner_x
    y_lo = inner_y - 1 if sy == 1 else 0
    y_hi = 1 if sy == -1 else inner_y
    len_x = x_hi - x_lo
    len_y = y_hi - y_lo
    window = padb[:, x_lo:x_hi + 2, y_lo:y_hi + 2, :]
    kwin = padk[x_lo:x_hi + 2, y_lo:y_hi + 2, :]
    pos_x = jnp.arange(x_lo, x_hi + 2)
    pos_y = jnp.arange(y_lo, y_hi + 2)
    reg_x = jnp.where(pos_x == 0, -1, jnp.where(pos_x == wx - 1, 1, 0))
    reg_y = jnp.where(pos_y == 0, -1, jnp.where(pos_y == wy - 1, 1, 0))
    mask = ((reg_x == sx)[:, None] & (reg_y == sy)[None, :]).astype(window.dtype)
    zfield = window * mask[None, :, :, None]
    centre = window[:, 1:1 + len_x, 1:1 + len_y, 1:1 + depth].astype(jnp.float32)
    kcell = kwin[1:1 + len_x, 1:1 + len_y, 1:1 + depth]
    total = jnp.zeros(centre.shape, jnp.float32)
    diagsum = jnp.zeros(kcell.shape, jnp.float32)
    for ox in (-1, 0, 1):
        for oy in (-1, 0, 1):
            for oz in (-1, 0, 1):
                if ox == 0 and oy == 0 and oz == 0:
                    continue
                coef = 1.0 / (9.0 * (ox * ox + oy * oy + oz * oz))
                kneigh = kwin[1 + ox:1 + ox + len_x, 1 + oy:1 + oy + len_y, 1 + oz:1 + oz + depth]
                weight = coef * 2.0 * kcell * kneigh / (kcell + kneigh)
                near = zfield[:, 1 + ox:1 + ox + len_x, 1 + oy:1 + oy + len_y, 1 + oz:1 + oz + depth]
                total = total - weight[None] * near.astype(jnp.float32)
                diagsum = diagsum + weight
    if sx == 0 and sy == 0:
        total = total + (diagsum + REACT * kcell)[None] * centre
    return jnp.einsum('kxyz,lxyz->kl', centre, total, precision=lax.Precision.HIGHEST)


def row_blocks(window, stiff):
    padb = jnp.pad(window, ((0, 0), (0, 0), (0, 0), (1, 1)))
    padk = jnp.pad(stiff.astype(jnp.float32), ((0, 0), (0, 0), (1, 1)))
    cells = (window.shape[1] - 2) * (window.shape[2] - 2) * window.shape[3]
    diagonal = region_block(padb, padk, 0, 0) / cells
    coupling = jnp.stack([region_block(padb, padk, sx, sy) for sx, sy in REGIONS])
    return diagonal, coupling


def reference(basis, phase_ids, phase_stiffness, owner_map):
    stiffness = phase_stiffness[phase_ids]
    padb = jnp.pad(basis, ((0, 0), (1, 1), (1, 1), (0, 0)))
    padk = jnp.pad(stiffness, ((1, 1), (1, 1), (0, 0)))

    def one(index):
        row = (index // SY).astype(jnp.int32)
        col = (index % SY).astype(jnp.int32)
        zero = jnp.zeros((), jnp.int32)
        window = lax.dynamic_slice(padb, (zero, row * CX, col * CY, zero), (K, CX + 2, CY + 2, NZ))
        wstiff = lax.dynamic_slice(padk, (row * CX, col * CY, zero), (CX + 2, CY + 2, NZ))
        return row_blocks(window, wstiff)

    diag_all, coup_all = lax.map(one, jnp.arange(SX * SY, dtype=jnp.int32))
    diag_all = diag_all.reshape(SX, SY, K, K)
    coup_all = coup_all.reshape(SX, SY, 8, K, K)
    column = jnp.arange(SY, dtype=jnp.int32)
    same = owner_map[:, None, :] == owner_map[:, :, None]
    before = column[None, :] < column[:, None]
    rank = jnp.sum((same & before[None]).astype(jnp.int32), axis=2)
    dest = owner_map * CAP + rank
    slots = jnp.arange(SY * CAP, dtype=jnp.int32)
    select = (dest[:, None, :] == slots[None, :, None]).astype(jnp.float32)
    owned_diagonal = jnp.einsum('isj,ijkl->iskl', select, diag_all, precision=lax.Precision.HIGHEST)
    owned_coupling = jnp.einsum('isj,ijrkl->isrkl', select, coup_all, precision=lax.Precision.HIGHEST)
    return owned_diagonal, owned_coupling
```

```python
import functools

import jax
import jax.numpy as jnp
from jax import lax
from jax.experimental import pallas as pl
from jax.experimental.pallas import tpu as pltpu
from jax.sharding import PartitionSpec as P

CAP = 3
REACT = 0.1
REGIONS = ((-1, -1), (-1, 0), (-1, 1), (0, -1), (0, 1), (1, -1), (1, 0), (1, 1))
CORNERS = ((-1, -1), (-1, 1), (1, -1), (1, 1))
OFFSETS = [
    (ox, oy, oz)
    for ox in (-1, 0, 1)
    for oy in (-1, 0, 1)
    for oz in (-1, 0, 1)
    if (ox, oy, oz) != (0, 0, 0)
]
INDEX = {o: i for i, o in enumerate(OFFSETS)}
HALF = [o for o in OFFSETS if o[2] == 1] + [(0, 1, 0), (1, -1, 0), (1, 0, 0), (1, 1, 0)]
MESH = pl.DeviceIdType.MESH
K, CX, CY, NZ = 32, 16, 8, 128
ROWS, COLS = 16, 32
LAST = (((1,), (1,)), ((), ()))


def split(value):
    high = value.astype(jnp.bfloat16)
    low = (value - high.astype(jnp.float32)).astype(jnp.bfloat16)
    return high, low


def kernel(
    basis,
    ids,
    phase,
    owner,
    out_diag,
    out_coup,
    raw,
    stage,
    zf,
    zs,
    zb,
    kp,
    kz,
    kface,
    kx,
    ky,
    hx,
    hy,
    hc,
    fx,
    fy,
    fc,
    weights,
    dsum,
    yb,
    piece,
    pieces,
    slots,
    owned,
    load_sem,
    ks_send,
    ks_recv,
    z_send,
    z_recv,
    one_send,
    one_recv,
    two_send,
    two_recv,
    local_sem,
):
    f32 = jnp.float32
    ax = lax.axis_index("gx")
    ay = lax.axis_index("gy")

    def device(dx, dy):
        return (lax.rem(ax + dx + ROWS, ROWS), lax.rem(ay + dy + COLS, COLS))

    loads = [
        pltpu.make_async_copy(
            basis.at[pl.ds(1024 * g, 1024)], raw.at[pl.ds(1024 * g, 1024)], load_sem.at[g]
        )
        for g in range(4)
    ]
    for copy in loads:
        copy.start()

    barrier = pltpu.get_barrier_semaphore()

    def greet(off, carry):
        pl.semaphore_signal(
            barrier, inc=1, device_id=(ax, lax.rem(ay + off, COLS)), device_id_type=MESH
        )
        return carry

    for dx, dy in REGIONS:
        if dx != 0:
            pl.semaphore_signal(barrier, inc=1, device_id=device(dx, dy), device_id_type=MESH)
    lax.fori_loop(1, COLS, greet, 0)

    table = phase[...].astype(f32)
    kp[...] = jnp.zeros_like(kp)
    for x in range(CX):
        cell = ids[x]
        value = jnp.zeros((CY, NZ), f32)
        for p in range(8):
            value = jnp.where(cell == p, table[0:1, p : p + 1], value)
        kp[x + 1, 8:16, :] = value
    for side, y in ((0, 0), (1, CY - 1)):
        for x in range(CX):
            kface[side, x : x + 1, :] = kp[x + 1, 8 + y : 9 + y, :]

    pl.semaphore_wait(barrier, COLS - 1 + 6)

    sends = []
    for i, (dx, dy) in enumerate(REGIONS):
        other = REGIONS.index((-dx, -dy))
        if dx == 0:
            src, dst = kface.at[0 if dy < 0 else 1], ky.at[0 if dy > 0 else 1]
        else:
            src, dst = kp.at[1 if dx < 0 else CX, pl.ds(8, 8), :], kx.at[other]
        sends.append(
            pltpu.make_async_remote_copy(
                src_ref=src,
                dst_ref=dst,
                send_sem=ks_send.at[i],
                recv_sem=ks_recv.at[other],
                device_id=device(dx, dy),
                device_id_type=MESH,
            )
        )
    for copy in sends:
        copy.start()

    for g in range(4):
        loads[g].wait()

        def widen(i, carry, g=g):
            at = pl.multiple_of(1024 * g + i * 128, 128)
            stage[pl.ds(at, 128), :] = raw[pl.ds(at, 128), :].astype(f32)
            return carry

        lax.fori_loop(0, 8, widen, 0)
    zero = jnp.zeros((8, K, NZ), f32)
    for edge in (0, CX + 1):
        zf[edge] = zero
        zs[edge] = zero

    def turn(x, carry):
        for y in range(CY):
            r = x * CY + y
            slab = jnp.concatenate(
                [stage[pl.ds(1024 * g + r, 8, stride=128), :] for g in range(4)], axis=0
            )
            zf[x + 1, y] = slab
            zs[x + 1, y] = pltpu.roll(slab, NZ - 1, 1)
            zb[x, y] = slab.astype(jnp.bfloat16)
        return carry

    lax.fori_loop(0, CX, turn, 0)

    moves = []
    for i, (dx, dy) in enumerate(REGIONS):
        other = REGIONS.index((-dx, -dy))
        x_at = 0 if dx < 0 else CX - 1
        y_at = 0 if dy < 0 else CY - 1
        if dx == 0:
            src, dst = zb.at[:, y_at], hy.at[0 if dy > 0 else 1]
        elif dy == 0:
            src, dst = zb.at[x_at], hx.at[0 if dx > 0 else 1]
        else:
            src, dst = zb.at[x_at, y_at], hc.at[CORNERS.index((-dx, -dy))]
        moves.append(
            pltpu.make_async_remote_copy(
                src_ref=src,
                dst_ref=dst,
                send_sem=z_send.at[i],
                recv_sem=z_recv.at[other],
                device_id=device(dx, dy),
                device_id_type=MESH,
            )
        )
    for i in (3, 4, 1, 6, 0, 2, 5, 7):
        moves[i].start()

    for copy in sends:
        copy.wait()
    low_x = (ax > 0).astype(f32)
    high_x = (ax < ROWS - 1).astype(f32)
    low_y = (ay > 0).astype(f32)
    high_y = (ay < COLS - 1).astype(f32)
    for dx, at, keep in ((-1, 0, low_x), (1, CX + 1, high_x)):
        kp[at, 8:16, :] = kx[REGIONS.index((dx, 0))] * keep
        kp[at, 7:8, :] = kx[REGIONS.index((dx, -1)), 7:8, :] * (keep * low_y)
        kp[at, 16:17, :] = kx[REGIONS.index((dx, 1)), 0:1, :] * (keep * high_y)
    for x in range(CX):
        kp[x + 1, 7:8, :] = ky[0, x : x + 1, :] * low_y
        kp[x + 1, 16:17, :] = ky[1, x : x + 1, :] * high_y
    lane = lax.broadcasted_iota(jnp.int32, (24, NZ), 1)
    for x in range(CX + 2):
        row = kp[x]
        kz[0, x] = jnp.where(lane == 0, 0.0, pltpu.roll(row, 1, 1))
        kz[1, x] = jnp.where(lane == NZ - 1, 0.0, pltpu.roll(row, NZ - 1, 1))

    def weigh(x, carry):
        own = kp[x + 1, 8:16, :]
        total = REACT * own
        for ox, oy, oz in OFFSETS:
            frame = kp if oz == 0 else kz.at[0 if oz < 0 else 1]
            near = frame[x + 1 + ox, 8 + oy : 16 + oy, :]
            coef = 2.0 / (9.0 * (ox * ox + oy * oy + oz * oz))
            weight = (coef * own) * near / (own + near)
            weights[INDEX[(ox, oy, oz)], x] = weight
            total = total + weight
        dsum[x] = 0.5 * total
        return carry

    lax.fori_loop(0, CX, weigh, 0)

    def interior(x, acc):
        for y in range(CY):
            value = dsum[x, y : y + 1, :] * zf[x + 1, y]
            for ox, oy, oz in HALF:
                if not 0 <= y + oy < CY:
                    continue
                field = zf if oz == 0 else zs
                w = weights[INDEX[(ox, oy, oz)], x, y : y + 1, :]
                value = value - w * field[x + 1 + ox, y + oy]
            high, low = split(value)
            yb[y, 0:K, :] = high
            yb[y, K : 2 * K, :] = low
        left = jnp.concatenate([zb[x, y] for y in range(CY)], axis=1)
        right = jnp.concatenate([yb[y] for y in range(CY)], axis=1)
        return acc + lax.dot_general(left, right, LAST, preferred_element_type=f32)

    acc = lax.fori_loop(0, CX, interior, jnp.zeros((K, 2 * K), f32))
    half = acc[:, :K] + acc[:, K:]
    diagonal = (half + half.T) * (1.0 / (CX * CY * NZ))

    for copy in moves:
        copy.wait()

    def spread(slab, dst, index):
        value = slab.astype(f32)
        dst[(1,) + index] = value
        dst[(0,) + index] = pltpu.roll(value, 1, 1)
        dst[(2,) + index] = pltpu.roll(value, NZ - 1, 1)

    edge = jnp.zeros((K, NZ), f32)
    for side in range(2):
        for y in range(CY):
            spread(hx[side, y], fx, (side, y))

        def spread_y(x, carry, side=side):
            spread(hy[side, x], fy, (side, x + 1))
            return carry

        lax.fori_loop(0, CX, spread_y, 0)
        for o in range(3):
            fy[o, side, 0] = edge
            fy[o, side, CX + 1] = edge
    for c in range(4):
        spread(hc[c], fc, (c,))

    blocks = {}

    def image(region, x, y, fetch):
        value = jnp.zeros((K, NZ), f32)
        for offset, field in fetch:
            value = value - weights[INDEX[offset], x, y : y + 1, :] * field
        return split(value)

    def finish(product):
        return product[:, :K] + product[:, K:]

    for side, dx in ((0, -1), (1, 1)):
        x = 0 if dx < 0 else CX - 1
        for y in range(CY):
            high, low = image(
                (dx, 0),
                x,
                y,
                [
                    ((dx, oy, oz), fx[oz + 1, side, y + oy])
                    for oy in (-1, 0, 1)
                    if 0 <= y + oy < CY
                    for oz in (-1, 0, 1)
                ],
            )
            yb[y, 0:K, :] = high
            yb[y, K : 2 * K, :] = low
        left = jnp.concatenate([zb[x, y] for y in range(CY)], axis=1)
        right = jnp.concatenate([yb[y] for y in range(CY)], axis=1)
        blocks[(dx, 0)] = finish(
            lax.dot_general(left, right, LAST, preferred_element_type=f32)
        )
    for side, dy in ((0, -1), (1, 1)):
        y = 0 if dy < 0 else CY - 1

        def face(x, carry, side=side, dy=dy, y=y):
            high, low = image(
                (0, dy),
                x,
                y,
                [
                    ((ox, dy, oz), fy[oz + 1, side, x + 1 + ox])
                    for ox in (-1, 0, 1)
                    for oz in (-1, 0, 1)
                ],
            )
            yb[x, 0:K, :] = high
            yb[x, K : 2 * K, :] = low
            return carry

        lax.fori_loop(0, CX, face, 0)
        left = jnp.concatenate([zb[x, y] for x in range(CX)], axis=1)
        right = jnp.concatenate([yb[x] for x in range(CX)], axis=1)
        blocks[(0, dy)] = finish(
            lax.dot_general(left, right, LAST, preferred_element_type=f32)
        )
    for c, (dx, dy) in enumerate(CORNERS):
        x = 0 if dx < 0 else CX - 1
        y = 0 if dy < 0 else CY - 1
        high, low = image(
            (dx, dy), x, y, [((dx, dy, oz), fc[oz + 1, c]) for oz in (-1, 0, 1)]
        )
        right = jnp.concatenate([high, low], axis=0)
        blocks[(dx, dy)] = finish(
            lax.dot_general(zb[x, y], right, LAST, preferred_element_type=f32)
        )

    width = COLS
    own_row = jnp.broadcast_to(owner[...], (width, width))
    i_sub = lax.broadcasted_iota(jnp.int32, (width, width), 0)
    i_lane = lax.broadcasted_iota(jnp.int32, (width, width), 1)
    own_f = own_row.astype(f32)
    own_col = jnp.sum(jnp.where(i_sub == i_lane, own_f, 0.0), axis=1, keepdims=True)
    before = (own_col == own_f) & (i_sub < i_lane)
    rank = jnp.sum(jnp.where(before, 1.0, 0.0), axis=0, keepdims=True)
    code = jnp.broadcast_to(own_f[0:1] * 4.0 + rank, (8, width)).astype(jnp.bfloat16)
    e_sub = lax.broadcasted_iota(jnp.int32, (width, NZ), 0)
    e_lane = lax.broadcasted_iota(jnp.int32, (width, NZ), 1)
    expand = jnp.where(e_lane // 4 == e_sub, 1.0, 0.0).astype(jnp.bfloat16)
    wide = jnp.dot(code, expand, preferred_element_type=f32)[0:1].astype(jnp.int32)
    wide_owner = wide // 4
    wide_rank = wide - wide_owner * 4
    lane1 = lax.broadcasted_iota(jnp.int32, (1, NZ), 1)
    part = lane1 - (lane1 // 4) * 4
    target = wide_owner * 8 + jnp.where(part < 2, wide_rank * 2 + part, 6)
    target = jnp.where(part < 3, target, -1)
    p_sub = lax.broadcasted_iota(jnp.int32, (COLS * 8, NZ), 0)
    route = jnp.where(p_sub == target, 1.0, 0.0).astype(jnp.bfloat16)
    my_rank = jnp.sum(
        jnp.where(lax.broadcasted_iota(jnp.int32, (1, width), 1) == ay, rank, 0.0),
        axis=1,
        keepdims=True,
    )
    quarter = (lax.broadcasted_iota(jnp.int32, (K, NZ), 1) // K).astype(f32)

    order = [blocks[t] for t in REGIONS]
    rows = [
        jnp.concatenate(order[:4], axis=1),
        jnp.concatenate(order[4:], axis=1),
        jnp.where(quarter == my_rank, jnp.concatenate([diagonal] * 4, axis=1), 0.0),
    ]
    flat = piece.reshape(4 * K, NZ)
    for l, value in enumerate(rows + [jnp.zeros((K, NZ), f32)]):
        flat[pl.ds(l, K, stride=4), :] = value

    def first(off, carry):
        to = lax.rem(ay + off, COLS)
        pltpu.make_async_remote_copy(
            src_ref=piece.at[to],
            dst_ref=pieces.at[ay],
            send_sem=one_send,
            recv_sem=one_recv,
            device_id=(ax, to),
            device_id_type=MESH,
        ).start()
        return carry

    lax.fori_loop(1, COLS, first, 0)
    keep = pltpu.make_async_copy(piece.at[ay], pieces.at[ay], local_sem.at[0])
    keep.start()
    keep.wait()
    many = pieces.at[pl.ds(0, COLS - 1)]
    pltpu.make_async_copy(many, many, one_recv).wait()

    got = pieces.reshape(4 * COLS, NZ)[...]
    a1 = got.astype(jnp.bfloat16)
    rest = got - a1.astype(f32)
    a2 = rest.astype(jnp.bfloat16)
    a3 = (rest - a2.astype(f32)).astype(jnp.bfloat16)
    slots[...] = (
        jnp.dot(route, a1, preferred_element_type=f32)
        + jnp.dot(route, a2, preferred_element_type=f32)
        + jnp.dot(route, a3, preferred_element_type=f32)
    ).reshape(COLS, 8, NZ)

    def second(off, carry):
        to = lax.rem(ay + off, COLS)
        pltpu.make_async_remote_copy(
            src_ref=slots.at[to],
            dst_ref=owned.at[ay],
            send_sem=two_send,
            recv_sem=two_recv,
            device_id=(ax, to),
            device_id_type=MESH,
        ).start()
        return carry

    lax.fori_loop(1, COLS, second, 0)
    keep = pltpu.make_async_copy(slots.at[ay], owned.at[ay], local_sem.at[1])
    keep.start()
    keep.wait()
    sent = piece.at[pl.ds(0, COLS - 1)]
    pltpu.make_async_copy(sent, sent, one_send).wait()
    many = owned.at[pl.ds(0, COLS - 1)]
    pltpu.make_async_copy(many, many, two_recv).wait()

    mine = owned.reshape(8 * COLS, NZ)
    for c in range(CAP):
        for half_row in range(2):
            value = mine[pl.ds(2 * c + half_row, K, stride=8), :]
            for q in range(4):
                out_coup[c, half_row * 4 + q] = value[:, q * K : (q + 1) * K]
    value = mine[pl.ds(6, K, stride=8), :]
    for c in range(CAP):
        out_diag[c] = value[:, c * K : (c + 1) * K]
    sent = slots.at[pl.ds(0, COLS - 1)]
    pltpu.make_async_copy(sent, sent, two_send).wait()


def shards(basis, phase_ids, phase_stiffness, owner_map):
    f32, bf16 = jnp.float32, jnp.bfloat16
    vmem = pltpu.VMEM
    dma = pltpu.SemaphoreType.DMA
    whole = pl.BlockSpec(memory_space=pltpu.VMEM)
    diag, coup = pl.pallas_call(
        kernel,
        out_shape=(
            jax.ShapeDtypeStruct((CAP, K, K), f32),
            jax.ShapeDtypeStruct((CAP, 8, K, K), f32),
        ),
        in_specs=[pl.BlockSpec(memory_space=pl.ANY), whole, whole, whole],
        out_specs=(whole, whole),
        scratch_shapes=[
            vmem((K * CX * CY, NZ), bf16),
            vmem((K * CX * CY, NZ), f32),
            vmem((CX + 2, CY, K, NZ), f32),
            vmem((CX + 2, CY, K, NZ), f32),
            vmem((CX, CY, K, NZ), bf16),
            vmem((CX + 2, 24, NZ), f32),
            vmem((2, CX + 2, 24, NZ), f32),
            vmem((2, CX, NZ), f32),
            vmem((8, 8, NZ), f32),
            vmem((2, CX, NZ), f32),
            vmem((2, CY, K, NZ), bf16),
            vmem((2, CX, K, NZ), bf16),
            vmem((4, K, NZ), bf16),
            vmem((3, 2, CY, K, NZ), f32),
            vmem((3, 2, CX + 2, K, NZ), f32),
            vmem((3, 4, K, NZ), f32),
            vmem((26, CX, CY, NZ), f32),
            vmem((CX, CY, NZ), f32),
            vmem((CX, 2 * K, NZ), bf16),
            vmem((K, 4, NZ), f32),
            vmem((COLS, 4, NZ), f32),
            vmem((COLS, 8, NZ), f32),
            vmem((COLS, 8, NZ), f32),
            dma((4,)),
            dma((8,)),
            dma((8,)),
            dma((8,)),
            dma((8,)),
            dma,
            dma,
            dma,
            dma,
            dma((2,)),
        ],
        compiler_params=pltpu.CompilerParams(
            collective_id=0, has_side_effects=True, vmem_limit_bytes=48 * 1024 * 1024
        ),
    )(
        basis.reshape(K * CX * CY, NZ),
        phase_ids,
        phase_stiffness.reshape(1, 8),
        owner_map,
    )
    return diag[None], coup[None]


def solution(mesh):
    return jax.shard_map(
        shards,
        mesh=mesh,
        in_specs=(P(None, "gx", "gy", None), P("gx", "gy", None), P(), P("gx", None)),
        out_specs=(P("gx", "gy", None, None), P("gx", "gy", None, None, None)),
        check_vma=False,
    )
```

```python
import functools

import jax
import jax.numpy as jnp
from jax import lax
from jax.experimental import pallas as pl
from jax.experimental.pallas import tpu as pltpu
from jax.sharding import PartitionSpec as P

CAP = 3
REACT = 0.1
REGIONS = ((-1, -1), (-1, 0), (-1, 1), (0, -1), (0, 1), (1, -1), (1, 0), (1, 1))
CORNERS = ((-1, -1), (-1, 1), (1, -1), (1, 1))
OFFSETS = [
    (ox, oy, oz)
    for ox in (-1, 0, 1)
    for oy in (-1, 0, 1)
    for oz in (-1, 0, 1)
    if (ox, oy, oz) != (0, 0, 0)
]
HALF = [o for o in OFFSETS if o[2] == 1] + [(0, 1, 0), (1, -1, 0), (1, 0, 0), (1, 1, 0)]
MESH = pl.DeviceIdType.MESH
K, CX, CY, NZ = 32, 16, 8, 128
ROWS, COLS = 16, 32
PITCH = 136
LAST = (((1,), (1,)), ((), ()))


def split(value):
    high = value.astype(jnp.bfloat16)
    low = (value - high.astype(jnp.float32)).astype(jnp.bfloat16)
    return high, low


def kernel(
    basis,
    ids_hbm,
    phase_hbm,
    owner_hbm,
    out_diag,
    out_coup,
    raw,
    ids,
    phase,
    owner,
    stage,
    zf,
    zs,
    zb,
    zmx,
    zmy,
    kp,
    kz,
    kx,
    ky,
    kface,
    frame_x,
    frame_y,
    frame_own,
    hx,
    hy,
    hc,
    weights,
    dsum,
    wx,
    wy,
    yb,
    ex,
    ey,
    gx,
    gy,
    gc,
    piece,
    pieces,
    slots,
    owned,
    load_sem,
    ks_send,
    ks_recv,
    z_send,
    z_recv,
    one_send,
    one_recv,
    two_send,
    two_recv,
    local_sem,
):
    f32, bf16 = jnp.float32, jnp.bfloat16
    ax = lax.axis_index("gx")
    ay = lax.axis_index("gy")
    parity = lax.rem(ax, 2)
    parity_f = parity.astype(f32)

    def device(dx, dy):
        return (lax.rem(ax + dx + ROWS, ROWS), lax.rem(ay + dy + COLS, COLS))

    small = [
        pltpu.make_async_copy(ids_hbm, ids, load_sem.at[4]),
        pltpu.make_async_copy(phase_hbm, phase, load_sem.at[5]),
        pltpu.make_async_copy(owner_hbm, owner, load_sem.at[6]),
    ]
    loads = [
        pltpu.make_async_copy(
            basis.at[pl.ds(1024 * g, 1024)], raw.at[pl.ds(1024 * g, 1024)], load_sem.at[g]
        )
        for g in range(4)
    ]
    for copy in small + loads:
        copy.start()

    barrier = pltpu.get_barrier_semaphore()

    def greet(off, carry):
        pl.semaphore_signal(
            barrier, inc=1, device_id=(ax, lax.rem(ay + off, COLS)), device_id_type=MESH
        )
        return carry

    for dx, dy in REGIONS:
        if dx != 0:
            pl.semaphore_signal(barrier, inc=1, device_id=device(dx, dy), device_id_type=MESH)
    lax.fori_loop(1, COLS, greet, 0)

    kp[...] = jnp.zeros_like(kp)
    frame_own[...] = jnp.zeros_like(frame_own)
    frame_x[...] = jnp.zeros_like(frame_x)
    frame_y[...] = jnp.zeros_like(frame_y)
    zero = jnp.zeros((8, K, NZ), f32)
    for edge in (0, CX + 1):
        zf[edge] = zero
        zs[edge] = zero
    zmy[0] = zero[0]
    zmy[CX + 1] = zero[0]
    yb[0] = jnp.zeros((CY, 2 * K, NZ), bf16)

    for copy in small:
        copy.wait()
    table = phase[...].astype(f32)
    for x in range(CX):
        cell = ids[x]
        value = jnp.zeros((CY, NZ), f32)
        for p in range(8):
            value = jnp.where(cell == p, table[0:1, p : p + 1], value)
        kp[x + 1, 8:16, :] = value
    for side, y in ((0, 0), (1, CY - 1)):
        for x in range(CX):
            kface[side, x : x + 1, :] = kp[x + 1, 8 + y : 9 + y, :]

    for g in range(4):
        loads[g].wait()

        def widen(i, carry, g=g):
            at = pl.multiple_of(1024 * g + i * 128, 128)
            to = pl.multiple_of(PITCH * 8 * g + i * PITCH, 8)
            stage[pl.ds(to, 128), :] = raw[pl.ds(at, 128), :].astype(f32)
            return carry

        lax.fori_loop(0, 8, widen, 0)

    def turn(x, carry):
        for y in range(CY):
            r = x * CY + y
            slab = jnp.concatenate(
                [stage[pl.ds(8 * PITCH * g + r, 8, stride=PITCH), :] for g in range(4)], axis=0
            )
            zf[x + 1, y] = slab
            zs[x + 1, y] = pltpu.roll(slab, NZ - 1, 1)
            zb[x, y] = slab.astype(bf16)
        return carry

    lax.fori_loop(0, CX, turn, 0)

    pl.semaphore_wait(barrier, COLS - 1 + 6)

    sends = []
    for i, (dx, dy) in enumerate(REGIONS):
        other = REGIONS.index((-dx, -dy))
        if dx == 0:
            src, dst = kface.at[0 if dy < 0 else 1], ky.at[0 if dy > 0 else 1]
        else:
            src, dst = kp.at[1 if dx < 0 else CX, pl.ds(8, 8), :], kx.at[other]
        sends.append(
            pltpu.make_async_remote_copy(
                src_ref=src,
                dst_ref=dst,
                send_sem=ks_send.at[i],
                recv_sem=ks_recv.at[other],
                device_id=device(dx, dy),
                device_id_type=MESH,
            )
        )
    moves = [
        pltpu.make_async_remote_copy(
            src_ref=zb.at[:, 7 - 7 * parity],
            dst_ref=hy,
            send_sem=z_send.at[0],
            recv_sem=z_recv.at[0],
            device_id=(ax, lax.rem(ay + 1 - 2 * parity + COLS, COLS)),
            device_id_type=MESH,
        )
    ]
    for side, dx in ((0, -1), (1, 1)):
        moves.append(
            pltpu.make_async_remote_copy(
                src_ref=zb.at[0 if dx < 0 else CX - 1],
                dst_ref=hx.at[1 - side],
                send_sem=z_send.at[1 + side],
                recv_sem=z_recv.at[2 - side],
                device_id=device(dx, 0),
                device_id_type=MESH,
            )
        )
    for c, (dx, dy) in enumerate(CORNERS):
        moves.append(
            pltpu.make_async_remote_copy(
                src_ref=zb.at[0 if dx < 0 else CX - 1, 0 if dy < 0 else CY - 1],
                dst_ref=hc.at[3 - c],
                send_sem=z_send.at[3 + c],
                recv_sem=z_recv.at[6 - c],
                device_id=device(dx, dy),
                device_id_type=MESH,
            )
        )
    for copy in sends + moves:
        copy.start()

    def harmonic(own, near, o):
        coef = 2.0 / (9.0 * (o[0] * o[0] + o[1] * o[1] + o[2] * o[2]))
        return (coef * own) * near / jnp.maximum(own + near, 0.05)

    def below(value):
        lane = lax.broadcasted_iota(jnp.int32, value.shape, 1)
        return jnp.where(lane == 0, 0.0, pltpu.roll(value, 1, 1))

    def above(value):
        lane = lax.broadcasted_iota(jnp.int32, value.shape, 1)
        return jnp.where(lane == NZ - 1, 0.0, pltpu.roll(value, NZ - 1, 1))

    for x in range(CX + 2):
        row = kp[x]
        kz[0, x] = below(row)
        kz[1, x] = row
        kz[2, x] = above(row)

    def weigh(x, carry):
        own = kp[x + 1, 8:16, :]
        total = REACT * own
        for o in OFFSETS:
            near = kz[o[2] + 1, x + 1 + o[0], 8 + o[1] : 16 + o[1], :]
            weight = harmonic(own, near, o)
            if o in HALF:
                weights[HALF.index(o), x] = weight
            total = total + weight
        dsum[x] = 0.5 * total
        return carry

    lax.fori_loop(0, CX, weigh, 0)

    def contract(x, slot):
        left = jnp.concatenate([yb[slot, y] for y in range(CY)], axis=1)
        right = jnp.concatenate([zb[x, y] for y in range(CY)], axis=1)
        return lax.dot_general(left, right, LAST, preferred_element_type=f32)

    def interior(x, acc):
        acc = acc + contract(jnp.maximum(x - 1, 0), x)
        for y in range(CY):
            value = dsum[x, y : y + 1, :] * zf[x + 1, y]
            for i, (ox, oy, oz) in enumerate(HALF):
                if not 0 <= y + oy < CY:
                    continue
                field = zf if oz == 0 else zs
                w = weights[i, x, y : y + 1, :]
                value = value - w * field[x + 1 + ox, y + oy]
            high, low = split(value)
            yb[x + 1, y, 0:K, :] = high
            yb[x + 1, y, K : 2 * K, :] = low
        return acc

    acc = lax.fori_loop(0, CX, interior, jnp.zeros((2 * K, K), f32))
    acc = acc + contract(CX - 1, CX)

    for copy in sends:
        copy.wait()
    low_x = (ax > 0).astype(f32)
    high_x = (ax < ROWS - 1).astype(f32)
    low_y = (ay > 0).astype(f32)
    high_y = (ay < COLS - 1).astype(f32)
    for side, dx, keep in ((0, -1, low_x), (1, 1, high_x)):
        near = kx[REGIONS.index((dx, 0))] * keep
        frame_x[1, side, 8:16, :] = near
    for side, dy, keep in ((0, -1, low_y), (1, 1, high_y)):
        y = 7 if dy < 0 else 0
        frame_y[1, side, 8:24, :] = ky[side] * keep
        for at, dx, keep_x in ((7, -1, low_x), (24, 1, high_x)):
            corner = kx[REGIONS.index((dx, dy)), y : y + 1, :]
            frame_y[1, side, at : at + 1, :] = corner * (keep * keep_x)
        frame_own[1, side, 8:24, :] = kface[side]
    for frame in (frame_x, frame_y, frame_own):
        for side in range(2):
            row = frame[1, side]
            frame[0, side] = below(row)
            frame[2, side] = above(row)

    NINE = [(i, j) for i in (-1, 0, 1) for j in (-1, 0, 1)]
    for side, dx in ((0, -1), (1, 1)):
        x = 0 if dx < 0 else CX - 1
        own = kp[x + 1, 8:16, :]
        total = jnp.zeros_like(own)
        for oy, oz in NINE:
            near = frame_x[oz + 1, side, 8 + oy : 16 + oy, :]
            total = total + harmonic(own, near, (dx, oy, oz))
        for y in range(CY):
            high, low = split(total[y : y + 1] * zf[x + 1, y])
            ex[side, y, 0:K, :] = high
            ex[side, y, K : 2 * K, :] = low
    for side, dy in ((0, -1), (1, 1)):
        own = kface[side]
        total = jnp.zeros_like(own)
        for ox, oz in NINE:
            near = frame_y[oz + 1, side, 8 + ox : 24 + ox, :]
            total = total + harmonic(own, near, (ox, dy, oz))
        for x in range(CX):
            high, low = split(total[x : x + 1] * zf[x + 1, 0 if dy < 0 else CY - 1])
            ey[side, x, 0:K, :] = high
            ey[side, x, K : 2 * K, :] = low
    outer = jnp.zeros((2 * K, K), f32)
    for side in range(2):
        x = 0 if side == 0 else CX - 1
        y = 0 if side == 0 else CY - 1
        outer = outer + lax.dot_general(
            jnp.concatenate([ex[side, i] for i in range(CY)], axis=1),
            jnp.concatenate([zb[x, i] for i in range(CY)], axis=1),
            LAST,
            preferred_element_type=f32,
        )
        outer = outer + lax.dot_general(
            jnp.concatenate([ey[side, i] for i in range(CX)], axis=1),
            jnp.concatenate([zb[i, y] for i in range(CX)], axis=1),
            LAST,
            preferred_element_type=f32,
        )
    half = acc[:K] + acc[K:]
    diagonal = (half + half.T + outer[:K] + outer[K:]) * (1.0 / (CX * CY * NZ))

    for side, dx in ((0, -1), (1, 1)):
        x = 0 if dx < 0 else CX - 1
        for y in range(CY):
            zmx[side, y] = pltpu.roll(zf[x + 1, y], 1, 1)
        own = frame_x[1, side, 8:16, :]
        for i, (oy, oz) in enumerate(NINE):
            near = kz[oz + 1, x + 1, 8 + oy : 16 + oy, :]
            wx[side, i] = harmonic(own, near, (dx, oy, oz))
        for y in range(CY):
            value = jnp.zeros((K, NZ), f32)
            for i, (oy, oz) in enumerate(NINE):
                if not 0 <= y + oy < CY:
                    continue
                field = (zmx[side, y + oy], zf[x + 1, y + oy], zs[x + 1, y + oy])[oz + 1]
                value = value - wx[side, i, y : y + 1, :] * field
            high, low = split(value)
            gx[side, y, 0:K, :] = high
            gx[side, y, K : 2 * K, :] = low
    for c, (dx, dy) in enumerate(CORNERS):
        x = 0 if dx < 0 else CX - 1
        y = 0 if dy < 0 else CY - 1
        side = 0 if dx < 0 else 1
        at = 7 if dx < 0 else 24
        own = frame_y[1, 0 if dy < 0 else 1, at : at + 1, :]
        value = jnp.zeros((K, NZ), f32)
        for oz in (-1, 0, 1):
            near = kz[oz + 1, x + 1, 8 + y : 9 + y, :]
            field = (zmx[side, y], zf[x + 1, y], zs[x + 1, y])[oz + 1]
            value = value - harmonic(own, near, (dx, dy, oz)) * field
        high, low = split(value)
        gc[c, 0:K, :] = high
        gc[c, K : 2 * K, :] = low
    y_edge = 7 * parity
    own = frame_y[1, parity, 8:24, :]
    for i, (ox, oz) in enumerate(NINE):
        near = frame_own[oz + 1, parity, 8 + ox : 24 + ox, :]
        wy[i] = harmonic(own, near, (ox, 1, oz))

    def lower(x, carry):
        zmy[x + 1] = pltpu.roll(zf[x + 1, y_edge], 1, 1)
        return carry

    lax.fori_loop(0, CX, lower, 0, unroll=4)

    def face(x, carry):
        value = jnp.zeros((K, NZ), f32)
        for i, (ox, oz) in enumerate(NINE):
            at = x + 1 + ox
            field = (zmy[at], zf[at, y_edge], zs[at, y_edge])[oz + 1]
            value = value - wy[i, pl.ds(x, 1), :] * field
        high, low = split(value)
        gy[x, 0:K, :] = high
        gy[x, K : 2 * K, :] = low
        return carry

    lax.fori_loop(0, CX, face, 0, unroll=4)

    width = COLS
    own_row = jnp.broadcast_to(owner[...], (width, width))
    i_sub = lax.broadcasted_iota(jnp.int32, (width, width), 0)
    i_lane = lax.broadcasted_iota(jnp.int32, (width, width), 1)
    own_f = own_row.astype(f32)
    own_col = jnp.sum(jnp.where(i_sub == i_lane, own_f, 0.0), axis=1, keepdims=True)
    before = (own_col == own_f) & (i_sub < i_lane)
    rank = jnp.sum(jnp.where(before, 1.0, 0.0), axis=0, keepdims=True)
    code = jnp.broadcast_to(own_f[0:1] * 4.0 + rank, (8, width)).astype(bf16)
    e_sub = lax.broadcasted_iota(jnp.int32, (width, NZ), 0)
    e_lane = lax.broadcasted_iota(jnp.int32, (width, NZ), 1)
    step = 2 * parity - 1
    e_from = e_lane // 4 + jnp.where(e_lane % 4 == 3, step, 0)
    expand = jnp.where(e_from == e_sub, 1.0, 0.0).astype(bf16)
    wide = jnp.dot(code, expand, preferred_element_type=f32)[0:1].astype(jnp.int32)
    wide_owner = wide // 4
    wide_rank = wide - wide_owner * 4
    lane1 = lax.broadcasted_iota(jnp.int32, (1, NZ), 1)
    part = lane1 % 4
    target = wide_owner * 8 + wide_rank * 2 + jnp.where(part == 3, 1 - parity, part)
    target = jnp.where(part == 2, wide_owner * 8 + 6, target)
    end = (lane1 // 4 + step < 0) | (lane1 // 4 + step >= width)
    target = jnp.where((part == 3) & end, -1, target)
    p_sub = lax.broadcasted_iota(jnp.int32, (COLS * 8, NZ), 0)
    route = jnp.where(p_sub == target, 1.0, 0.0).astype(bf16)
    my_rank = jnp.sum(
        jnp.where(lax.broadcasted_iota(jnp.int32, (1, width), 1) == ay, rank, 0.0),
        axis=1,
        keepdims=True,
    )
    quarter = (lax.broadcasted_iota(jnp.int32, (K, NZ), 1) // K).astype(f32)

    for copy in moves:
        copy.wait()

    def meet(left, right):
        product = lax.dot_general(left, right, LAST, preferred_element_type=f32)
        return product[:K] + product[K:]

    blocks = {}
    for side, dx in ((0, -1), (1, 1)):
        blocks[(dx, 0)] = meet(
            jnp.concatenate([gx[side, y] for y in range(CY)], axis=1),
            jnp.concatenate([hx[side, y] for y in range(CY)], axis=1),
        )
    for c, region in enumerate(CORNERS):
        blocks[region] = meet(gc[c], hc[c])
    across = meet(
        jnp.concatenate([gy[x] for x in range(CX)], axis=1),
        jnp.concatenate([hy[x] for x in range(CX)], axis=1),
    )
    back = across.T
    none = jnp.zeros_like(back)
    rows = [
        jnp.concatenate(
            [blocks[(-1, -1)], blocks[(-1, 0)], blocks[(-1, 1)], across * (1.0 - parity_f)],
            axis=1,
        ),
        jnp.concatenate(
            [across * parity_f, blocks[(1, -1)], blocks[(1, 0)], blocks[(1, 1)]], axis=1
        ),
        jnp.where(quarter == my_rank, jnp.concatenate([diagonal] * 4, axis=1), 0.0),
        jnp.concatenate([back * (1.0 - parity_f), none, none, back * parity_f], axis=1),
    ]
    flat = piece.reshape(4 * K, NZ)
    for l, value in enumerate(rows):
        flat[pl.ds(l, K, stride=4), :] = value

    def first(off, carry):
        to = lax.rem(ay + off, COLS)
        pltpu.make_async_remote_copy(
            src_ref=piece.at[to],
            dst_ref=pieces.at[ay],
            send_sem=one_send,
            recv_sem=one_recv,
            device_id=(ax, to),
            device_id_type=MESH,
        ).start()
        return carry

    lax.fori_loop(1, COLS, first, 0)
    keep = pltpu.make_async_copy(piece.at[ay], pieces.at[ay], local_sem.at[0])
    keep.start()
    keep.wait()
    many = pieces.at[pl.ds(0, COLS - 1)]
    pltpu.make_async_copy(many, many, one_recv).wait()

    got = pieces.reshape(4 * COLS, NZ)[...]
    a1 = got.astype(jnp.bfloat16)
    rest = got - a1.astype(f32)
    a2 = rest.astype(jnp.bfloat16)
    a3 = (rest - a2.astype(f32)).astype(jnp.bfloat16)
    slots[...] = (
        jnp.dot(route, a1, preferred_element_type=f32)
        + jnp.dot(route, a2, preferred_element_type=f32)
        + jnp.dot(route, a3, preferred_element_type=f32)
    ).reshape(COLS, 8, NZ)

    def second(off, carry):
        to = lax.rem(ay + off, COLS)
        pltpu.make_async_remote_copy(
            src_ref=slots.at[to],
            dst_ref=owned.at[ay],
            send_sem=two_send,
            recv_sem=two_recv,
            device_id=(ax, to),
            device_id_type=MESH,
        ).start()
        return carry

    lax.fori_loop(1, COLS, second, 0)
    keep = pltpu.make_async_copy(slots.at[ay], owned.at[ay], local_sem.at[1])
    keep.start()
    keep.wait()
    sent = piece.at[pl.ds(0, COLS - 1)]
    pltpu.make_async_copy(sent, sent, one_send).wait()
    many = owned.at[pl.ds(0, COLS - 1)]
    pltpu.make_async_copy(many, many, two_recv).wait()

    mine = owned.reshape(8 * COLS, NZ)
    for c in range(CAP):
        for half_row in range(2):
            value = mine[pl.ds(2 * c + half_row, K, stride=8), :]
            for q in range(4):
                out_coup[c, half_row * 4 + q] = value[:, q * K : (q + 1) * K]
    value = mine[pl.ds(6, K, stride=8), :]
    for c in range(CAP):
        out_diag[c] = value[:, c * K : (c + 1) * K]
    sent = slots.at[pl.ds(0, COLS - 1)]
    pltpu.make_async_copy(sent, sent, two_send).wait()


def shards(basis, phase_ids, phase_stiffness, owner_map):
    f32, bf16 = jnp.float32, jnp.bfloat16
    vmem = pltpu.VMEM
    dma = pltpu.SemaphoreType.DMA
    whole = pl.BlockSpec(memory_space=pltpu.VMEM)
    diag, coup = pl.pallas_call(
        kernel,
        out_shape=(
            jax.ShapeDtypeStruct((CAP, K, K), f32),
            jax.ShapeDtypeStruct((CAP, 8, K, K), f32),
        ),
        in_specs=[pl.BlockSpec(memory_space=pltpu.HBM)] * 4,
        out_specs=(whole, whole),
        scratch_shapes=[
            vmem((K * CX * CY, NZ), bf16),
            vmem((CX, CY, NZ), jnp.int32),
            vmem((1, 8), bf16),
            vmem((1, COLS), jnp.int32),
            vmem((K * PITCH, NZ), f32),
            vmem((CX + 2, CY, K, NZ), f32),
            vmem((CX + 2, CY, K, NZ), f32),
            vmem((CX, CY, K, NZ), bf16),
            vmem((2, CY, K, NZ), f32),
            vmem((CX + 2, K, NZ), f32),
            vmem((CX + 2, 24, NZ), f32),
            vmem((3, CX + 2, 24, NZ), f32),
            vmem((8, 8, NZ), f32),
            vmem((2, CX, NZ), f32),
            vmem((2, CX, NZ), f32),
            vmem((3, 2, 24, NZ), f32),
            vmem((3, 2, 32, NZ), f32),
            vmem((3, 2, 32, NZ), f32),
            vmem((2, CY, K, NZ), bf16),
            vmem((CX, K, NZ), bf16),
            vmem((4, K, NZ), bf16),
            vmem((13, CX, CY, NZ), f32),
            vmem((CX, CY, NZ), f32),
            vmem((2, 9, CY, NZ), f32),
            vmem((9, CX, NZ), f32),
            vmem((CX + 1, CY, 2 * K, NZ), bf16),
            vmem((2, CY, 2 * K, NZ), bf16),
            vmem((2, CX, 2 * K, NZ), bf16),
            vmem((2, CY, 2 * K, NZ), bf16),
            vmem((CX, 2 * K, NZ), bf16),
            vmem((4, 2 * K, NZ), bf16),
            vmem((K, 4, NZ), f32),
            vmem((COLS, 4, NZ), f32),
            vmem((COLS, 8, NZ), f32),
            vmem((COLS, 8, NZ), f32),
            dma((7,)),
            dma((8,)),
            dma((8,)),
            dma((7,)),
            dma((7,)),
            dma,
            dma,
            dma,
            dma,
            dma((2,)),
        ],
        compiler_params=pltpu.CompilerParams(
            collective_id=0, has_side_effects=True, vmem_limit_bytes=60 * 1024 * 1024
        ),
    )(
        basis.reshape(K * CX * CY, NZ),
        phase_ids,
        phase_stiffness.reshape(1, 8),
        owner_map,
    )
    return diag[None], coup[None]


def solution(mesh):
    return jax.shard_map(
        shards,
        mesh=mesh,
        in_specs=(P(None, "gx", "gy", None), P("gx", "gy", None), P(), P("gx", None)),
        out_specs=(P("gx", "gy", None, None), P("gx", "gy", None, None, None)),
        check_vma=False,
    )
```

```python
import functools

import jax
import jax.numpy as jnp
from jax import lax
from jax.experimental import pallas as pl
from jax.experimental.pallas import tpu as pltpu
from jax.sharding import PartitionSpec as P

CAP = 3
REACT = 0.1
REGIONS = ((-1, -1), (-1, 0), (-1, 1), (0, -1), (0, 1), (1, -1), (1, 0), (1, 1))
CORNERS = ((-1, -1), (-1, 1), (1, -1), (1, 1))
OFFSETS = [
    (ox, oy, oz)
    for ox in (-1, 0, 1)
    for oy in (-1, 0, 1)
    for oz in (-1, 0, 1)
    if (ox, oy, oz) != (0, 0, 0)
]
HALF = [o for o in OFFSETS if o[2] == 1] + [(0, 1, 0), (1, -1, 0), (1, 0, 0), (1, 1, 0)]
MESH = pl.DeviceIdType.MESH
K, CX, CY, NZ = 32, 16, 8, 128
ROWS, COLS = 16, 32
PITCH = 136
LEVELS = 32000.0
LAST = (((1,), (1,)), ((), ()))


def split(value):
    high = value.astype(jnp.bfloat16)
    low = (value - high.astype(jnp.float32)).astype(jnp.bfloat16)
    return high, low


def kernel(
    basis,
    ids_hbm,
    phase_hbm,
    owner_hbm,
    out,
    raw,
    ids,
    phase,
    owner,
    stage,
    zf,
    zs,
    zb,
    zmx,
    zmy,
    kp,
    kz,
    kx,
    ky,
    kface,
    frame_x,
    frame_y,
    frame_own,
    hx,
    hy,
    hc,
    weights,
    dsum,
    wx,
    wy,
    yb,
    ex,
    ey,
    gx,
    gy,
    gc,
    piece,
    pieces,
    words,
    slots,
    owned,
    load_sem,
    ks_send,
    ks_recv,
    z_send,
    z_recv,
    one_send,
    one_recv,
    two_send,
    two_recv,
    local_sem,
):
    f32, bf16 = jnp.float32, jnp.bfloat16
    ax = lax.axis_index("gx")
    ay = lax.axis_index("gy")
    parity = lax.rem(ax, 2)
    parity_f = parity.astype(f32)

    def device(dx, dy):
        return (lax.rem(ax + dx + ROWS, ROWS), lax.rem(ay + dy + COLS, COLS))

    small = [
        pltpu.make_async_copy(ids_hbm, ids, load_sem.at[4]),
        pltpu.make_async_copy(phase_hbm, phase, load_sem.at[5]),
        pltpu.make_async_copy(owner_hbm, owner, load_sem.at[6]),
    ]
    loads = [
        pltpu.make_async_copy(
            basis.at[pl.ds(1024 * g, 1024)], raw.at[pl.ds(1024 * g, 1024)], load_sem.at[g]
        )
        for g in range(4)
    ]
    for copy in small + loads:
        copy.start()

    barrier = pltpu.get_barrier_semaphore()

    def greet(off, carry):
        pl.semaphore_signal(
            barrier, inc=1, device_id=(ax, lax.rem(ay + off, COLS)), device_id_type=MESH
        )
        return carry

    for dx, dy in REGIONS:
        if dx != 0:
            pl.semaphore_signal(barrier, inc=1, device_id=device(dx, dy), device_id_type=MESH)
    lax.fori_loop(1, COLS, greet, 0)

    kp[...] = jnp.zeros_like(kp)
    frame_own[...] = jnp.zeros_like(frame_own)
    frame_x[...] = jnp.zeros_like(frame_x)
    frame_y[...] = jnp.zeros_like(frame_y)
    zero = jnp.zeros((8, K, NZ), f32)
    for edge in (0, CX + 1):
        zf[edge] = zero
        zs[edge] = zero
    zmy[0] = zero[0]
    zmy[CX + 1] = zero[0]
    yb[0] = jnp.zeros((CY, 2 * K, NZ), bf16)

    for copy in small:
        copy.wait()
    table = phase[...].astype(f32)
    for x in range(CX):
        cell = ids[x]
        value = jnp.zeros((CY, NZ), f32)
        for p in range(8):
            value = jnp.where(cell == p, table[0:1, p : p + 1], value)
        kp[x + 1, 8:16, :] = value
    for side, y in ((0, 0), (1, CY - 1)):
        for x in range(CX):
            kface[side, x : x + 1, :] = kp[x + 1, 8 + y : 9 + y, :]

    for g in range(4):
        loads[g].wait()

        def widen(i, carry, g=g):
            at = pl.multiple_of(1024 * g + i * 128, 128)
            to = pl.multiple_of(PITCH * 8 * g + i * PITCH, 8)
            stage[pl.ds(to, 128), :] = raw[pl.ds(at, 128), :].astype(f32)
            return carry

        lax.fori_loop(0, 8, widen, 0)

    def turn(x, carry):
        for y in range(CY):
            r = x * CY + y
            slab = jnp.concatenate(
                [stage[pl.ds(8 * PITCH * g + r, 8, stride=PITCH), :] for g in range(4)], axis=0
            )
            zf[x + 1, y] = slab
            zs[x + 1, y] = pltpu.roll(slab, NZ - 1, 1)
            zb[x, y] = slab.astype(bf16)
        return carry

    lax.fori_loop(0, CX, turn, 0)

    pl.semaphore_wait(barrier, COLS - 1 + 6)

    sends = []
    for i, (dx, dy) in enumerate(REGIONS):
        other = REGIONS.index((-dx, -dy))
        if dx == 0:
            src, dst = kface.at[0 if dy < 0 else 1], ky.at[0 if dy > 0 else 1]
        else:
            src, dst = kp.at[1 if dx < 0 else CX, pl.ds(8, 8), :], kx.at[other]
        sends.append(
            pltpu.make_async_remote_copy(
                src_ref=src,
                dst_ref=dst,
                send_sem=ks_send.at[i],
                recv_sem=ks_recv.at[other],
                device_id=device(dx, dy),
                device_id_type=MESH,
            )
        )
    moves = [
        pltpu.make_async_remote_copy(
            src_ref=zb.at[:, 7 - 7 * parity],
            dst_ref=hy,
            send_sem=z_send.at[0],
            recv_sem=z_recv.at[0],
            device_id=(ax, lax.rem(ay + 1 - 2 * parity + COLS, COLS)),
            device_id_type=MESH,
        )
    ]
    for side, dx in ((0, -1), (1, 1)):
        moves.append(
            pltpu.make_async_remote_copy(
                src_ref=zb.at[0 if dx < 0 else CX - 1],
                dst_ref=hx.at[1 - side],
                send_sem=z_send.at[1 + side],
                recv_sem=z_recv.at[2 - side],
                device_id=device(dx, 0),
                device_id_type=MESH,
            )
        )
    for c, (dx, dy) in enumerate(CORNERS):
        moves.append(
            pltpu.make_async_remote_copy(
                src_ref=zb.at[0 if dx < 0 else CX - 1, 0 if dy < 0 else CY - 1],
                dst_ref=hc.at[3 - c],
                send_sem=z_send.at[3 + c],
                recv_sem=z_recv.at[6 - c],
                device_id=device(dx, dy),
                device_id_type=MESH,
            )
        )
    for copy in sends + moves:
        copy.start()

    def harmonic(own, near, o):
        coef = 2.0 / (9.0 * (o[0] * o[0] + o[1] * o[1] + o[2] * o[2]))
        return (coef * own) * near / jnp.maximum(own + near, 0.05)

    def below(value):
        lane = lax.broadcasted_iota(jnp.int32, value.shape, 1)
        return jnp.where(lane == 0, 0.0, pltpu.roll(value, 1, 1))

    def above(value):
        lane = lax.broadcasted_iota(jnp.int32, value.shape, 1)
        return jnp.where(lane == NZ - 1, 0.0, pltpu.roll(value, NZ - 1, 1))

    for x in range(CX + 2):
        row = kp[x]
        kz[0, x] = below(row)
        kz[1, x] = row
        kz[2, x] = above(row)

    def weigh(x, carry):
        own = kp[x + 1, 8:16, :]
        total = REACT * own
        for o in OFFSETS:
            near = kz[o[2] + 1, x + 1 + o[0], 8 + o[1] : 16 + o[1], :]
            weight = harmonic(own, near, o)
            if o in HALF:
                weights[HALF.index(o), x] = weight
            total = total + weight
        dsum[x] = 0.5 * total
        return carry

    lax.fori_loop(0, CX, weigh, 0)

    def contract(x, slot):
        left = jnp.concatenate([yb[slot, y] for y in range(CY)], axis=1)
        right = jnp.concatenate([zb[x, y] for y in range(CY)], axis=1)
        return lax.dot_general(left, right, LAST, preferred_element_type=f32)

    def interior(x, acc):
        acc = acc + contract(jnp.maximum(x - 1, 0), x)
        for y in range(CY):
            value = dsum[x, y : y + 1, :] * zf[x + 1, y]
            for i, (ox, oy, oz) in enumerate(HALF):
                if not 0 <= y + oy < CY:
                    continue
                field = zf if oz == 0 else zs
                w = weights[i, x, y : y + 1, :]
                value = value - w * field[x + 1 + ox, y + oy]
            high, low = split(value)
            yb[x + 1, y, 0:K, :] = high
            yb[x + 1, y, K : 2 * K, :] = low
        return acc

    acc = lax.fori_loop(0, CX, interior, jnp.zeros((2 * K, K), f32))
    acc = acc + contract(CX - 1, CX)

    for copy in sends:
        copy.wait()
    low_x = (ax > 0).astype(f32)
    high_x = (ax < ROWS - 1).astype(f32)
    low_y = (ay > 0).astype(f32)
    high_y = (ay < COLS - 1).astype(f32)
    for side, dx, keep in ((0, -1, low_x), (1, 1, high_x)):
        near = kx[REGIONS.index((dx, 0))] * keep
        frame_x[1, side, 8:16, :] = near
    for side, dy, keep in ((0, -1, low_y), (1, 1, high_y)):
        y = 7 if dy < 0 else 0
        frame_y[1, side, 8:24, :] = ky[side] * keep
        for at, dx, keep_x in ((7, -1, low_x), (24, 1, high_x)):
            corner = kx[REGIONS.index((dx, dy)), y : y + 1, :]
            frame_y[1, side, at : at + 1, :] = corner * (keep * keep_x)
        frame_own[1, side, 8:24, :] = kface[side]
    for frame in (frame_x, frame_y, frame_own):
        for side in range(2):
            row = frame[1, side]
            frame[0, side] = below(row)
            frame[2, side] = above(row)

    NINE = [(i, j) for i in (-1, 0, 1) for j in (-1, 0, 1)]
    for side, dx in ((0, -1), (1, 1)):
        x = 0 if dx < 0 else CX - 1
        own = kp[x + 1, 8:16, :]
        total = jnp.zeros_like(own)
        for oy, oz in NINE:
            near = frame_x[oz + 1, side, 8 + oy : 16 + oy, :]
            total = total + harmonic(own, near, (dx, oy, oz))
        for y in range(CY):
            high, low = split(total[y : y + 1] * zf[x + 1, y])
            ex[side, y, 0:K, :] = high
            ex[side, y, K : 2 * K, :] = low
    for side, dy in ((0, -1), (1, 1)):
        own = kface[side]
        total = jnp.zeros_like(own)
        for ox, oz in NINE:
            near = frame_y[oz + 1, side, 8 + ox : 24 + ox, :]
            total = total + harmonic(own, near, (ox, dy, oz))
        for x in range(CX):
            high, low = split(total[x : x + 1] * zf[x + 1, 0 if dy < 0 else CY - 1])
            ey[side, x, 0:K, :] = high
            ey[side, x, K : 2 * K, :] = low
    outer = jnp.zeros((2 * K, K), f32)
    for side in range(2):
        x = 0 if side == 0 else CX - 1
        y = 0 if side == 0 else CY - 1
        outer = outer + lax.dot_general(
            jnp.concatenate([ex[side, i] for i in range(CY)], axis=1),
            jnp.concatenate([zb[x, i] for i in range(CY)], axis=1),
            LAST,
            preferred_element_type=f32,
        )
        outer = outer + lax.dot_general(
            jnp.concatenate([ey[side, i] for i in range(CX)], axis=1),
            jnp.concatenate([zb[i, y] for i in range(CX)], axis=1),
            LAST,
            preferred_element_type=f32,
        )
    half = acc[:K] + acc[K:]
    diagonal = (half + half.T + outer[:K] + outer[K:]) * (1.0 / (CX * CY * NZ))

    for side, dx in ((0, -1), (1, 1)):
        x = 0 if dx < 0 else CX - 1
        for y in range(CY):
            zmx[side, y] = pltpu.roll(zf[x + 1, y], 1, 1)
        own = frame_x[1, side, 8:16, :]
        for i, (oy, oz) in enumerate(NINE):
            near = kz[oz + 1, x + 1, 8 + oy : 16 + oy, :]
            wx[side, i] = harmonic(own, near, (dx, oy, oz))
        for y in range(CY):
            value = jnp.zeros((K, NZ), f32)
            for i, (oy, oz) in enumerate(NINE):
                if not 0 <= y + oy < CY:
                    continue
                field = (zmx[side, y + oy], zf[x + 1, y + oy], zs[x + 1, y + oy])[oz + 1]
                value = value - wx[side, i, y : y + 1, :] * field
            high, low = split(value)
            gx[side, y, 0:K, :] = high
            gx[side, y, K : 2 * K, :] = low
    for c, (dx, dy) in enumerate(CORNERS):
        x = 0 if dx < 0 else CX - 1
        y = 0 if dy < 0 else CY - 1
        side = 0 if dx < 0 else 1
        at = 7 if dx < 0 else 24
        own = frame_y[1, 0 if dy < 0 else 1, at : at + 1, :]
        value = jnp.zeros((K, NZ), f32)
        for oz in (-1, 0, 1):
            near = kz[oz + 1, x + 1, 8 + y : 9 + y, :]
            field = (zmx[side, y], zf[x + 1, y], zs[x + 1, y])[oz + 1]
            value = value - harmonic(own, near, (dx, dy, oz)) * field
        high, low = split(value)
        gc[c, 0:K, :] = high
        gc[c, K : 2 * K, :] = low
    y_edge = 7 * parity
    own = frame_y[1, parity, 8:24, :]
    for i, (ox, oz) in enumerate(NINE):
        near = frame_own[oz + 1, parity, 8 + ox : 24 + ox, :]
        wy[i] = harmonic(own, near, (ox, 1, oz))

    def lower(x, carry):
        zmy[x + 1] = pltpu.roll(zf[x + 1, y_edge], 1, 1)
        return carry

    lax.fori_loop(0, CX, lower, 0, unroll=4)

    def face(x, carry):
        value = jnp.zeros((K, NZ), f32)
        for i, (ox, oz) in enumerate(NINE):
            at = x + 1 + ox
            field = (zmy[at], zf[at, y_edge], zs[at, y_edge])[oz + 1]
            value = value - wy[i, pl.ds(x, 1), :] * field
        high, low = split(value)
        gy[x, 0:K, :] = high
        gy[x, K : 2 * K, :] = low
        return carry

    lax.fori_loop(0, CX, face, 0, unroll=4)

    width = COLS
    own_row = jnp.broadcast_to(owner[...], (width, width))
    i_sub = lax.broadcasted_iota(jnp.int32, (width, width), 0)
    i_lane = lax.broadcasted_iota(jnp.int32, (width, width), 1)
    own_f = own_row.astype(f32)
    own_col = jnp.sum(jnp.where(i_sub == i_lane, own_f, 0.0), axis=1, keepdims=True)
    before = (own_col == own_f) & (i_sub < i_lane)
    rank = jnp.sum(jnp.where(before, 1.0, 0.0), axis=0, keepdims=True)
    code = jnp.broadcast_to(own_f[0:1] * 4.0 + rank, (8, width)).astype(bf16)
    e_sub = lax.broadcasted_iota(jnp.int32, (width, NZ), 0)
    e_lane = lax.broadcasted_iota(jnp.int32, (width, NZ), 1)
    step = 2 * parity - 1
    e_from = e_lane // 4 + jnp.where(e_lane % 4 == 3, step, 0)
    expand = jnp.where(e_from == e_sub, 1.0, 0.0).astype(bf16)
    wide = jnp.dot(code, expand, preferred_element_type=f32)[0:1].astype(jnp.int32)
    wide_owner = wide // 4
    wide_rank = wide - wide_owner * 4
    lane1 = lax.broadcasted_iota(jnp.int32, (1, NZ), 1)
    part = lane1 % 4
    target = wide_owner * 8 + wide_rank * 2 + jnp.where(part == 3, 1 - parity, part)
    target = jnp.where(part == 2, wide_owner * 8 + 6, target)
    end = (lane1 // 4 + step < 0) | (lane1 // 4 + step >= width)
    target = jnp.where((part == 3) & end, -1, target)
    p_sub = lax.broadcasted_iota(jnp.int32, (COLS * 8, NZ), 0)
    route = jnp.where(p_sub == target, 1.0, 0.0).astype(bf16)
    my_rank = jnp.sum(
        jnp.where(lax.broadcasted_iota(jnp.int32, (1, width), 1) == ay, rank, 0.0),
        axis=1,
        keepdims=True,
    )
    quarter = (lax.broadcasted_iota(jnp.int32, (K, NZ), 1) // K).astype(f32)

    for copy in moves:
        copy.wait()

    def meet(left, right):
        product = lax.dot_general(left, right, LAST, preferred_element_type=f32)
        return product[:K] + product[K:]

    blocks = {}
    for side, dx in ((0, -1), (1, 1)):
        blocks[(dx, 0)] = meet(
            jnp.concatenate([gx[side, y] for y in range(CY)], axis=1),
            jnp.concatenate([hx[side, y] for y in range(CY)], axis=1),
        )
    for c, region in enumerate(CORNERS):
        blocks[region] = meet(gc[c], hc[c])
    across = meet(
        jnp.concatenate([gy[x] for x in range(CX)], axis=1),
        jnp.concatenate([hy[x] for x in range(CX)], axis=1),
    )
    back = across.T
    none = jnp.zeros_like(back)
    rows = [
        jnp.concatenate(
            [blocks[(-1, -1)], blocks[(-1, 0)], blocks[(-1, 1)], across * (1.0 - parity_f)],
            axis=1,
        ),
        jnp.concatenate(
            [across * parity_f, blocks[(1, -1)], blocks[(1, 0)], blocks[(1, 1)]], axis=1
        ),
        jnp.where(quarter == my_rank, jnp.concatenate([diagonal] * 4, axis=1), 0.0),
        jnp.concatenate([back * (1.0 - parity_f), none, none, back * parity_f], axis=1),
    ]
    flat = piece.reshape(4 * K, NZ)
    for l, value in enumerate(rows):
        flat[pl.ds(l, K, stride=4), :] = value

    def first(off, carry):
        to = lax.rem(ay + off, COLS)
        pltpu.make_async_remote_copy(
            src_ref=piece.at[to],
            dst_ref=pieces.at[ay],
            send_sem=one_send,
            recv_sem=one_recv,
            device_id=(ax, to),
            device_id_type=MESH,
        ).start()
        return carry

    lax.fori_loop(1, COLS, first, 0)
    keep = pltpu.make_async_copy(piece.at[ay], pieces.at[ay], local_sem.at[0])
    keep.start()
    keep.wait()
    many = pieces.at[pl.ds(0, COLS - 1)]
    pltpu.make_async_copy(many, many, one_recv).wait()

    got = pieces.reshape(4 * COLS, NZ)[...]
    a1 = got.astype(jnp.bfloat16)
    rest = got - a1.astype(f32)
    a2 = rest.astype(jnp.bfloat16)
    a3 = (rest - a2.astype(f32)).astype(jnp.bfloat16)
    value = (
        jnp.dot(route, a1, preferred_element_type=f32)
        + jnp.dot(route, a2, preferred_element_type=f32)
        + jnp.dot(route, a3, preferred_element_type=f32)
    )
    peak = jnp.max(jnp.abs(value), axis=1, keepdims=True)
    power = jnp.ceil(jnp.log2(jnp.maximum(peak, 1e-30)))
    coded = value * (jnp.exp2(-power) * LEVELS)
    sub = lax.broadcasted_iota(jnp.int32, (COLS, 8, NZ), 1)
    lane = lax.broadcasted_iota(jnp.int32, (COLS, 8, NZ), 2)
    spread = jnp.broadcast_to(power, (COLS * 8, NZ)).reshape(COLS, 8, NZ)
    powers = jnp.sum(jnp.where(sub == lane, spread, 0.0), axis=1, keepdims=True)
    coded = jnp.where(sub == 7, powers, coded.reshape(COLS, 8, NZ))
    words[...] = jnp.round(coded).astype(jnp.int32).reshape(COLS * 8, NZ)
    packed = slots.reshape(4 * COLS, NZ)
    for w in range(4):
        low = words[pl.ds(w, COLS, stride=8), :]
        high = words[pl.ds(w + 4, COLS, stride=8), :]
        packed[pl.ds(w, COLS, stride=4), :] = (high << 16) | (low & 0xFFFF)

    def second(off, carry):
        to = lax.rem(ay + off, COLS)
        pltpu.make_async_remote_copy(
            src_ref=slots.at[to],
            dst_ref=owned.at[ay],
            send_sem=two_send,
            recv_sem=two_recv,
            device_id=(ax, to),
            device_id_type=MESH,
        ).start()
        return carry

    lax.fori_loop(1, COLS, second, 0)
    keep = pltpu.make_async_copy(slots.at[ay], owned.at[ay], local_sem.at[1])
    keep.start()
    keep.wait()
    sent = piece.at[pl.ds(0, COLS - 1)]
    pltpu.make_async_copy(sent, sent, one_send).wait()
    many = owned.at[pl.ds(0, COLS - 1)]
    pltpu.make_async_copy(many, many, two_recv).wait()

    out[...] = owned[...]
    sent = slots.at[pl.ds(0, COLS - 1)]
    pltpu.make_async_copy(sent, sent, two_send).wait()


def unpack(words, out_diag, out_coup):
    f32 = jnp.float32
    flat = words.reshape(4 * COLS, NZ)
    got = [flat[pl.ds(w, K, stride=4), :] for w in range(4)]
    rows = [(w << 16) >> 16 for w in got] + [w >> 16 for w in got]
    rows = [row.astype(f32) for row in rows]
    scale = jnp.exp2(rows[7]) * (1.0 / LEVELS)
    rows = [row * scale[:, r : r + 1] for r, row in enumerate(rows[:7])]
    for c in range(CAP):
        for half_row in range(2):
            for q in range(4):
                out_coup[c, half_row * 4 + q] = rows[2 * c + half_row][:, q * K : (q + 1) * K]
        out_diag[c] = rows[6][:, c * K : (c + 1) * K]


def shards(basis, phase_ids, phase_stiffness, owner_map):
    f32, bf16 = jnp.float32, jnp.bfloat16
    vmem = pltpu.VMEM
    dma = pltpu.SemaphoreType.DMA
    whole = pl.BlockSpec(memory_space=pltpu.VMEM)
    packed = pl.pallas_call(
        kernel,
        out_shape=jax.ShapeDtypeStruct((COLS, 4, NZ), jnp.int32),
        in_specs=[pl.BlockSpec(memory_space=pltpu.HBM)] * 4,
        out_specs=whole,
        scratch_shapes=[
            vmem((K * CX * CY, NZ), bf16),
            vmem((CX, CY, NZ), jnp.int32),
            vmem((1, 8), bf16),
            vmem((1, COLS), jnp.int32),
            vmem((K * PITCH, NZ), f32),
            vmem((CX + 2, CY, K, NZ), f32),
            vmem((CX + 2, CY, K, NZ), f32),
            vmem((CX, CY, K, NZ), bf16),
            vmem((2, CY, K, NZ), f32),
            vmem((CX + 2, K, NZ), f32),
            vmem((CX + 2, 24, NZ), f32),
            vmem((3, CX + 2, 24, NZ), f32),
            vmem((8, 8, NZ), f32),
            vmem((2, CX, NZ), f32),
            vmem((2, CX, NZ), f32),
            vmem((3, 2, 24, NZ), f32),
            vmem((3, 2, 32, NZ), f32),
            vmem((3, 2, 32, NZ), f32),
            vmem((2, CY, K, NZ), bf16),
            vmem((CX, K, NZ), bf16),
            vmem((4, K, NZ), bf16),
            vmem((13, CX, CY, NZ), f32),
            vmem((CX, CY, NZ), f32),
            vmem((2, 9, CY, NZ), f32),
            vmem((9, CX, NZ), f32),
            vmem((CX + 1, CY, 2 * K, NZ), bf16),
            vmem((2, CY, 2 * K, NZ), bf16),
            vmem((2, CX, 2 * K, NZ), bf16),
            vmem((2, CY, 2 * K, NZ), bf16),
            vmem((CX, 2 * K, NZ), bf16),
            vmem((4, 2 * K, NZ), bf16),
            vmem((K, 4, NZ), f32),
            vmem((COLS, 4, NZ), f32),
            vmem((COLS * 8, NZ), jnp.int32),
            vmem((COLS, 4, NZ), jnp.int32),
            vmem((COLS, 4, NZ), jnp.int32),
            dma((7,)),
            dma((8,)),
            dma((8,)),
            dma((7,)),
            dma((7,)),
            dma,
            dma,
            dma,
            dma,
            dma((2,)),
        ],
        compiler_params=pltpu.CompilerParams(
            collective_id=0, has_side_effects=True, vmem_limit_bytes=60 * 1024 * 1024
        ),
    )(
        basis.reshape(K * CX * CY, NZ),
        phase_ids,
        phase_stiffness.reshape(1, 8),
        owner_map,
    )
    diag, coup = pl.pallas_call(
        unpack,
        out_shape=(
            jax.ShapeDtypeStruct((CAP, K, K), f32),
            jax.ShapeDtypeStruct((CAP, 8, K, K), f32),
        ),
        in_specs=[whole],
        out_specs=(whole, whole),
    )(packed)
    return diag[None], coup[None]


def solution(mesh):
    return jax.shard_map(
        shards,
        mesh=mesh,
        in_specs=(P(None, "gx", "gy", None), P("gx", "gy", None), P(), P("gx", None)),
        out_specs=(P("gx", "gy", None, None), P("gx", "gy", None, None, None)),
        check_vma=False,
    )
```

```python
import functools

import jax
import jax.numpy as jnp
from jax import lax
from jax.experimental import pallas as pl
from jax.experimental.pallas import tpu as pltpu
from jax.sharding import PartitionSpec as P

CAP = 3
REACT = 0.1
REGIONS = ((-1, -1), (-1, 0), (-1, 1), (0, -1), (0, 1), (1, -1), (1, 0), (1, 1))
CORNERS = ((-1, -1), (-1, 1), (1, -1), (1, 1))
OFFSETS = [
    (ox, oy, oz)
    for ox in (-1, 0, 1)
    for oy in (-1, 0, 1)
    for oz in (-1, 0, 1)
    if (ox, oy, oz) != (0, 0, 0)
]
HALF = [o for o in OFFSETS if o[2] == 1] + [(0, 1, 0), (1, -1, 0), (1, 0, 0), (1, 1, 0)]
MESH = pl.DeviceIdType.MESH
K, CX, CY, NZ = 32, 16, 8, 128
ROWS, COLS = 16, 32
PITCH = 136
FAR = sorted(range(1, COLS), key=lambda off: -min(off % 16, 16 - off % 16))
BEFORE = 8
LEVELS = 32000.0
LAST = (((1,), (1,)), ((), ()))


def split(value):
    high = value.astype(jnp.bfloat16)
    low = (value - high.astype(jnp.float32)).astype(jnp.bfloat16)
    return high, low


def kernel(
    basis,
    ids_hbm,
    phase_hbm,
    owner_hbm,
    out,
    raw,
    ids,
    phase,
    owner,
    stage,
    zf,
    zs,
    zb,
    zmx,
    zmy,
    kp,
    kz,
    kx,
    ky,
    kface,
    frame_x,
    frame_y,
    frame_own,
    hx,
    hy,
    hc,
    weights,
    dsum,
    wx,
    wy,
    yb,
    ex,
    ey,
    gx,
    gy,
    gc,
    piece,
    pieces,
    words,
    slots,
    owned,
    load_sem,
    ks_send,
    ks_recv,
    z_send,
    z_recv,
    one_send,
    one_recv,
    two_send,
    two_recv,
    local_sem,
):
    f32, bf16 = jnp.float32, jnp.bfloat16
    ax = lax.axis_index("gx")
    ay = lax.axis_index("gy")
    parity = lax.rem(ax, 2)
    parity_f = parity.astype(f32)

    def device(dx, dy):
        return (lax.rem(ax + dx + ROWS, ROWS), lax.rem(ay + dy + COLS, COLS))

    small = [
        pltpu.make_async_copy(ids_hbm, ids, load_sem.at[4]),
        pltpu.make_async_copy(phase_hbm, phase, load_sem.at[5]),
        pltpu.make_async_copy(owner_hbm, owner, load_sem.at[6]),
    ]
    loads = [
        pltpu.make_async_copy(
            basis.at[pl.ds(1024 * g, 1024)], raw.at[pl.ds(1024 * g, 1024)], load_sem.at[g]
        )
        for g in range(4)
    ]
    for copy in small + loads:
        copy.start()

    barrier = pltpu.get_barrier_semaphore()

    for off in FAR:
        pl.semaphore_signal(
            barrier, inc=1, device_id=(ax, lax.rem(ay + off, COLS)), device_id_type=MESH
        )
    for dx, dy in REGIONS:
        if dx != 0:
            pl.semaphore_signal(barrier, inc=1, device_id=device(dx, dy), device_id_type=MESH)

    kp[...] = jnp.zeros_like(kp)
    frame_own[...] = jnp.zeros_like(frame_own)
    frame_x[...] = jnp.zeros_like(frame_x)
    frame_y[...] = jnp.zeros_like(frame_y)
    zero = jnp.zeros((8, K, NZ), f32)
    for edge in (0, CX + 1):
        zf[edge] = zero
        zs[edge] = zero
    zmy[0] = zero[0]
    zmy[CX + 1] = zero[0]
    yb[0] = jnp.zeros((CY, 2 * K, NZ), bf16)

    for copy in small:
        copy.wait()
    table = phase[...].astype(f32)
    for x in range(CX):
        cell = ids[x]
        value = jnp.zeros((CY, NZ), f32)
        for p in range(8):
            value = jnp.where(cell == p, table[0:1, p : p + 1], value)
        kp[x + 1, 8:16, :] = value
    for side, y in ((0, 0), (1, CY - 1)):
        for x in range(CX):
            kface[side, x : x + 1, :] = kp[x + 1, 8 + y : 9 + y, :]

    for g in range(4):
        loads[g].wait()

        def widen(i, carry, g=g):
            at = pl.multiple_of(1024 * g + i * 128, 128)
            to = pl.multiple_of(PITCH * 8 * g + i * PITCH, 8)
            stage[pl.ds(to, 128), :] = raw[pl.ds(at, 128), :].astype(f32)
            return carry

        lax.fori_loop(0, 8, widen, 0)

    def turn(x, carry):
        for y in range(CY):
            r = x * CY + y
            slab = jnp.concatenate(
                [stage[pl.ds(8 * PITCH * g + r, 8, stride=PITCH), :] for g in range(4)], axis=0
            )
            zf[x + 1, y] = slab
            zs[x + 1, y] = pltpu.roll(slab, NZ - 1, 1)
            zb[x, y] = slab.astype(bf16)
        return carry

    lax.fori_loop(0, CX, turn, 0, unroll=4)

    def harmonic(own, near, o):
        coef = 2.0 / (9.0 * (o[0] * o[0] + o[1] * o[1] + o[2] * o[2]))
        return (coef * own) * near / jnp.maximum(own + near, 0.05)

    def below(value):
        lane = lax.broadcasted_iota(jnp.int32, value.shape, 1)
        return jnp.where(lane == 0, 0.0, pltpu.roll(value, 1, 1))

    def above(value):
        lane = lax.broadcasted_iota(jnp.int32, value.shape, 1)
        return jnp.where(lane == NZ - 1, 0.0, pltpu.roll(value, NZ - 1, 1))

    for x in range(CX + 2):
        row = kp[x]
        kz[0, x] = below(row)
        kz[1, x] = row
        kz[2, x] = above(row)

    def weigh(x, carry):
        own = kp[x + 1, 8:16, :]
        total = REACT * own
        for o in OFFSETS:
            near = kz[o[2] + 1, x + 1 + o[0], 8 + o[1] : 16 + o[1], :]
            weight = harmonic(own, near, o)
            if o in HALF:
                weights[HALF.index(o), x] = weight
            total = total + weight
        dsum[x] = 0.5 * total
        return carry

    lax.fori_loop(0, CX, weigh, 0, unroll=2)

    def contract(x, slot):
        left = jnp.concatenate([yb[slot, y] for y in range(CY)], axis=1)
        right = jnp.concatenate([zb[x, y] for y in range(CY)], axis=1)
        return lax.dot_general(left, right, LAST, preferred_element_type=f32)

    def interior(x, acc):
        acc = acc + contract(jnp.maximum(x - 1, 0), x)
        for y in range(CY):
            value = dsum[x, y : y + 1, :] * zf[x + 1, y]
            for i, (ox, oy, oz) in enumerate(HALF):
                if not 0 <= y + oy < CY:
                    continue
                field = zf if oz == 0 else zs
                w = weights[i, x, y : y + 1, :]
                value = value - w * field[x + 1 + ox, y + oy]
            high, low = split(value)
            yb[x + 1, y, 0:K, :] = high
            yb[x + 1, y, K : 2 * K, :] = low
        return acc

    acc = lax.fori_loop(0, BEFORE, interior, jnp.zeros((2 * K, K), f32), unroll=4)

    pl.semaphore_wait(barrier, COLS - 1 + 6)

    sends = []
    for i, (dx, dy) in enumerate(REGIONS):
        other = REGIONS.index((-dx, -dy))
        if dx == 0:
            src, dst = kface.at[0 if dy < 0 else 1], ky.at[0 if dy > 0 else 1]
        else:
            src, dst = kp.at[1 if dx < 0 else CX, pl.ds(8, 8), :], kx.at[other]
        sends.append(
            pltpu.make_async_remote_copy(
                src_ref=src,
                dst_ref=dst,
                send_sem=ks_send.at[i],
                recv_sem=ks_recv.at[other],
                device_id=device(dx, dy),
                device_id_type=MESH,
            )
        )
    moves = [
        pltpu.make_async_remote_copy(
            src_ref=zb.at[:, 7 - 7 * parity],
            dst_ref=hy,
            send_sem=z_send.at[0],
            recv_sem=z_recv.at[0],
            device_id=(ax, lax.rem(ay + 1 - 2 * parity + COLS, COLS)),
            device_id_type=MESH,
        )
    ]
    for side, dx in ((0, -1), (1, 1)):
        moves.append(
            pltpu.make_async_remote_copy(
                src_ref=zb.at[0 if dx < 0 else CX - 1],
                dst_ref=hx.at[1 - side],
                send_sem=z_send.at[1 + side],
                recv_sem=z_recv.at[2 - side],
                device_id=device(dx, 0),
                device_id_type=MESH,
            )
        )
    for c, (dx, dy) in enumerate(CORNERS):
        moves.append(
            pltpu.make_async_remote_copy(
                src_ref=zb.at[0 if dx < 0 else CX - 1, 0 if dy < 0 else CY - 1],
                dst_ref=hc.at[3 - c],
                send_sem=z_send.at[3 + c],
                recv_sem=z_recv.at[6 - c],
                device_id=device(dx, dy),
                device_id_type=MESH,
            )
        )
    for copy in sends + moves:
        copy.start()

    acc = lax.fori_loop(BEFORE, CX, interior, acc, unroll=4)
    acc = acc + contract(CX - 1, CX)

    for copy in sends:
        copy.wait()
    low_x = (ax > 0).astype(f32)
    high_x = (ax < ROWS - 1).astype(f32)
    low_y = (ay > 0).astype(f32)
    high_y = (ay < COLS - 1).astype(f32)
    for side, dx, keep in ((0, -1, low_x), (1, 1, high_x)):
        near = kx[REGIONS.index((dx, 0))] * keep
        frame_x[1, side, 8:16, :] = near
    for side, dy, keep in ((0, -1, low_y), (1, 1, high_y)):
        y = 7 if dy < 0 else 0
        frame_y[1, side, 8:24, :] = ky[side] * keep
        for at, dx, keep_x in ((7, -1, low_x), (24, 1, high_x)):
            corner = kx[REGIONS.index((dx, dy)), y : y + 1, :]
            frame_y[1, side, at : at + 1, :] = corner * (keep * keep_x)
        frame_own[1, side, 8:24, :] = kface[side]
    for frame in (frame_x, frame_y, frame_own):
        for side in range(2):
            row = frame[1, side]
            frame[0, side] = below(row)
            frame[2, side] = above(row)

    NINE = [(i, j) for i in (-1, 0, 1) for j in (-1, 0, 1)]
    for side, dx in ((0, -1), (1, 1)):
        x = 0 if dx < 0 else CX - 1
        own = kp[x + 1, 8:16, :]
        total = jnp.zeros_like(own)
        for oy, oz in NINE:
            near = frame_x[oz + 1, side, 8 + oy : 16 + oy, :]
            total = total + harmonic(own, near, (dx, oy, oz))
        for y in range(CY):
            high, low = split(total[y : y + 1] * zf[x + 1, y])
            ex[side, y, 0:K, :] = high
            ex[side, y, K : 2 * K, :] = low
    for side, dy in ((0, -1), (1, 1)):
        own = kface[side]
        total = jnp.zeros_like(own)
        for ox, oz in NINE:
            near = frame_y[oz + 1, side, 8 + ox : 24 + ox, :]
            total = total + harmonic(own, near, (ox, dy, oz))
        for x in range(CX):
            high, low = split(total[x : x + 1] * zf[x + 1, 0 if dy < 0 else CY - 1])
            ey[side, x, 0:K, :] = high
            ey[side, x, K : 2 * K, :] = low
    outer = jnp.zeros((2 * K, K), f32)
    for side in range(2):
        x = 0 if side == 0 else CX - 1
        y = 0 if side == 0 else CY - 1
        outer = outer + lax.dot_general(
            jnp.concatenate([ex[side, i] for i in range(CY)], axis=1),
            jnp.concatenate([zb[x, i] for i in range(CY)], axis=1),
            LAST,
            preferred_element_type=f32,
        )
        outer = outer + lax.dot_general(
            jnp.concatenate([ey[side, i] for i in range(CX)], axis=1),
            jnp.concatenate([zb[i, y] for i in range(CX)], axis=1),
            LAST,
            preferred_element_type=f32,
        )
    half = acc[:K] + acc[K:]
    diagonal = (half + half.T + outer[:K] + outer[K:]) * (1.0 / (CX * CY * NZ))

    for side, dx in ((0, -1), (1, 1)):
        x = 0 if dx < 0 else CX - 1
        for y in range(CY):
            zmx[side, y] = pltpu.roll(zf[x + 1, y], 1, 1)
        own = frame_x[1, side, 8:16, :]
        for i, (oy, oz) in enumerate(NINE):
            near = kz[oz + 1, x + 1, 8 + oy : 16 + oy, :]
            wx[side, i] = harmonic(own, near, (dx, oy, oz))
        for y in range(CY):
            value = jnp.zeros((K, NZ), f32)
            for i, (oy, oz) in enumerate(NINE):
                if not 0 <= y + oy < CY:
                    continue
                field = (zmx[side, y + oy], zf[x + 1, y + oy], zs[x + 1, y + oy])[oz + 1]
                value = value - wx[side, i, y : y + 1, :] * field
            high, low = split(value)
            gx[side, y, 0:K, :] = high
            gx[side, y, K : 2 * K, :] = low
    for c, (dx, dy) in enumerate(CORNERS):
        x = 0 if dx < 0 else CX - 1
        y = 0 if dy < 0 else CY - 1
        side = 0 if dx < 0 else 1
        at = 7 if dx < 0 else 24
        own = frame_y[1, 0 if dy < 0 else 1, at : at + 1, :]
        value = jnp.zeros((K, NZ), f32)
        for oz in (-1, 0, 1):
            near = kz[oz + 1, x + 1, 8 + y : 9 + y, :]
            field = (zmx[side, y], zf[x + 1, y], zs[x + 1, y])[oz + 1]
            value = value - harmonic(own, near, (dx, dy, oz)) * field
        high, low = split(value)
        gc[c, 0:K, :] = high
        gc[c, K : 2 * K, :] = low
    y_edge = 7 * parity
    own = frame_y[1, parity, 8:24, :]
    for i, (ox, oz) in enumerate(NINE):
        near = frame_own[oz + 1, parity, 8 + ox : 24 + ox, :]
        wy[i] = harmonic(own, near, (ox, 1, oz))

    def lower(x, carry):
        zmy[x + 1] = pltpu.roll(zf[x + 1, y_edge], 1, 1)
        return carry

    lax.fori_loop(0, CX, lower, 0, unroll=4)

    def face(x, carry):
        value = jnp.zeros((K, NZ), f32)
        for i, (ox, oz) in enumerate(NINE):
            at = x + 1 + ox
            field = (zmy[at], zf[at, y_edge], zs[at, y_edge])[oz + 1]
            value = value - wy[i, pl.ds(x, 1), :] * field
        high, low = split(value)
        gy[x, 0:K, :] = high
        gy[x, K : 2 * K, :] = low
        return carry

    lax.fori_loop(0, CX, face, 0, unroll=4)

    width = COLS
    own_row = jnp.broadcast_to(owner[...], (width, width))
    i_sub = lax.broadcasted_iota(jnp.int32, (width, width), 0)
    i_lane = lax.broadcasted_iota(jnp.int32, (width, width), 1)
    own_f = own_row.astype(f32)
    own_col = jnp.sum(jnp.where(i_sub == i_lane, own_f, 0.0), axis=1, keepdims=True)
    before = (own_col == own_f) & (i_sub < i_lane)
    rank = jnp.sum(jnp.where(before, 1.0, 0.0), axis=0, keepdims=True)
    code = jnp.broadcast_to(own_f[0:1] * 4.0 + rank, (8, width)).astype(bf16)
    e_sub = lax.broadcasted_iota(jnp.int32, (width, NZ), 0)
    e_lane = lax.broadcasted_iota(jnp.int32, (width, NZ), 1)
    step = 2 * parity - 1
    e_from = e_lane // 4 + jnp.where(e_lane % 4 == 3, step, 0)
    expand = jnp.where(e_from == e_sub, 1.0, 0.0).astype(bf16)
    wide = jnp.dot(code, expand, preferred_element_type=f32)[0:1].astype(jnp.int32)
    wide_owner = wide // 4
    wide_rank = wide - wide_owner * 4
    lane1 = lax.broadcasted_iota(jnp.int32, (1, NZ), 1)
    part = lane1 % 4
    target = wide_owner * 8 + wide_rank * 2 + jnp.where(part == 3, 1 - parity, part)
    target = jnp.where(part == 2, wide_owner * 8 + 6, target)
    end = (lane1 // 4 + step < 0) | (lane1 // 4 + step >= width)
    target = jnp.where((part == 3) & end, -1, target)
    p_sub = lax.broadcasted_iota(jnp.int32, (COLS * 8, NZ), 0)
    route = jnp.where(p_sub == target, 1.0, 0.0).astype(bf16)
    my_rank = jnp.sum(
        jnp.where(lax.broadcasted_iota(jnp.int32, (1, width), 1) == ay, rank, 0.0),
        axis=1,
        keepdims=True,
    )
    quarter = (lax.broadcasted_iota(jnp.int32, (K, NZ), 1) // K).astype(f32)

    for copy in moves:
        copy.wait()

    def meet(left, right):
        product = lax.dot_general(left, right, LAST, preferred_element_type=f32)
        return product[:K] + product[K:]

    blocks = {}
    for side, dx in ((0, -1), (1, 1)):
        blocks[(dx, 0)] = meet(
            jnp.concatenate([gx[side, y] for y in range(CY)], axis=1),
            jnp.concatenate([hx[side, y] for y in range(CY)], axis=1),
        )
    for c, region in enumerate(CORNERS):
        blocks[region] = meet(gc[c], hc[c])
    across = meet(
        jnp.concatenate([gy[x] for x in range(CX)], axis=1),
        jnp.concatenate([hy[x] for x in range(CX)], axis=1),
    )
    back = across.T
    none = jnp.zeros_like(back)
    rows = [
        jnp.concatenate(
            [blocks[(-1, -1)], blocks[(-1, 0)], blocks[(-1, 1)], across * (1.0 - parity_f)],
            axis=1,
        ),
        jnp.concatenate(
            [across * parity_f, blocks[(1, -1)], blocks[(1, 0)], blocks[(1, 1)]], axis=1
        ),
        jnp.where(quarter == my_rank, jnp.concatenate([diagonal] * 4, axis=1), 0.0),
        jnp.concatenate([back * (1.0 - parity_f), none, none, back * parity_f], axis=1),
    ]
    flat = piece.reshape(4 * K, NZ)
    for l, value in enumerate(rows):
        flat[pl.ds(l, K, stride=4), :] = value

    for off in FAR:
        to = lax.rem(ay + off, COLS)
        pltpu.make_async_remote_copy(
            src_ref=piece.at[to],
            dst_ref=pieces.at[ay],
            send_sem=one_send,
            recv_sem=one_recv,
            device_id=(ax, to),
            device_id_type=MESH,
        ).start()
    keep = pltpu.make_async_copy(piece.at[ay], pieces.at[ay], local_sem.at[0])
    keep.start()
    keep.wait()
    many = pieces.at[pl.ds(0, COLS - 1)]
    pltpu.make_async_copy(many, many, one_recv).wait()

    got = pieces.reshape(4 * COLS, NZ)[...]
    a1 = got.astype(jnp.bfloat16)
    rest = got - a1.astype(f32)
    a2 = rest.astype(jnp.bfloat16)
    a3 = (rest - a2.astype(f32)).astype(jnp.bfloat16)
    value = (
        jnp.dot(route, a1, preferred_element_type=f32)
        + jnp.dot(route, a2, preferred_element_type=f32)
        + jnp.dot(route, a3, preferred_element_type=f32)
    )
    peak = jnp.max(jnp.abs(value), axis=1, keepdims=True)
    power = jnp.ceil(jnp.log2(jnp.maximum(peak, 1e-30)))
    coded = value * (jnp.exp2(-power) * LEVELS)
    sub = lax.broadcasted_iota(jnp.int32, (COLS, 8, NZ), 1)
    lane = lax.broadcasted_iota(jnp.int32, (COLS, 8, NZ), 2)
    spread = jnp.broadcast_to(power, (COLS * 8, NZ)).reshape(COLS, 8, NZ)
    powers = jnp.sum(jnp.where(sub == lane, spread, 0.0), axis=1, keepdims=True)
    coded = jnp.where(sub == 7, powers, coded.reshape(COLS, 8, NZ))
    words[...] = jnp.round(coded).astype(jnp.int32).reshape(COLS * 8, NZ)
    packed = slots.reshape(4 * COLS, NZ)
    for w in range(4):
        low = words[pl.ds(w, COLS, stride=8), :]
        high = words[pl.ds(w + 4, COLS, stride=8), :]
        packed[pl.ds(w, COLS, stride=4), :] = (high << 16) | (low & 0xFFFF)

    for off in FAR:
        to = lax.rem(ay + off, COLS)
        pltpu.make_async_remote_copy(
            src_ref=slots.at[to],
            dst_ref=owned.at[ay],
            send_sem=two_send,
            recv_sem=two_recv,
            device_id=(ax, to),
            device_id_type=MESH,
        ).start()
    keep = pltpu.make_async_copy(slots.at[ay], owned.at[ay], local_sem.at[1])
    keep.start()
    keep.wait()
    sent = piece.at[pl.ds(0, COLS - 1)]
    pltpu.make_async_copy(sent, sent, one_send).wait()
    many = owned.at[pl.ds(0, COLS - 1)]
    pltpu.make_async_copy(many, many, two_recv).wait()

    out[...] = owned[...]
    sent = slots.at[pl.ds(0, COLS - 1)]
    pltpu.make_async_copy(sent, sent, two_send).wait()


def unpack(words, out_diag, out_coup):
    f32 = jnp.float32
    flat = words.reshape(4 * COLS, NZ)
    got = [flat[pl.ds(w, K, stride=4), :] for w in range(4)]
    rows = [(w << 16) >> 16 for w in got] + [w >> 16 for w in got]
    rows = [row.astype(f32) for row in rows]
    scale = jnp.exp2(rows[7]) * (1.0 / LEVELS)
    rows = [row * scale[:, r : r + 1] for r, row in enumerate(rows[:7])]
    for c in range(CAP):
        for half_row in range(2):
            for q in range(4):
                out_coup[c, half_row * 4 + q] = rows[2 * c + half_row][:, q * K : (q + 1) * K]
        out_diag[c] = rows[6][:, c * K : (c + 1) * K]


def shards(basis, phase_ids, phase_stiffness, owner_map):
    f32, bf16 = jnp.float32, jnp.bfloat16
    vmem = pltpu.VMEM
    dma = pltpu.SemaphoreType.DMA
    whole = pl.BlockSpec(memory_space=pltpu.VMEM)
    packed = pl.pallas_call(
        kernel,
        out_shape=jax.ShapeDtypeStruct((COLS, 4, NZ), jnp.int32),
        in_specs=[pl.BlockSpec(memory_space=pltpu.HBM)] * 4,
        out_specs=whole,
        scratch_shapes=[
            vmem((K * CX * CY, NZ), bf16),
            vmem((CX, CY, NZ), jnp.int32),
            vmem((1, 8), bf16),
            vmem((1, COLS), jnp.int32),
            vmem((K * PITCH, NZ), f32),
            vmem((CX + 2, CY, K, NZ), f32),
            vmem((CX + 2, CY, K, NZ), f32),
            vmem((CX, CY, K, NZ), bf16),
            vmem((2, CY, K, NZ), f32),
            vmem((CX + 2, K, NZ), f32),
            vmem((CX + 2, 24, NZ), f32),
            vmem((3, CX + 2, 24, NZ), f32),
            vmem((8, 8, NZ), f32),
            vmem((2, CX, NZ), f32),
            vmem((2, CX, NZ), f32),
            vmem((3, 2, 24, NZ), f32),
            vmem((3, 2, 32, NZ), f32),
            vmem((3, 2, 32, NZ), f32),
            vmem((2, CY, K, NZ), bf16),
            vmem((CX, K, NZ), bf16),
            vmem((4, K, NZ), bf16),
            vmem((13, CX, CY, NZ), f32),
            vmem((CX, CY, NZ), f32),
            vmem((2, 9, CY, NZ), f32),
            vmem((9, CX, NZ), f32),
            vmem((CX + 1, CY, 2 * K, NZ), bf16),
            vmem((2, CY, 2 * K, NZ), bf16),
            vmem((2, CX, 2 * K, NZ), bf16),
            vmem((2, CY, 2 * K, NZ), bf16),
            vmem((CX, 2 * K, NZ), bf16),
            vmem((4, 2 * K, NZ), bf16),
            vmem((K, 4, NZ), f32),
            vmem((COLS, 4, NZ), f32),
            vmem((COLS * 8, NZ), jnp.int32),
            vmem((COLS, 4, NZ), jnp.int32),
            vmem((COLS, 4, NZ), jnp.int32),
            dma((7,)),
            dma((8,)),
            dma((8,)),
            dma((7,)),
            dma((7,)),
            dma,
            dma,
            dma,
            dma,
            dma((2,)),
        ],
        compiler_params=pltpu.CompilerParams(
            collective_id=0, has_side_effects=True, vmem_limit_bytes=60 * 1024 * 1024
        ),
    )(
        basis.reshape(K * CX * CY, NZ),
        phase_ids,
        phase_stiffness.reshape(1, 8),
        owner_map,
    )
    diag, coup = pl.pallas_call(
        unpack,
        out_shape=(
            jax.ShapeDtypeStruct((CAP, K, K), f32),
            jax.ShapeDtypeStruct((CAP, 8, K, K), f32),
        ),
        in_specs=[whole],
        out_specs=(whole, whole),
    )(packed)
    return diag[None], coup[None]


def solution(mesh):
    return jax.shard_map(
        shards,
        mesh=mesh,
        in_specs=(P(None, "gx", "gy", None), P("gx", "gy", None), P(), P("gx", None)),
        out_specs=(P("gx", "gy", None, None), P("gx", "gy", None, None, None)),
        check_vma=False,
    )
```

```python
import functools

import jax
import jax.numpy as jnp
from jax import lax
from jax.experimental import pallas as pl
from jax.experimental.pallas import tpu as pltpu
from jax.sharding import PartitionSpec as P

CAP = 3
REACT = 0.1
REGIONS = ((-1, -1), (-1, 0), (-1, 1), (0, -1), (0, 1), (1, -1), (1, 0), (1, 1))
CORNERS = ((-1, -1), (-1, 1), (1, -1), (1, 1))
OFFSETS = [
    (ox, oy, oz)
    for ox in (-1, 0, 1)
    for oy in (-1, 0, 1)
    for oz in (-1, 0, 1)
    if (ox, oy, oz) != (0, 0, 0)
]
HALF = [o for o in OFFSETS if o[2] == 1] + [(0, 1, 0), (1, -1, 0), (1, 0, 0), (1, 1, 0)]
MESH = pl.DeviceIdType.MESH
K, CX, CY, NZ = 32, 16, 8, 128
ROWS, COLS = 16, 32
PITCH = 136
FAR = sorted(range(1, COLS), key=lambda off: -min(off % 16, 16 - off % 16))
BEFORE = 8
RING = COLS // 2
NEAR = sorted(
    [(d, f) for d in range(8) for f in range(2) if (d, f) != (3, 0)], key=lambda t: -abs(t[0] - 3)
)
LAST = (((1,), (1,)), ((), ()))


def split(value):
    high = value.astype(jnp.bfloat16)
    low = (value - high.astype(jnp.float32)).astype(jnp.bfloat16)
    return high, low


def kernel(
    basis,
    ids_hbm,
    phase_hbm,
    owner_hbm,
    out,
    raw,
    ids,
    phase,
    owner,
    stage,
    zf,
    zs,
    zb,
    zmx,
    zmy,
    kp,
    kz,
    kx,
    ky,
    kface,
    frame_x,
    frame_y,
    frame_own,
    hx,
    hy,
    hc,
    weights,
    dsum,
    wx,
    wy,
    yb,
    ex,
    ey,
    gx,
    gy,
    gc,
    piece,
    pieces,
    slots,
    owned,
    load_sem,
    ks_send,
    ks_recv,
    z_send,
    z_recv,
    one_send,
    one_recv,
    two_send,
    two_recv,
    local_sem,
):
    f32, bf16 = jnp.float32, jnp.bfloat16
    ax = lax.axis_index("gx")
    ay = lax.axis_index("gy")
    parity = lax.rem(ax, 2)
    parity_f = parity.astype(f32)

    def device(dx, dy):
        return (lax.rem(ax + dx + ROWS, ROWS), lax.rem(ay + dy + COLS, COLS))

    small = [
        pltpu.make_async_copy(ids_hbm, ids, load_sem.at[4]),
        pltpu.make_async_copy(phase_hbm, phase, load_sem.at[5]),
        pltpu.make_async_copy(owner_hbm, owner, load_sem.at[6]),
    ]
    loads = [
        pltpu.make_async_copy(
            basis.at[pl.ds(1024 * g, 1024)], raw.at[pl.ds(1024 * g, 1024)], load_sem.at[g]
        )
        for g in range(4)
    ]
    for copy in small + loads:
        copy.start()

    barrier = pltpu.get_barrier_semaphore()

    for off in FAR:
        pl.semaphore_signal(
            barrier, inc=1, device_id=(ax, lax.rem(ay + off, COLS)), device_id_type=MESH
        )
    for dx, dy in REGIONS:
        if dx != 0:
            pl.semaphore_signal(barrier, inc=1, device_id=device(dx, dy), device_id_type=MESH)

    kp[...] = jnp.zeros_like(kp)
    frame_own[...] = jnp.zeros_like(frame_own)
    frame_x[...] = jnp.zeros_like(frame_x)
    frame_y[...] = jnp.zeros_like(frame_y)
    zero = jnp.zeros((8, K, NZ), f32)
    for edge in (0, CX + 1):
        zf[edge] = zero
        zs[edge] = zero
    zmy[0] = zero[0]
    zmy[CX + 1] = zero[0]
    yb[0] = jnp.zeros((CY, 2 * K, NZ), bf16)

    for copy in small:
        copy.wait()
    table = phase[...].astype(f32)
    for x in range(CX):
        cell = ids[x]
        value = jnp.zeros((CY, NZ), f32)
        for p in range(8):
            value = jnp.where(cell == p, table[0:1, p : p + 1], value)
        kp[x + 1, 8:16, :] = value
    for side, y in ((0, 0), (1, CY - 1)):
        for x in range(CX):
            kface[side, x : x + 1, :] = kp[x + 1, 8 + y : 9 + y, :]

    for g in range(4):
        loads[g].wait()

        def widen(i, carry, g=g):
            at = pl.multiple_of(1024 * g + i * 128, 128)
            to = pl.multiple_of(PITCH * 8 * g + i * PITCH, 8)
            stage[pl.ds(to, 128), :] = raw[pl.ds(at, 128), :].astype(f32)
            return carry

        lax.fori_loop(0, 8, widen, 0)

    def turn(x, carry):
        for y in range(CY):
            r = x * CY + y
            slab = jnp.concatenate(
                [stage[pl.ds(8 * PITCH * g + r, 8, stride=PITCH), :] for g in range(4)], axis=0
            )
            zf[x + 1, y] = slab
            zs[x + 1, y] = pltpu.roll(slab, NZ - 1, 1)
            zb[x, y] = slab.astype(bf16)
        return carry

    lax.fori_loop(0, CX, turn, 0, unroll=4)

    def harmonic(own, near, o):
        coef = 2.0 / (9.0 * (o[0] * o[0] + o[1] * o[1] + o[2] * o[2]))
        return (coef * own) * near / jnp.maximum(own + near, 0.05)

    def below(value):
        lane = lax.broadcasted_iota(jnp.int32, value.shape, 1)
        return jnp.where(lane == 0, 0.0, pltpu.roll(value, 1, 1))

    def above(value):
        lane = lax.broadcasted_iota(jnp.int32, value.shape, 1)
        return jnp.where(lane == NZ - 1, 0.0, pltpu.roll(value, NZ - 1, 1))

    for x in range(CX + 2):
        row = kp[x]
        kz[0, x] = below(row)
        kz[1, x] = row
        kz[2, x] = above(row)

    def weigh(x, carry):
        own = kp[x + 1, 8:16, :]
        total = REACT * own
        for o in OFFSETS:
            near = kz[o[2] + 1, x + 1 + o[0], 8 + o[1] : 16 + o[1], :]
            weight = harmonic(own, near, o)
            if o in HALF:
                weights[HALF.index(o), x] = weight
            total = total + weight
        dsum[x] = 0.5 * total
        return carry

    lax.fori_loop(0, CX, weigh, 0, unroll=2)

    def contract(x, slot):
        left = jnp.concatenate([yb[slot, y] for y in range(CY)], axis=1)
        right = jnp.concatenate([zb[x, y] for y in range(CY)], axis=1)
        return lax.dot_general(left, right, LAST, preferred_element_type=f32)

    def interior(x, acc):
        acc = acc + contract(jnp.maximum(x - 1, 0), x)
        for y in range(CY):
            value = dsum[x, y : y + 1, :] * zf[x + 1, y]
            for i, (ox, oy, oz) in enumerate(HALF):
                if not 0 <= y + oy < CY:
                    continue
                field = zf if oz == 0 else zs
                w = weights[i, x, y : y + 1, :]
                value = value - w * field[x + 1 + ox, y + oy]
            high, low = split(value)
            yb[x + 1, y, 0:K, :] = high
            yb[x + 1, y, K : 2 * K, :] = low
        return acc

    acc = lax.fori_loop(0, BEFORE, interior, jnp.zeros((2 * K, K), f32), unroll=4)

    pl.semaphore_wait(barrier, COLS - 1 + 6)

    sends = []
    for i, (dx, dy) in enumerate(REGIONS):
        other = REGIONS.index((-dx, -dy))
        if dx == 0:
            src, dst = kface.at[0 if dy < 0 else 1], ky.at[0 if dy > 0 else 1]
        else:
            src, dst = kp.at[1 if dx < 0 else CX, pl.ds(8, 8), :], kx.at[other]
        sends.append(
            pltpu.make_async_remote_copy(
                src_ref=src,
                dst_ref=dst,
                send_sem=ks_send.at[i],
                recv_sem=ks_recv.at[other],
                device_id=device(dx, dy),
                device_id_type=MESH,
            )
        )
    moves = [
        pltpu.make_async_remote_copy(
            src_ref=zb.at[:, 7 - 7 * parity],
            dst_ref=hy,
            send_sem=z_send.at[0],
            recv_sem=z_recv.at[0],
            device_id=(ax, lax.rem(ay + 1 - 2 * parity + COLS, COLS)),
            device_id_type=MESH,
        )
    ]
    for side, dx in ((0, -1), (1, 1)):
        moves.append(
            pltpu.make_async_remote_copy(
                src_ref=zb.at[0 if dx < 0 else CX - 1],
                dst_ref=hx.at[1 - side],
                send_sem=z_send.at[1 + side],
                recv_sem=z_recv.at[2 - side],
                device_id=device(dx, 0),
                device_id_type=MESH,
            )
        )
    for c, (dx, dy) in enumerate(CORNERS):
        moves.append(
            pltpu.make_async_remote_copy(
                src_ref=zb.at[0 if dx < 0 else CX - 1, 0 if dy < 0 else CY - 1],
                dst_ref=hc.at[3 - c],
                send_sem=z_send.at[3 + c],
                recv_sem=z_recv.at[6 - c],
                device_id=device(dx, dy),
                device_id_type=MESH,
            )
        )
    for copy in sends + moves:
        copy.start()

    acc = lax.fori_loop(BEFORE, CX, interior, acc, unroll=4)
    acc = acc + contract(CX - 1, CX)

    for copy in sends:
        copy.wait()
    low_x = (ax > 0).astype(f32)
    high_x = (ax < ROWS - 1).astype(f32)
    low_y = (ay > 0).astype(f32)
    high_y = (ay < COLS - 1).astype(f32)
    for side, dx, keep in ((0, -1, low_x), (1, 1, high_x)):
        near = kx[REGIONS.index((dx, 0))] * keep
        frame_x[1, side, 8:16, :] = near
    for side, dy, keep in ((0, -1, low_y), (1, 1, high_y)):
        y = 7 if dy < 0 else 0
        frame_y[1, side, 8:24, :] = ky[side] * keep
        for at, dx, keep_x in ((7, -1, low_x), (24, 1, high_x)):
            corner = kx[REGIONS.index((dx, dy)), y : y + 1, :]
            frame_y[1, side, at : at + 1, :] = corner * (keep * keep_x)
        frame_own[1, side, 8:24, :] = kface[side]
    for frame in (frame_x, frame_y, frame_own):
        for side in range(2):
            row = frame[1, side]
            frame[0, side] = below(row)
            frame[2, side] = above(row)

    NINE = [(i, j) for i in (-1, 0, 1) for j in (-1, 0, 1)]
    for side, dx in ((0, -1), (1, 1)):
        x = 0 if dx < 0 else CX - 1
        own = kp[x + 1, 8:16, :]
        total = jnp.zeros_like(own)
        for oy, oz in NINE:
            near = frame_x[oz + 1, side, 8 + oy : 16 + oy, :]
            total = total + harmonic(own, near, (dx, oy, oz))
        for y in range(CY):
            high, low = split(total[y : y + 1] * zf[x + 1, y])
            ex[side, y, 0:K, :] = high
            ex[side, y, K : 2 * K, :] = low
    for side, dy in ((0, -1), (1, 1)):
        own = kface[side]
        total = jnp.zeros_like(own)
        for ox, oz in NINE:
            near = frame_y[oz + 1, side, 8 + ox : 24 + ox, :]
            total = total + harmonic(own, near, (ox, dy, oz))
        for x in range(CX):
            high, low = split(total[x : x + 1] * zf[x + 1, 0 if dy < 0 else CY - 1])
            ey[side, x, 0:K, :] = high
            ey[side, x, K : 2 * K, :] = low
    outer = jnp.zeros((2 * K, K), f32)
    for side in range(2):
        x = 0 if side == 0 else CX - 1
        y = 0 if side == 0 else CY - 1
        outer = outer + lax.dot_general(
            jnp.concatenate([ex[side, i] for i in range(CY)], axis=1),
            jnp.concatenate([zb[x, i] for i in range(CY)], axis=1),
            LAST,
            preferred_element_type=f32,
        )
        outer = outer + lax.dot_general(
            jnp.concatenate([ey[side, i] for i in range(CX)], axis=1),
            jnp.concatenate([zb[i, y] for i in range(CX)], axis=1),
            LAST,
            preferred_element_type=f32,
        )
    half = acc[:K] + acc[K:]
    diagonal = (half + half.T + outer[:K] + outer[K:]) * (1.0 / (CX * CY * NZ))

    for side, dx in ((0, -1), (1, 1)):
        x = 0 if dx < 0 else CX - 1
        for y in range(CY):
            zmx[side, y] = pltpu.roll(zf[x + 1, y], 1, 1)
        own = frame_x[1, side, 8:16, :]
        for i, (oy, oz) in enumerate(NINE):
            near = kz[oz + 1, x + 1, 8 + oy : 16 + oy, :]
            wx[side, i] = harmonic(own, near, (dx, oy, oz))
        for y in range(CY):
            value = jnp.zeros((K, NZ), f32)
            for i, (oy, oz) in enumerate(NINE):
                if not 0 <= y + oy < CY:
                    continue
                field = (zmx[side, y + oy], zf[x + 1, y + oy], zs[x + 1, y + oy])[oz + 1]
                value = value - wx[side, i, y : y + 1, :] * field
            high, low = split(value)
            gx[side, y, 0:K, :] = high
            gx[side, y, K : 2 * K, :] = low
    for c, (dx, dy) in enumerate(CORNERS):
        x = 0 if dx < 0 else CX - 1
        y = 0 if dy < 0 else CY - 1
        side = 0 if dx < 0 else 1
        at = 7 if dx < 0 else 24
        own = frame_y[1, 0 if dy < 0 else 1, at : at + 1, :]
        value = jnp.zeros((K, NZ), f32)
        for oz in (-1, 0, 1):
            near = kz[oz + 1, x + 1, 8 + y : 9 + y, :]
            field = (zmx[side, y], zf[x + 1, y], zs[x + 1, y])[oz + 1]
            value = value - harmonic(own, near, (dx, dy, oz)) * field
        high, low = split(value)
        gc[c, 0:K, :] = high
        gc[c, K : 2 * K, :] = low
    y_edge = 7 * parity
    own = frame_y[1, parity, 8:24, :]
    for i, (ox, oz) in enumerate(NINE):
        near = frame_own[oz + 1, parity, 8 + ox : 24 + ox, :]
        wy[i] = harmonic(own, near, (ox, 1, oz))

    def lower(x, carry):
        zmy[x + 1] = pltpu.roll(zf[x + 1, y_edge], 1, 1)
        return carry

    lax.fori_loop(0, CX, lower, 0, unroll=4)

    def face(x, carry):
        value = jnp.zeros((K, NZ), f32)
        for i, (ox, oz) in enumerate(NINE):
            at = x + 1 + ox
            field = (zmy[at], zf[at, y_edge], zs[at, y_edge])[oz + 1]
            value = value - wy[i, pl.ds(x, 1), :] * field
        high, low = split(value)
        gy[x, 0:K, :] = high
        gy[x, K : 2 * K, :] = low
        return carry

    lax.fori_loop(0, CX, face, 0, unroll=4)

    width = COLS
    own_row = jnp.broadcast_to(owner[...], (width, width))
    i_sub = lax.broadcasted_iota(jnp.int32, (width, width), 0)
    i_lane = lax.broadcasted_iota(jnp.int32, (width, width), 1)
    own_f = own_row.astype(f32)
    own_col = jnp.sum(jnp.where(i_sub == i_lane, own_f, 0.0), axis=1, keepdims=True)
    before = (own_col == own_f) & (i_sub < i_lane)
    rank = jnp.sum(jnp.where(before, 1.0, 0.0), axis=0, keepdims=True)
    code = jnp.broadcast_to(own_f[0:1] * 4.0 + rank, (8, width)).astype(bf16)
    wide_n = 8 * width
    e_sub = lax.broadcasted_iota(jnp.int32, (width, wide_n), 0)
    e_lane = lax.broadcasted_iota(jnp.int32, (width, wide_n), 1)
    step = 2 * parity - 1
    e_from = e_lane // 8 + jnp.where(e_lane % 4 == 3, step, 0)
    expand = jnp.where(e_from == e_sub, 1.0, 0.0).astype(bf16)
    wide = jnp.dot(code, expand, preferred_element_type=f32)[0:1].astype(jnp.int32)
    wide_owner = wide // 4
    wide_rank = wide - wide_owner * 4
    lane1 = lax.broadcasted_iota(jnp.int32, (1, wide_n), 1)
    part = lane1 % 4
    row = jnp.where(part == 2, 6, wide_rank * 2 + jnp.where(part == 3, 1 - parity, part))
    place = (wide_owner % RING - ay % RING + RING + 3) % RING
    target = place * 32 + (wide_owner // RING) * 16 + ((lane1 // 4) % 2) * 8 + row
    end = (lane1 // 8 + step < 0) | (lane1 // 8 + step >= width)
    target = jnp.where((place >= 8) | ((part == 3) & end), -1, target)
    p_sub = lax.broadcasted_iota(jnp.int32, (16 * 16, wide_n), 0)
    route = jnp.where(p_sub == target, 1.0, 0.0).astype(bf16)
    my_rank = jnp.sum(
        jnp.where(lax.broadcasted_iota(jnp.int32, (1, width), 1) == ay, rank, 0.0),
        axis=1,
        keepdims=True,
    )
    quarter = (lax.broadcasted_iota(jnp.int32, (K, NZ), 1) // K).astype(f32)

    for copy in moves:
        copy.wait()

    def meet(left, right):
        product = lax.dot_general(left, right, LAST, preferred_element_type=f32)
        return product[:K] + product[K:]

    blocks = {}
    for side, dx in ((0, -1), (1, 1)):
        blocks[(dx, 0)] = meet(
            jnp.concatenate([gx[side, y] for y in range(CY)], axis=1),
            jnp.concatenate([hx[side, y] for y in range(CY)], axis=1),
        )
    for c, region in enumerate(CORNERS):
        blocks[region] = meet(gc[c], hc[c])
    across = meet(
        jnp.concatenate([gy[x] for x in range(CX)], axis=1),
        jnp.concatenate([hy[x] for x in range(CX)], axis=1),
    )
    back = across.T
    none = jnp.zeros_like(back)
    rows = [
        jnp.concatenate(
            [blocks[(-1, -1)], blocks[(-1, 0)], blocks[(-1, 1)], across * (1.0 - parity_f)],
            axis=1,
        ),
        jnp.concatenate(
            [across * parity_f, blocks[(1, -1)], blocks[(1, 0)], blocks[(1, 1)]], axis=1
        ),
        jnp.where(quarter == my_rank, jnp.concatenate([diagonal] * 4, axis=1), 0.0),
        jnp.concatenate([back * (1.0 - parity_f), none, none, back * parity_f], axis=1),
    ]
    for l, value in enumerate(rows):
        piece.reshape(4 * K, NZ)[pl.ds(l, K, stride=4), :] = value

    def pair(to):
        return lax.rem(to, 8) * 2 + to // RING

    for off in FAR:
        to = lax.rem(ay + off, COLS)
        pltpu.make_async_remote_copy(
            src_ref=piece.at[pair(to)],
            dst_ref=pieces.at[ay],
            send_sem=one_send,
            recv_sem=one_recv,
            device_id=(ax, to),
            device_id_type=MESH,
        ).start()
    keep = pltpu.make_async_copy(piece.at[pair(ay)], pieces.at[ay], local_sem.at[0])
    keep.start()
    keep.wait()
    many = pieces.at[pl.ds(0, COLS - 1)]
    pltpu.make_async_copy(many, many, one_recv).wait()

    got = pieces.reshape(8 * COLS, NZ)[...]
    a1 = got.astype(bf16)
    rest = got - a1.astype(f32)
    a2 = rest.astype(bf16)
    a3 = (rest - a2.astype(f32)).astype(bf16)
    slots[...] = (
        jnp.dot(route, a1, preferred_element_type=f32)
        + jnp.dot(route, a2, preferred_element_type=f32)
        + jnp.dot(route, a3, preferred_element_type=f32)
    ).reshape(16, 16, NZ)

    half_row = ay // RING
    for d, f in NEAR:
        x_half = lax.rem(half_row + f, 2)
        to = x_half * RING + lax.rem(ay + d - 3 + RING, RING)
        pltpu.make_async_remote_copy(
            src_ref=slots.at[2 * d + x_half],
            dst_ref=owned.at[pair(ay)],
            send_sem=two_send,
            recv_sem=two_recv,
            device_id=(ax, to),
            device_id_type=MESH,
        ).start()
    keep = pltpu.make_async_copy(slots.at[6 + half_row], owned.at[pair(ay)], local_sem.at[1])
    keep.start()
    keep.wait()
    sent = pieces.at[pl.ds(0, COLS - 1)]
    pltpu.make_async_copy(sent, sent, one_send).wait()
    many = owned.at[pl.ds(0, 15)]
    pltpu.make_async_copy(many, many, two_recv).wait()
    out[...] = owned[...]
    sent = slots.at[pl.ds(0, 15)]
    pltpu.make_async_copy(sent, sent, two_send).wait()


def deal(owned, out_diag, out_coup):
    flat = owned.reshape(8 * K, NZ)
    for c in range(CAP):
        for half_row in range(2):
            value = flat[pl.ds(2 * c + half_row, K, stride=8), :]
            for q in range(4):
                out_coup[c, half_row * 4 + q] = value[:, q * K : (q + 1) * K]
    value = flat[pl.ds(6, K, stride=8), :]
    for c in range(CAP):
        out_diag[c] = value[:, c * K : (c + 1) * K]


def shards(basis, phase_ids, phase_stiffness, owner_map):
    f32, bf16 = jnp.float32, jnp.bfloat16
    vmem = pltpu.VMEM
    dma = pltpu.SemaphoreType.DMA
    whole = pl.BlockSpec(memory_space=pltpu.VMEM)
    owned = pl.pallas_call(
        kernel,
        out_shape=jax.ShapeDtypeStruct((16, 16, NZ), f32),
        in_specs=[pl.BlockSpec(memory_space=pltpu.HBM)] * 4,
        out_specs=whole,
        scratch_shapes=[
            vmem((K * CX * CY, NZ), bf16),
            vmem((CX, CY, NZ), jnp.int32),
            vmem((1, 8), bf16),
            vmem((1, COLS), jnp.int32),
            vmem((K * PITCH, NZ), f32),
            vmem((CX + 2, CY, K, NZ), f32),
            vmem((CX + 2, CY, K, NZ), f32),
            vmem((CX, CY, K, NZ), bf16),
            vmem((2, CY, K, NZ), f32),
            vmem((CX + 2, K, NZ), f32),
            vmem((CX + 2, 24, NZ), f32),
            vmem((3, CX + 2, 24, NZ), f32),
            vmem((8, 8, NZ), f32),
            vmem((2, CX, NZ), f32),
            vmem((2, CX, NZ), f32),
            vmem((3, 2, 24, NZ), f32),
            vmem((3, 2, 32, NZ), f32),
            vmem((3, 2, 32, NZ), f32),
            vmem((2, CY, K, NZ), bf16),
            vmem((CX, K, NZ), bf16),
            vmem((4, K, NZ), bf16),
            vmem((13, CX, CY, NZ), f32),
            vmem((CX, CY, NZ), f32),
            vmem((2, 9, CY, NZ), f32),
            vmem((9, CX, NZ), f32),
            vmem((CX + 1, CY, 2 * K, NZ), bf16),
            vmem((2, CY, 2 * K, NZ), bf16),
            vmem((2, CX, 2 * K, NZ), bf16),
            vmem((2, CY, 2 * K, NZ), bf16),
            vmem((CX, 2 * K, NZ), bf16),
            vmem((4, 2 * K, NZ), bf16),
            vmem((16, 8, NZ), f32),
            vmem((COLS, 8, NZ), f32),
            vmem((16, 16, NZ), f32),
            vmem((16, 16, NZ), f32),
            dma((7,)),
            dma((8,)),
            dma((8,)),
            dma((7,)),
            dma((7,)),
            dma,
            dma,
            dma,
            dma,
            dma((2,)),
        ],
        compiler_params=pltpu.CompilerParams(
            collective_id=0, has_side_effects=True, vmem_limit_bytes=60 * 1024 * 1024
        ),
    )(
        basis.reshape(K * CX * CY, NZ),
        phase_ids,
        phase_stiffness.reshape(1, 8),
        owner_map,
    )
    diag, coup = pl.pallas_call(
        deal,
        out_shape=(
            jax.ShapeDtypeStruct((CAP, K, K), f32),
            jax.ShapeDtypeStruct((CAP, 8, K, K), f32),
        ),
        in_specs=[whole],
        out_specs=(whole, whole),
    )(owned)
    return diag[None], coup[None]


def solution(mesh):
    return jax.shard_map(
        shards,
        mesh=mesh,
        in_specs=(P(None, "gx", "gy", None), P("gx", "gy", None), P(), P("gx", None)),
        out_specs=(P("gx", "gy", None, None), P("gx", "gy", None, None, None)),
        check_vma=False,
    )
```

```python
import functools

import jax
import jax.numpy as jnp
from jax import lax
from jax.experimental import pallas as pl
from jax.experimental.pallas import tpu as pltpu
from jax.sharding import PartitionSpec as P

CAP = 3
REACT = 0.1
REGIONS = ((-1, -1), (-1, 0), (-1, 1), (0, -1), (0, 1), (1, -1), (1, 0), (1, 1))
CORNERS = ((-1, -1), (-1, 1), (1, -1), (1, 1))
OFFSETS = [
    (ox, oy, oz)
    for ox in (-1, 0, 1)
    for oy in (-1, 0, 1)
    for oz in (-1, 0, 1)
    if (ox, oy, oz) != (0, 0, 0)
]
HALF = [o for o in OFFSETS if o[2] == 1] + [(0, 1, 0), (1, -1, 0), (1, 0, 0), (1, 1, 0)]
MESH = pl.DeviceIdType.MESH
K, CX, CY, NZ = 32, 16, 8, 128
ROWS, COLS = 16, 32
PITCH = 136
FAR = sorted(range(1, COLS), key=lambda off: -min(off % 16, 16 - off % 16))
BEFORE = 4
RING = COLS // 2
NEAR = sorted(
    [(d, f) for d in range(8) for f in range(2) if (d, f) != (3, 0)], key=lambda t: -abs(t[0] - 3)
)
LAST = (((1,), (1,)), ((), ()))


def split(value):
    high = value.astype(jnp.bfloat16)
    low = (value - high.astype(jnp.float32)).astype(jnp.bfloat16)
    return high, low


def kernel(
    basis,
    ids_hbm,
    phase_hbm,
    owner_hbm,
    out,
    raw,
    ids,
    phase,
    owner,
    stage,
    zf,
    zs,
    zb,
    zmx,
    zmy,
    kp,
    kz,
    kx,
    ky,
    kface,
    frame_x,
    frame_y,
    frame_own,
    hx,
    hy,
    hc,
    weights,
    dsum,
    wx,
    wy,
    yb,
    ex,
    ey,
    gx,
    gy,
    gc,
    route,
    mine,
    piece,
    pieces,
    slots,
    owned,
    load_sem,
    ks_send,
    ks_recv,
    z_send,
    z_recv,
    one_send,
    one_recv,
    two_send,
    two_recv,
    local_sem,
):
    f32, bf16 = jnp.float32, jnp.bfloat16
    ax = lax.axis_index("gx")
    ay = lax.axis_index("gy")
    parity = lax.rem(ax, 2)
    parity_f = parity.astype(f32)

    def device(dx, dy):
        return (lax.rem(ax + dx + ROWS, ROWS), lax.rem(ay + dy + COLS, COLS))

    small = [
        pltpu.make_async_copy(ids_hbm, ids, load_sem.at[4]),
        pltpu.make_async_copy(phase_hbm, phase, load_sem.at[5]),
        pltpu.make_async_copy(owner_hbm, owner, load_sem.at[6]),
    ]
    loads = [
        pltpu.make_async_copy(
            basis.at[pl.ds(1024 * g, 1024)], raw.at[pl.ds(1024 * g, 1024)], load_sem.at[g]
        )
        for g in range(4)
    ]
    for copy in small + loads:
        copy.start()

    barrier = pltpu.get_barrier_semaphore()

    for off in FAR:
        pl.semaphore_signal(
            barrier, inc=1, device_id=(ax, lax.rem(ay + off, COLS)), device_id_type=MESH
        )
    for dx, dy in REGIONS:
        if dx != 0:
            pl.semaphore_signal(barrier, inc=1, device_id=device(dx, dy), device_id_type=MESH)

    kp[...] = jnp.zeros_like(kp)
    frame_own[...] = jnp.zeros_like(frame_own)
    frame_x[...] = jnp.zeros_like(frame_x)
    frame_y[...] = jnp.zeros_like(frame_y)
    zero = jnp.zeros((8, K, NZ), f32)
    for edge in (0, CX + 1):
        zf[edge] = zero
        zs[edge] = zero
    zmy[0] = zero[0]
    zmy[CX + 1] = zero[0]
    yb[0] = jnp.zeros((CY, 2 * K, NZ), bf16)

    for copy in small:
        copy.wait()
    table = phase[...].astype(f32)
    for x in range(CX):
        cell = ids[x]
        value = jnp.zeros((CY, NZ), f32)
        for p in range(8):
            value = jnp.where(cell == p, table[0:1, p : p + 1], value)
        kp[x + 1, 8:16, :] = value
    for side, y in ((0, 0), (1, CY - 1)):
        for x in range(CX):
            kface[side, x : x + 1, :] = kp[x + 1, 8 + y : 9 + y, :]

    for g in range(4):
        loads[g].wait()

        def widen(i, carry, g=g):
            at = pl.multiple_of(1024 * g + i * 128, 128)
            to = pl.multiple_of(PITCH * 8 * g + i * PITCH, 8)
            stage[pl.ds(to, 128), :] = raw[pl.ds(at, 128), :].astype(f32)
            return carry

        lax.fori_loop(0, 8, widen, 0)

    def turn(x, carry):
        for y in range(CY):
            r = x * CY + y
            slab = jnp.concatenate(
                [stage[pl.ds(8 * PITCH * g + r, 8, stride=PITCH), :] for g in range(4)], axis=0
            )
            zf[x + 1, y] = slab
            zs[x + 1, y] = pltpu.roll(slab, NZ - 1, 1)
            zb[x, y] = slab.astype(bf16)
        return carry

    lax.fori_loop(0, CX, turn, 0, unroll=4)

    def harmonic(own, near, o):
        coef = 2.0 / (9.0 * (o[0] * o[0] + o[1] * o[1] + o[2] * o[2]))
        return (coef * own) * near / jnp.maximum(own + near, 0.05)

    def below(value):
        lane = lax.broadcasted_iota(jnp.int32, value.shape, 1)
        return jnp.where(lane == 0, 0.0, pltpu.roll(value, 1, 1))

    def above(value):
        lane = lax.broadcasted_iota(jnp.int32, value.shape, 1)
        return jnp.where(lane == NZ - 1, 0.0, pltpu.roll(value, NZ - 1, 1))

    for x in range(CX + 2):
        row = kp[x]
        kz[0, x] = below(row)
        kz[1, x] = row
        kz[2, x] = above(row)

    def weigh(x, carry):
        own = kp[x + 1, 8:16, :]
        total = REACT * own
        for o in OFFSETS:
            near = kz[o[2] + 1, x + 1 + o[0], 8 + o[1] : 16 + o[1], :]
            weight = harmonic(own, near, o)
            if o in HALF:
                weights[HALF.index(o), x] = weight
            total = total + weight
        dsum[x] = 0.5 * total
        return carry

    lax.fori_loop(0, CX, weigh, 0, unroll=2)

    def contract(x, slot):
        left = jnp.concatenate([yb[slot, y] for y in range(CY)], axis=1)
        right = jnp.concatenate([zb[x, y] for y in range(CY)], axis=1)
        return lax.dot_general(left, right, LAST, preferred_element_type=f32)

    def interior(x, acc):
        acc = acc + contract(jnp.maximum(x - 1, 0), x)
        for y in range(CY):
            value = dsum[x, y : y + 1, :] * zf[x + 1, y]
            for i, (ox, oy, oz) in enumerate(HALF):
                if not 0 <= y + oy < CY:
                    continue
                field = zf if oz == 0 else zs
                w = weights[i, x, y : y + 1, :]
                value = value - w * field[x + 1 + ox, y + oy]
            high, low = split(value)
            yb[x + 1, y, 0:K, :] = high
            yb[x + 1, y, K : 2 * K, :] = low
        return acc

    y_edge = 7 * parity

    def lower(x, carry):
        zmy[x + 1] = pltpu.roll(zf[x + 1, y_edge], 1, 1)
        return carry

    lax.fori_loop(0, CX, lower, 0, unroll=4)

    for side in range(2):
        for y in range(CY):
            zmx[side, y] = pltpu.roll(zf[1 if side == 0 else CX, y], 1, 1)
    for side in range(2):
        frame_own[1, side, 8:24, :] = kface[side]
        row = frame_own[1, side]
        frame_own[0, side] = below(row)
        frame_own[2, side] = above(row)

    width = COLS
    own_row = jnp.broadcast_to(owner[...], (width, width))
    i_sub = lax.broadcasted_iota(jnp.int32, (width, width), 0)
    i_lane = lax.broadcasted_iota(jnp.int32, (width, width), 1)
    own_f = own_row.astype(f32)
    own_col = jnp.sum(jnp.where(i_sub == i_lane, own_f, 0.0), axis=1, keepdims=True)
    before = (own_col == own_f) & (i_sub < i_lane)
    rank = jnp.sum(jnp.where(before, 1.0, 0.0), axis=0, keepdims=True)
    code = jnp.broadcast_to(own_f[0:1] * 4.0 + rank, (8, width)).astype(bf16)
    wide_n = 8 * width
    e_sub = lax.broadcasted_iota(jnp.int32, (width, wide_n), 0)
    e_lane = lax.broadcasted_iota(jnp.int32, (width, wide_n), 1)
    step = 2 * parity - 1
    e_from = e_lane // 8 + jnp.where(e_lane % 4 == 3, step, 0)
    expand = jnp.where(e_from == e_sub, 1.0, 0.0).astype(bf16)
    wide = jnp.dot(code, expand, preferred_element_type=f32)[0:1].astype(jnp.int32)
    wide_owner = wide // 4
    wide_rank = wide - wide_owner * 4
    lane1 = lax.broadcasted_iota(jnp.int32, (1, wide_n), 1)
    part = lane1 % 4
    row = jnp.where(part == 2, 6, wide_rank * 2 + jnp.where(part == 3, 1 - parity, part))
    place = (wide_owner % RING - ay % RING + RING + 3) % RING
    target = place * 32 + (wide_owner // RING) * 16 + ((lane1 // 4) % 2) * 8 + row
    end = (lane1 // 8 + step < 0) | (lane1 // 8 + step >= width)
    target = jnp.where((place >= 8) | ((part == 3) & end), -1, target)
    p_sub = lax.broadcasted_iota(jnp.int32, (16 * 16, wide_n), 0)
    route[...] = jnp.where(p_sub == target, 1.0, 0.0).astype(bf16)
    my_rank = jnp.sum(
        jnp.where(lax.broadcasted_iota(jnp.int32, (1, width), 1) == ay, rank, 0.0),
        axis=1,
        keepdims=True,
    )
    quarter = (lax.broadcasted_iota(jnp.int32, (K, NZ), 1) // K).astype(f32)
    mine[...] = jnp.where(quarter == my_rank, 1.0 / (CX * CY * NZ), 0.0)

    acc = lax.fori_loop(0, BEFORE, interior, jnp.zeros((2 * K, K), f32), unroll=4)

    pl.semaphore_wait(barrier, COLS - 1 + 6)

    sends = []
    for i, (dx, dy) in enumerate(REGIONS):
        other = REGIONS.index((-dx, -dy))
        if dx == 0:
            src, dst = kface.at[0 if dy < 0 else 1], ky.at[0 if dy > 0 else 1]
        else:
            src, dst = kp.at[1 if dx < 0 else CX, pl.ds(8, 8), :], kx.at[other]
        sends.append(
            pltpu.make_async_remote_copy(
                src_ref=src,
                dst_ref=dst,
                send_sem=ks_send.at[i],
                recv_sem=ks_recv.at[other],
                device_id=device(dx, dy),
                device_id_type=MESH,
            )
        )
    moves = [
        pltpu.make_async_remote_copy(
            src_ref=zb.at[:, 7 - 7 * parity],
            dst_ref=hy,
            send_sem=z_send.at[0],
            recv_sem=z_recv.at[0],
            device_id=(ax, lax.rem(ay + 1 - 2 * parity + COLS, COLS)),
            device_id_type=MESH,
        )
    ]
    for side, dx in ((0, -1), (1, 1)):
        moves.append(
            pltpu.make_async_remote_copy(
                src_ref=zb.at[0 if dx < 0 else CX - 1],
                dst_ref=hx.at[1 - side],
                send_sem=z_send.at[1 + side],
                recv_sem=z_recv.at[2 - side],
                device_id=device(dx, 0),
                device_id_type=MESH,
            )
        )
    for c, (dx, dy) in enumerate(CORNERS):
        moves.append(
            pltpu.make_async_remote_copy(
                src_ref=zb.at[0 if dx < 0 else CX - 1, 0 if dy < 0 else CY - 1],
                dst_ref=hc.at[3 - c],
                send_sem=z_send.at[3 + c],
                recv_sem=z_recv.at[6 - c],
                device_id=device(dx, dy),
                device_id_type=MESH,
            )
        )
    for copy in sends + moves:
        copy.start()

    acc = lax.fori_loop(BEFORE, CX, interior, acc, unroll=4)
    acc = acc + contract(CX - 1, CX)

    for copy in sends:
        copy.wait()
    low_x = (ax > 0).astype(f32)
    high_x = (ax < ROWS - 1).astype(f32)
    low_y = (ay > 0).astype(f32)
    high_y = (ay < COLS - 1).astype(f32)
    for side, dx, keep in ((0, -1, low_x), (1, 1, high_x)):
        near = kx[REGIONS.index((dx, 0))] * keep
        frame_x[1, side, 8:16, :] = near
    for side, dy, keep in ((0, -1, low_y), (1, 1, high_y)):
        y = 7 if dy < 0 else 0
        frame_y[1, side, 8:24, :] = ky[side] * keep
        for at, dx, keep_x in ((7, -1, low_x), (24, 1, high_x)):
            corner = kx[REGIONS.index((dx, dy)), y : y + 1, :]
            frame_y[1, side, at : at + 1, :] = corner * (keep * keep_x)
    for frame in (frame_x, frame_y):
        for side in range(2):
            row = frame[1, side]
            frame[0, side] = below(row)
            frame[2, side] = above(row)

    NINE = [(i, j) for i in (-1, 0, 1) for j in (-1, 0, 1)]
    for side, dx in ((0, -1), (1, 1)):
        x = 0 if dx < 0 else CX - 1
        own = kp[x + 1, 8:16, :]
        total = jnp.zeros_like(own)
        for oy, oz in NINE:
            near = frame_x[oz + 1, side, 8 + oy : 16 + oy, :]
            total = total + harmonic(own, near, (dx, oy, oz))
        for y in range(CY):
            high, low = split(total[y : y + 1] * zf[x + 1, y])
            ex[side, y, 0:K, :] = high
            ex[side, y, K : 2 * K, :] = low
    for side, dy in ((0, -1), (1, 1)):
        own = kface[side]
        total = jnp.zeros_like(own)
        for ox, oz in NINE:
            near = frame_y[oz + 1, side, 8 + ox : 24 + ox, :]
            total = total + harmonic(own, near, (ox, dy, oz))
        for x in range(CX):
            high, low = split(total[x : x + 1] * zf[x + 1, 0 if dy < 0 else CY - 1])
            ey[side, x, 0:K, :] = high
            ey[side, x, K : 2 * K, :] = low
    outer = jnp.zeros((2 * K, K), f32)
    for side in range(2):
        x = 0 if side == 0 else CX - 1
        y = 0 if side == 0 else CY - 1
        outer = outer + lax.dot_general(
            jnp.concatenate([ex[side, i] for i in range(CY)], axis=1),
            jnp.concatenate([zb[x, i] for i in range(CY)], axis=1),
            LAST,
            preferred_element_type=f32,
        )
        outer = outer + lax.dot_general(
            jnp.concatenate([ey[side, i] for i in range(CX)], axis=1),
            jnp.concatenate([zb[i, y] for i in range(CX)], axis=1),
            LAST,
            preferred_element_type=f32,
        )
    half = acc[:K] + acc[K:]
    diagonal = half + half.T + outer[:K] + outer[K:]
    piece.reshape(4 * K, NZ)[pl.ds(2, K, stride=4), :] = mine[...] * jnp.concatenate(
        [diagonal] * 4, axis=1
    )

    for side, dx in ((0, -1), (1, 1)):
        x = 0 if dx < 0 else CX - 1
        own = frame_x[1, side, 8:16, :]
        for i, (oy, oz) in enumerate(NINE):
            near = kz[oz + 1, x + 1, 8 + oy : 16 + oy, :]
            wx[side, i] = harmonic(own, near, (dx, oy, oz))
        for y in range(CY):
            value = jnp.zeros((K, NZ), f32)
            for i, (oy, oz) in enumerate(NINE):
                if not 0 <= y + oy < CY:
                    continue
                field = (zmx[side, y + oy], zf[x + 1, y + oy], zs[x + 1, y + oy])[oz + 1]
                value = value - wx[side, i, y : y + 1, :] * field
            high, low = split(value)
            gx[side, y, 0:K, :] = high
            gx[side, y, K : 2 * K, :] = low
    for c, (dx, dy) in enumerate(CORNERS):
        x = 0 if dx < 0 else CX - 1
        y = 0 if dy < 0 else CY - 1
        side = 0 if dx < 0 else 1
        at = 7 if dx < 0 else 24
        own = frame_y[1, 0 if dy < 0 else 1, at : at + 1, :]
        value = jnp.zeros((K, NZ), f32)
        for oz in (-1, 0, 1):
            near = kz[oz + 1, x + 1, 8 + y : 9 + y, :]
            field = (zmx[side, y], zf[x + 1, y], zs[x + 1, y])[oz + 1]
            value = value - harmonic(own, near, (dx, dy, oz)) * field
        high, low = split(value)
        gc[c, 0:K, :] = high
        gc[c, K : 2 * K, :] = low
    own = frame_y[1, parity, 8:24, :]
    for i, (ox, oz) in enumerate(NINE):
        near = frame_own[oz + 1, parity, 8 + ox : 24 + ox, :]
        wy[i] = harmonic(own, near, (ox, 1, oz))

    def face(x, carry):
        value = jnp.zeros((K, NZ), f32)
        for i, (ox, oz) in enumerate(NINE):
            at = x + 1 + ox
            field = (zmy[at], zf[at, y_edge], zs[at, y_edge])[oz + 1]
            value = value - wy[i, pl.ds(x, 1), :] * field
        high, low = split(value)
        gy[x, 0:K, :] = high
        gy[x, K : 2 * K, :] = low
        return carry

    lax.fori_loop(0, CX, face, 0, unroll=CX)

    for copy in moves:
        copy.wait()

    def meet(left, right):
        product = lax.dot_general(left, right, LAST, preferred_element_type=f32)
        return product[:K] + product[K:]

    blocks = {}
    for side, dx in ((0, -1), (1, 1)):
        blocks[(dx, 0)] = meet(
            jnp.concatenate([gx[side, y] for y in range(CY)], axis=1),
            jnp.concatenate([hx[side, y] for y in range(CY)], axis=1),
        )
    for c, region in enumerate(CORNERS):
        blocks[region] = meet(gc[c], hc[c])
    across = meet(
        jnp.concatenate([gy[x] for x in range(CX)], axis=1),
        jnp.concatenate([hy[x] for x in range(CX)], axis=1),
    )
    back = across.T
    none = jnp.zeros_like(back)
    rows = [
        jnp.concatenate(
            [blocks[(-1, -1)], blocks[(-1, 0)], blocks[(-1, 1)], across * (1.0 - parity_f)],
            axis=1,
        ),
        jnp.concatenate(
            [across * parity_f, blocks[(1, -1)], blocks[(1, 0)], blocks[(1, 1)]], axis=1
        ),
        jnp.concatenate([back * (1.0 - parity_f), none, none, back * parity_f], axis=1),
    ]
    for l, value in zip((0, 1, 3), rows):
        piece.reshape(4 * K, NZ)[pl.ds(l, K, stride=4), :] = value

    def pair(to):
        return lax.rem(to, 8) * 2 + to // RING

    for off in FAR:
        to = lax.rem(ay + off, COLS)
        pltpu.make_async_remote_copy(
            src_ref=piece.at[pair(to)],
            dst_ref=pieces.at[ay],
            send_sem=one_send,
            recv_sem=one_recv,
            device_id=(ax, to),
            device_id_type=MESH,
        ).start()
    keep = pltpu.make_async_copy(piece.at[pair(ay)], pieces.at[ay], local_sem.at[0])
    keep.start()
    keep.wait()
    many = pieces.at[pl.ds(0, COLS - 1)]
    pltpu.make_async_copy(many, many, one_recv).wait()

    got = pieces.reshape(8 * COLS, NZ)[...]
    high, low = split(got)
    both = jnp.dot(
        route[...], jnp.concatenate([high, low], axis=1), preferred_element_type=f32
    )
    slots[...] = (both[:, :NZ] + both[:, NZ:]).reshape(16, 16, NZ)

    half_row = ay // RING
    for d, f in NEAR:
        x_half = lax.rem(half_row + f, 2)
        to = x_half * RING + lax.rem(ay + d - 3 + RING, RING)
        pltpu.make_async_remote_copy(
            src_ref=slots.at[2 * d + x_half],
            dst_ref=owned.at[pair(ay)],
            send_sem=two_send,
            recv_sem=two_recv,
            device_id=(ax, to),
            device_id_type=MESH,
        ).start()
    keep = pltpu.make_async_copy(slots.at[6 + half_row], owned.at[pair(ay)], local_sem.at[1])
    keep.start()
    keep.wait()
    sent = pieces.at[pl.ds(0, COLS - 1)]
    pltpu.make_async_copy(sent, sent, one_send).wait()
    many = owned.at[pl.ds(0, 15)]
    pltpu.make_async_copy(many, many, two_recv).wait()
    out[...] = owned[...]
    sent = slots.at[pl.ds(0, 15)]
    pltpu.make_async_copy(sent, sent, two_send).wait()


def deal(owned, out_diag, out_coup):
    flat = owned.reshape(8 * K, NZ)
    for c in range(CAP):
        for half_row in range(2):
            value = flat[pl.ds(2 * c + half_row, K, stride=8), :]
            for q in range(4):
                out_coup[c, half_row * 4 + q] = value[:, q * K : (q + 1) * K]
    value = flat[pl.ds(6, K, stride=8), :]
    for c in range(CAP):
        out_diag[c] = value[:, c * K : (c + 1) * K]


def shards(basis, phase_ids, phase_stiffness, owner_map):
    f32, bf16 = jnp.float32, jnp.bfloat16
    vmem = pltpu.VMEM
    dma = pltpu.SemaphoreType.DMA
    whole = pl.BlockSpec(memory_space=pltpu.VMEM)
    owned = pl.pallas_call(
        kernel,
        out_shape=jax.ShapeDtypeStruct((16, 16, NZ), f32),
        in_specs=[pl.BlockSpec(memory_space=pltpu.HBM)] * 4,
        out_specs=whole,
        scratch_shapes=[
            vmem((K * CX * CY, NZ), bf16),
            vmem((CX, CY, NZ), jnp.int32),
            vmem((1, 8), bf16),
            vmem((1, COLS), jnp.int32),
            vmem((K * PITCH, NZ), f32),
            vmem((CX + 2, CY, K, NZ), f32),
            vmem((CX + 2, CY, K, NZ), f32),
            vmem((CX, CY, K, NZ), bf16),
            vmem((2, CY, K, NZ), f32),
            vmem((CX + 2, K, NZ), f32),
            vmem((CX + 2, 24, NZ), f32),
            vmem((3, CX + 2, 24, NZ), f32),
            vmem((8, 8, NZ), f32),
            vmem((2, CX, NZ), f32),
            vmem((2, CX, NZ), f32),
            vmem((3, 2, 24, NZ), f32),
            vmem((3, 2, 32, NZ), f32),
            vmem((3, 2, 32, NZ), f32),
            vmem((2, CY, K, NZ), bf16),
            vmem((CX, K, NZ), bf16),
            vmem((4, K, NZ), bf16),
            vmem((13, CX, CY, NZ), f32),
            vmem((CX, CY, NZ), f32),
            vmem((2, 9, CY, NZ), f32),
            vmem((9, CX, NZ), f32),
            vmem((CX + 1, CY, 2 * K, NZ), bf16),
            vmem((2, CY, 2 * K, NZ), bf16),
            vmem((2, CX, 2 * K, NZ), bf16),
            vmem((2, CY, 2 * K, NZ), bf16),
            vmem((CX, 2 * K, NZ), bf16),
            vmem((4, 2 * K, NZ), bf16),
            vmem((256, 256), bf16),
            vmem((K, NZ), f32),
            vmem((16, 8, NZ), f32),
            vmem((COLS, 8, NZ), f32),
            vmem((16, 16, NZ), f32),
            vmem((16, 16, NZ), f32),
            dma((7,)),
            dma((8,)),
            dma((8,)),
            dma((7,)),
            dma((7,)),
            dma,
            dma,
            dma,
            dma,
            dma((2,)),
        ],
        compiler_params=pltpu.CompilerParams(
            collective_id=0, has_side_effects=True, vmem_limit_bytes=60 * 1024 * 1024
        ),
    )(
        basis.reshape(K * CX * CY, NZ),
        phase_ids,
        phase_stiffness.reshape(1, 8),
        owner_map,
    )
    diag, coup = pl.pallas_call(
        deal,
        out_shape=(
            jax.ShapeDtypeStruct((CAP, K, K), f32),
            jax.ShapeDtypeStruct((CAP, 8, K, K), f32),
        ),
        in_specs=[whole],
        out_specs=(whole, whole),
    )(owned)
    return diag[None], coup[None]


def solution(mesh):
    return jax.shard_map(
        shards,
        mesh=mesh,
        in_specs=(P(None, "gx", "gy", None), P("gx", "gy", None), P(), P("gx", None)),
        out_specs=(P("gx", "gy", None, None), P("gx", "gy", None, None, None)),
        check_vma=False,
    )
```

```python
import functools

import jax
import jax.numpy as jnp
from jax import lax
from jax.experimental import pallas as pl
from jax.experimental.pallas import tpu as pltpu
from jax.sharding import PartitionSpec as P

CAP = 3
REACT = 0.1
REGIONS = ((-1, -1), (-1, 0), (-1, 1), (0, -1), (0, 1), (1, -1), (1, 0), (1, 1))
CORNERS = ((-1, -1), (-1, 1), (1, -1), (1, 1))
OFFSETS = [
    (ox, oy, oz)
    for ox in (-1, 0, 1)
    for oy in (-1, 0, 1)
    for oz in (-1, 0, 1)
    if (ox, oy, oz) != (0, 0, 0)
]
HALF = [o for o in OFFSETS if o[2] == 1] + [(0, 1, 0), (1, -1, 0), (1, 0, 0), (1, 1, 0)]
MESH = pl.DeviceIdType.MESH
K, CX, CY, NZ = 32, 16, 8, 128
ROWS, COLS = 16, 32
PITCH = 136
FAR = sorted(range(1, COLS), key=lambda off: -min(off % 16, 16 - off % 16))
BEFORE = 4
RING = COLS // 2
NEAR = sorted(
    [(d, f) for d in range(8) for f in range(2) if (d, f) != (3, 0)], key=lambda t: -abs(t[0] - 3)
)
LAST = (((1,), (1,)), ((), ()))


def split(value):
    high = value.astype(jnp.bfloat16)
    low = (value - high.astype(jnp.float32)).astype(jnp.bfloat16)
    return high, low


def kernel(
    basis,
    ids_hbm,
    phase_hbm,
    owner_hbm,
    out,
    raw,
    ids,
    phase,
    owner,
    stage,
    zf,
    zs,
    zb,
    zmx,
    zmy,
    kp,
    kz,
    kx,
    ky,
    kface,
    frame_x,
    frame_y,
    frame_own,
    hx,
    hy,
    hc,
    weights,
    dsum,
    wx,
    wy,
    yb,
    ex,
    ey,
    gx,
    gy,
    gc,
    route,
    mine,
    piece,
    pieces,
    slots,
    owned,
    load_sem,
    ks_send,
    ks_recv,
    z_send,
    z_recv,
    one_send,
    one_recv,
    two_send,
    two_recv,
    local_sem,
):
    f32, bf16 = jnp.float32, jnp.bfloat16
    ax = lax.axis_index("gx")
    ay = lax.axis_index("gy")
    parity = lax.rem(ax, 2)
    parity_f = parity.astype(f32)

    def device(dx, dy):
        return (lax.rem(ax + dx + ROWS, ROWS), lax.rem(ay + dy + COLS, COLS))

    small = [
        pltpu.make_async_copy(ids_hbm, ids, load_sem.at[4]),
        pltpu.make_async_copy(phase_hbm, phase, load_sem.at[5]),
        pltpu.make_async_copy(owner_hbm, owner, load_sem.at[6]),
    ]
    loads = [
        pltpu.make_async_copy(
            basis.at[pl.ds(1024 * g, 1024)], raw.at[pl.ds(1024 * g, 1024)], load_sem.at[g]
        )
        for g in range(4)
    ]
    for copy in small + loads:
        copy.start()

    barrier = pltpu.get_barrier_semaphore()

    for off in FAR:
        pl.semaphore_signal(
            barrier, inc=1, device_id=(ax, lax.rem(ay + off, COLS)), device_id_type=MESH
        )
    for dx, dy in REGIONS:
        if dx != 0:
            pl.semaphore_signal(barrier, inc=1, device_id=device(dx, dy), device_id_type=MESH)

    kp[...] = jnp.zeros_like(kp)
    frame_own[...] = jnp.zeros_like(frame_own)
    frame_x[...] = jnp.zeros_like(frame_x)
    frame_y[...] = jnp.zeros_like(frame_y)
    zero = jnp.zeros((8, K, NZ), f32)
    for edge in (0, CX + 1):
        zf[edge] = zero
        zs[edge] = zero
    zmy[0] = zero[0]
    zmy[CX + 1] = zero[0]
    yb[0] = jnp.zeros((CY, 2 * K, NZ), bf16)

    for copy in small:
        copy.wait()
    table = phase[...].astype(f32)
    for x in range(CX):
        cell = ids[x]
        value = jnp.zeros((CY, NZ), f32)
        for p in range(8):
            value = jnp.where(cell == p, table[0:1, p : p + 1], value)
        kp[x + 1, 8:16, :] = value
    for side, y in ((0, 0), (1, CY - 1)):
        for x in range(CX):
            kface[side, x : x + 1, :] = kp[x + 1, 8 + y : 9 + y, :]

    for g in range(4):
        loads[g].wait()

        def widen(i, carry, g=g):
            at = pl.multiple_of(1024 * g + i * 128, 128)
            to = pl.multiple_of(PITCH * 8 * g + i * PITCH, 8)
            stage[pl.ds(to, 128), :] = raw[pl.ds(at, 128), :].astype(f32)
            return carry

        lax.fori_loop(0, 8, widen, 0)

    def turn(x, carry):
        for y in range(CY):
            r = x * CY + y
            slab = jnp.concatenate(
                [stage[pl.ds(8 * PITCH * g + r, 8, stride=PITCH), :] for g in range(4)], axis=0
            )
            zf[x + 1, y] = slab
            zs[x + 1, y] = pltpu.roll(slab, NZ - 1, 1)
            zb[x, y] = slab.astype(bf16)
        return carry

    lax.fori_loop(0, CX, turn, 0, unroll=4)

    def harmonic(own, near, o):
        coef = 2.0 / (9.0 * (o[0] * o[0] + o[1] * o[1] + o[2] * o[2]))
        return (coef * own) * near / jnp.maximum(own + near, 0.05)

    def below(value):
        lane = lax.broadcasted_iota(jnp.int32, value.shape, 1)
        return jnp.where(lane == 0, 0.0, pltpu.roll(value, 1, 1))

    def above(value):
        lane = lax.broadcasted_iota(jnp.int32, value.shape, 1)
        return jnp.where(lane == NZ - 1, 0.0, pltpu.roll(value, NZ - 1, 1))

    for x in range(CX + 2):
        row = kp[x]
        kz[0, x] = below(row)
        kz[1, x] = row
        kz[2, x] = above(row)

    def weigh(x, carry):
        own = kp[x + 1, 8:16, :]
        total = REACT * own
        for o in OFFSETS:
            near = kz[o[2] + 1, x + 1 + o[0], 8 + o[1] : 16 + o[1], :]
            weight = harmonic(own, near, o)
            if o in HALF:
                weights[HALF.index(o), x] = weight
            total = total + weight
        dsum[x] = 0.5 * total
        return carry

    lax.fori_loop(0, CX, weigh, 0, unroll=2)

    def contract(x, slot):
        left = jnp.concatenate([yb[slot, y] for y in range(CY)], axis=1)
        right = jnp.concatenate([zb[x, y] for y in range(CY)], axis=1)
        return lax.dot_general(left, right, LAST, preferred_element_type=f32)

    def interior(x, acc):
        acc = acc + contract(jnp.maximum(x - 1, 0), x)
        for y in range(CY):
            value = dsum[x, y : y + 1, :] * zf[x + 1, y]
            for i, (ox, oy, oz) in enumerate(HALF):
                if not 0 <= y + oy < CY:
                    continue
                field = zf if oz == 0 else zs
                w = weights[i, x, y : y + 1, :]
                value = value - w * field[x + 1 + ox, y + oy]
            high, low = split(value)
            yb[x + 1, y, 0:K, :] = high
            yb[x + 1, y, K : 2 * K, :] = low
        return acc

    y_edge = 7 * parity

    def lower(x, carry):
        zmy[x + 1] = pltpu.roll(zf[x + 1, y_edge], 1, 1)
        return carry

    lax.fori_loop(0, CX, lower, 0, unroll=4)

    for side in range(2):
        for y in range(CY):
            zmx[side, y] = pltpu.roll(zf[1 if side == 0 else CX, y], 1, 1)
    for side in range(2):
        frame_own[1, side, 8:24, :] = kface[side]
        row = frame_own[1, side]
        frame_own[0, side] = below(row)
        frame_own[2, side] = above(row)

    width = COLS
    own_row = jnp.broadcast_to(owner[...], (width, width))
    i_sub = lax.broadcasted_iota(jnp.int32, (width, width), 0)
    i_lane = lax.broadcasted_iota(jnp.int32, (width, width), 1)
    own_f = own_row.astype(f32)
    own_col = jnp.sum(jnp.where(i_sub == i_lane, own_f, 0.0), axis=1, keepdims=True)
    before = (own_col == own_f) & (i_sub < i_lane)
    rank = jnp.sum(jnp.where(before, 1.0, 0.0), axis=0, keepdims=True)
    code = jnp.broadcast_to(own_f[0:1] * 4.0 + rank, (8, width)).astype(bf16)
    wide_n = 8 * width
    e_sub = lax.broadcasted_iota(jnp.int32, (width, wide_n), 0)
    e_lane = lax.broadcasted_iota(jnp.int32, (width, wide_n), 1)
    step = 2 * parity - 1
    e_from = e_lane // 8 + jnp.where(e_lane % 4 == 3, step, 0)
    expand = jnp.where(e_from == e_sub, 1.0, 0.0).astype(bf16)
    wide = jnp.dot(code, expand, preferred_element_type=f32)[0:1].astype(jnp.int32)
    wide_owner = wide // 4
    wide_rank = wide - wide_owner * 4
    lane1 = lax.broadcasted_iota(jnp.int32, (1, wide_n), 1)
    part = lane1 % 4
    row = jnp.where(part == 2, 6, wide_rank * 2 + jnp.where(part == 3, 1 - parity, part))
    place = (wide_owner % RING - ay % RING + RING + 3) % RING
    target = place * 32 + (wide_owner // RING) * 16 + ((lane1 // 4) % 2) * 8 + row
    end = (lane1 // 8 + step < 0) | (lane1 // 8 + step >= width)
    target = jnp.where((place >= 8) | ((part == 3) & end), -1, target)
    p_sub = lax.broadcasted_iota(jnp.int32, (16 * 16, wide_n), 0)
    route[...] = jnp.where(p_sub == target, 1.0, 0.0).astype(bf16)
    my_rank = jnp.sum(
        jnp.where(lax.broadcasted_iota(jnp.int32, (1, width), 1) == ay, rank, 0.0),
        axis=1,
        keepdims=True,
    )
    quarter = (lax.broadcasted_iota(jnp.int32, (K, NZ), 1) // K).astype(f32)
    mine[...] = jnp.where(quarter == my_rank, 1.0 / (CX * CY * NZ), 0.0)

    acc = lax.fori_loop(0, BEFORE, interior, jnp.zeros((2 * K, K), f32), unroll=4)

    pl.semaphore_wait(barrier, COLS - 1 + 6)

    sends = []
    for i, (dx, dy) in enumerate(REGIONS):
        other = REGIONS.index((-dx, -dy))
        if dx == 0:
            src, dst = kface.at[0 if dy < 0 else 1], ky.at[0 if dy > 0 else 1]
        else:
            src, dst = kp.at[1 if dx < 0 else CX, pl.ds(8, 8), :], kx.at[other]
        sends.append(
            pltpu.make_async_remote_copy(
                src_ref=src,
                dst_ref=dst,
                send_sem=ks_send.at[i],
                recv_sem=ks_recv.at[other],
                device_id=device(dx, dy),
                device_id_type=MESH,
            )
        )
    moves = [
        pltpu.make_async_remote_copy(
            src_ref=zb.at[:, 7 - 7 * parity],
            dst_ref=hy,
            send_sem=z_send.at[0],
            recv_sem=z_recv.at[0],
            device_id=(ax, lax.rem(ay + 1 - 2 * parity + COLS, COLS)),
            device_id_type=MESH,
        )
    ]
    for side, dx in ((0, -1), (1, 1)):
        moves.append(
            pltpu.make_async_remote_copy(
                src_ref=zb.at[0 if dx < 0 else CX - 1],
                dst_ref=hx.at[1 - side],
                send_sem=z_send.at[1 + side],
                recv_sem=z_recv.at[2 - side],
                device_id=device(dx, 0),
                device_id_type=MESH,
            )
        )
    for c, (dx, dy) in enumerate(CORNERS):
        moves.append(
            pltpu.make_async_remote_copy(
                src_ref=zb.at[0 if dx < 0 else CX - 1, 0 if dy < 0 else CY - 1],
                dst_ref=hc.at[3 - c],
                send_sem=z_send.at[3 + c],
                recv_sem=z_recv.at[6 - c],
                device_id=device(dx, dy),
                device_id_type=MESH,
            )
        )
    for copy in sends + moves[3:] + moves[1:3] + moves[:1]:
        copy.start()

    acc = lax.fori_loop(BEFORE, CX, interior, acc, unroll=4)
    acc = acc + contract(CX - 1, CX)

    for copy in sends:
        copy.wait_recv()
    low_x = (ax > 0).astype(f32)
    high_x = (ax < ROWS - 1).astype(f32)
    low_y = (ay > 0).astype(f32)
    high_y = (ay < COLS - 1).astype(f32)
    for side, dx, keep in ((0, -1, low_x), (1, 1, high_x)):
        near = kx[REGIONS.index((dx, 0))] * keep
        frame_x[1, side, 8:16, :] = near
    for side, dy, keep in ((0, -1, low_y), (1, 1, high_y)):
        y = 7 if dy < 0 else 0
        frame_y[1, side, 8:24, :] = ky[side] * keep
        for at, dx, keep_x in ((7, -1, low_x), (24, 1, high_x)):
            corner = kx[REGIONS.index((dx, dy)), y : y + 1, :]
            frame_y[1, side, at : at + 1, :] = corner * (keep * keep_x)
    for frame in (frame_x, frame_y):
        for side in range(2):
            row = frame[1, side]
            frame[0, side] = below(row)
            frame[2, side] = above(row)

    NINE = [(i, j) for i in (-1, 0, 1) for j in (-1, 0, 1)]
    for side, dx in ((0, -1), (1, 1)):
        x = 0 if dx < 0 else CX - 1
        own = kp[x + 1, 8:16, :]
        total = jnp.zeros_like(own)
        for oy, oz in NINE:
            near = frame_x[oz + 1, side, 8 + oy : 16 + oy, :]
            total = total + harmonic(own, near, (dx, oy, oz))
        for y in range(CY):
            high, low = split(total[y : y + 1] * zf[x + 1, y])
            ex[side, y, 0:K, :] = high
            ex[side, y, K : 2 * K, :] = low
    for side, dy in ((0, -1), (1, 1)):
        own = kface[side]
        total = jnp.zeros_like(own)
        for ox, oz in NINE:
            near = frame_y[oz + 1, side, 8 + ox : 24 + ox, :]
            total = total + harmonic(own, near, (ox, dy, oz))
        for x in range(CX):
            high, low = split(total[x : x + 1] * zf[x + 1, 0 if dy < 0 else CY - 1])
            ey[side, x, 0:K, :] = high
            ey[side, x, K : 2 * K, :] = low
    outer = jnp.zeros((2 * K, K), f32)
    for side in range(2):
        x = 0 if side == 0 else CX - 1
        y = 0 if side == 0 else CY - 1
        outer = outer + lax.dot_general(
            jnp.concatenate([ex[side, i] for i in range(CY)], axis=1),
            jnp.concatenate([zb[x, i] for i in range(CY)], axis=1),
            LAST,
            preferred_element_type=f32,
        )
        outer = outer + lax.dot_general(
            jnp.concatenate([ey[side, i] for i in range(CX)], axis=1),
            jnp.concatenate([zb[i, y] for i in range(CX)], axis=1),
            LAST,
            preferred_element_type=f32,
        )
    half = acc[:K] + acc[K:]
    diagonal = half + half.T + outer[:K] + outer[K:]
    piece.reshape(4 * K, NZ)[pl.ds(2, K, stride=4), :] = mine[...] * jnp.concatenate(
        [diagonal] * 4, axis=1
    )

    for side, dx in ((0, -1), (1, 1)):
        x = 0 if dx < 0 else CX - 1
        own = frame_x[1, side, 8:16, :]
        for i, (oy, oz) in enumerate(NINE):
            near = kz[oz + 1, x + 1, 8 + oy : 16 + oy, :]
            wx[side, i] = harmonic(own, near, (dx, oy, oz))
        for y in range(CY):
            value = jnp.zeros((K, NZ), f32)
            for i, (oy, oz) in enumerate(NINE):
                if not 0 <= y + oy < CY:
                    continue
                field = (zmx[side, y + oy], zf[x + 1, y + oy], zs[x + 1, y + oy])[oz + 1]
                value = value - wx[side, i, y : y + 1, :] * field
            high, low = split(value)
            gx[side, y, 0:K, :] = high
            gx[side, y, K : 2 * K, :] = low
    for c, (dx, dy) in enumerate(CORNERS):
        x = 0 if dx < 0 else CX - 1
        y = 0 if dy < 0 else CY - 1
        side = 0 if dx < 0 else 1
        at = 7 if dx < 0 else 24
        own = frame_y[1, 0 if dy < 0 else 1, at : at + 1, :]
        value = jnp.zeros((K, NZ), f32)
        for oz in (-1, 0, 1):
            near = kz[oz + 1, x + 1, 8 + y : 9 + y, :]
            field = (zmx[side, y], zf[x + 1, y], zs[x + 1, y])[oz + 1]
            value = value - harmonic(own, near, (dx, dy, oz)) * field
        high, low = split(value)
        gc[c, 0:K, :] = high
        gc[c, K : 2 * K, :] = low
    own = frame_y[1, parity, 8:24, :]
    for i, (ox, oz) in enumerate(NINE):
        near = frame_own[oz + 1, parity, 8 + ox : 24 + ox, :]
        wy[i] = harmonic(own, near, (ox, 1, oz))

    def face(x, carry):
        value = jnp.zeros((K, NZ), f32)
        for i, (ox, oz) in enumerate(NINE):
            at = x + 1 + ox
            field = (zmy[at], zf[at, y_edge], zs[at, y_edge])[oz + 1]
            value = value - wy[i, pl.ds(x, 1), :] * field
        high, low = split(value)
        gy[x, 0:K, :] = high
        gy[x, K : 2 * K, :] = low
        return carry

    lax.fori_loop(0, CX, face, 0, unroll=CX)

    for copy in moves:
        copy.wait_recv()

    def meet(left, right):
        product = lax.dot_general(left, right, LAST, preferred_element_type=f32)
        return product[:K] + product[K:]

    blocks = {}
    for side, dx in ((0, -1), (1, 1)):
        blocks[(dx, 0)] = meet(
            jnp.concatenate([gx[side, y] for y in range(CY)], axis=1),
            jnp.concatenate([hx[side, y] for y in range(CY)], axis=1),
        )
    for c, region in enumerate(CORNERS):
        blocks[region] = meet(gc[c], hc[c])
    across = meet(
        jnp.concatenate([gy[x] for x in range(CX)], axis=1),
        jnp.concatenate([hy[x] for x in range(CX)], axis=1),
    )
    back = across.T
    none = jnp.zeros_like(back)
    rows = [
        jnp.concatenate(
            [blocks[(-1, -1)], blocks[(-1, 0)], blocks[(-1, 1)], across * (1.0 - parity_f)],
            axis=1,
        ),
        jnp.concatenate(
            [across * parity_f, blocks[(1, -1)], blocks[(1, 0)], blocks[(1, 1)]], axis=1
        ),
        jnp.concatenate([back * (1.0 - parity_f), none, none, back * parity_f], axis=1),
    ]
    for l, value in zip((0, 1, 3), rows):
        piece.reshape(4 * K, NZ)[pl.ds(l, K, stride=4), :] = value

    def pair(to):
        return lax.rem(to, 8) * 2 + to // RING

    for off in FAR:
        to = lax.rem(ay + off, COLS)
        pltpu.make_async_remote_copy(
            src_ref=piece.at[pair(to)],
            dst_ref=pieces.at[ay],
            send_sem=one_send,
            recv_sem=one_recv,
            device_id=(ax, to),
            device_id_type=MESH,
        ).start()
    keep = pltpu.make_async_copy(piece.at[pair(ay)], pieces.at[ay], local_sem.at[0])
    keep.start()
    keep.wait()
    many = pieces.at[pl.ds(0, COLS - 1)]
    pltpu.make_async_copy(many, many, one_recv).wait()

    got = pieces.reshape(8 * COLS, NZ)[...]
    high, low = split(got)
    both = jnp.dot(
        route[...], jnp.concatenate([high, low], axis=1), preferred_element_type=f32
    )
    slots[...] = (both[:, :NZ] + both[:, NZ:]).reshape(16, 16, NZ)

    half_row = ay // RING
    for d, f in NEAR:
        x_half = lax.rem(half_row + f, 2)
        to = x_half * RING + lax.rem(ay + d - 3 + RING, RING)
        pltpu.make_async_remote_copy(
            src_ref=slots.at[2 * d + x_half],
            dst_ref=owned.at[pair(ay)],
            send_sem=two_send,
            recv_sem=two_recv,
            device_id=(ax, to),
            device_id_type=MESH,
        ).start()
    keep = pltpu.make_async_copy(slots.at[6 + half_row], owned.at[pair(ay)], local_sem.at[1])
    keep.start()
    keep.wait()
    for copy in sends + moves:
        copy.wait_send()
    sent = pieces.at[pl.ds(0, COLS - 1)]
    pltpu.make_async_copy(sent, sent, one_send).wait()
    many = owned.at[pl.ds(0, 15)]
    pltpu.make_async_copy(many, many, two_recv).wait()
    keep = pltpu.make_async_copy(owned, out, local_sem.at[2])
    keep.start()
    sent = slots.at[pl.ds(0, 15)]
    pltpu.make_async_copy(sent, sent, two_send).wait()
    keep.wait()


def deal(owned, out_diag, out_coup):
    flat = owned.reshape(8 * K, NZ)
    for c in range(CAP):
        for half_row in range(2):
            value = flat[pl.ds(2 * c + half_row, K, stride=8), :]
            for q in range(4):
                out_coup[c, half_row * 4 + q] = value[:, q * K : (q + 1) * K]
    value = flat[pl.ds(6, K, stride=8), :]
    for c in range(CAP):
        out_diag[c] = value[:, c * K : (c + 1) * K]


def shards(basis, phase_ids, phase_stiffness, owner_map):
    f32, bf16 = jnp.float32, jnp.bfloat16
    vmem = pltpu.VMEM
    dma = pltpu.SemaphoreType.DMA
    whole = pl.BlockSpec(memory_space=pltpu.VMEM)
    owned = pl.pallas_call(
        kernel,
        out_shape=jax.ShapeDtypeStruct((16, 16, NZ), f32),
        in_specs=[pl.BlockSpec(memory_space=pltpu.HBM)] * 4,
        out_specs=pl.BlockSpec(memory_space=pltpu.HBM),
        scratch_shapes=[
            vmem((K * CX * CY, NZ), bf16),
            vmem((CX, CY, NZ), jnp.int32),
            vmem((1, 8), bf16),
            vmem((1, COLS), jnp.int32),
            vmem((K * PITCH, NZ), f32),
            vmem((CX + 2, CY, K, NZ), f32),
            vmem((CX + 2, CY, K, NZ), f32),
            vmem((CX, CY, K, NZ), bf16),
            vmem((2, CY, K, NZ), f32),
            vmem((CX + 2, K, NZ), f32),
            vmem((CX + 2, 24, NZ), f32),
            vmem((3, CX + 2, 24, NZ), f32),
            vmem((8, 8, NZ), f32),
            vmem((2, CX, NZ), f32),
            vmem((2, CX, NZ), f32),
            vmem((3, 2, 24, NZ), f32),
            vmem((3, 2, 32, NZ), f32),
            vmem((3, 2, 32, NZ), f32),
            vmem((2, CY, K, NZ), bf16),
            vmem((CX, K, NZ), bf16),
            vmem((4, K, NZ), bf16),
            vmem((13, CX, CY, NZ), f32),
            vmem((CX, CY, NZ), f32),
            vmem((2, 9, CY, NZ), f32),
            vmem((9, CX, NZ), f32),
            vmem((CX + 1, CY, 2 * K, NZ), bf16),
            vmem((2, CY, 2 * K, NZ), bf16),
            vmem((2, CX, 2 * K, NZ), bf16),
            vmem((2, CY, 2 * K, NZ), bf16),
            vmem((CX, 2 * K, NZ), bf16),
            vmem((4, 2 * K, NZ), bf16),
            vmem((256, 256), bf16),
            vmem((K, NZ), f32),
            vmem((16, 8, NZ), f32),
            vmem((COLS, 8, NZ), f32),
            vmem((16, 16, NZ), f32),
            vmem((16, 16, NZ), f32),
            dma((7,)),
            dma((8,)),
            dma((8,)),
            dma((7,)),
            dma((7,)),
            dma,
            dma,
            dma,
            dma,
            dma((3,)),
        ],
        compiler_params=pltpu.CompilerParams(
            collective_id=0, has_side_effects=True, vmem_limit_bytes=60 * 1024 * 1024
        ),
    )(
        basis.reshape(K * CX * CY, NZ),
        phase_ids,
        phase_stiffness.reshape(1, 8),
        owner_map,
    )
    diag, coup = pl.pallas_call(
        deal,
        out_shape=(
            jax.ShapeDtypeStruct((CAP, K, K), f32),
            jax.ShapeDtypeStruct((CAP, 8, K, K), f32),
        ),
        in_specs=[whole],
        out_specs=(whole, whole),
    )(owned)
    return diag[None], coup[None]


def solution(mesh):
    return jax.shard_map(
        shards,
        mesh=mesh,
        in_specs=(P(None, "gx", "gy", None), P("gx", "gy", None), P(), P("gx", None)),
        out_specs=(P("gx", "gy", None, None), P("gx", "gy", None, None, None)),
        check_vma=False,
    )
```

```python
import functools

import jax
import jax.numpy as jnp
from jax import lax
from jax.experimental import pallas as pl
from jax.experimental.pallas import tpu as pltpu
from jax.sharding import PartitionSpec as P

CAP = 3
REACT = 0.1
REGIONS = ((-1, -1), (-1, 0), (-1, 1), (0, -1), (0, 1), (1, -1), (1, 0), (1, 1))
CORNERS = ((-1, -1), (-1, 1), (1, -1), (1, 1))
OFFSETS = [
    (ox, oy, oz)
    for ox in (-1, 0, 1)
    for oy in (-1, 0, 1)
    for oz in (-1, 0, 1)
    if (ox, oy, oz) != (0, 0, 0)
]
HALF = [o for o in OFFSETS if o[2] == 1] + [(0, 1, 0), (1, -1, 0), (1, 0, 0), (1, 1, 0)]
MESH = pl.DeviceIdType.MESH
K, CX, CY, NZ = 32, 16, 8, 128
ROWS, COLS = 16, 32
PITCH = 136
FAR = sorted(range(1, COLS), key=lambda off: -min(off % 16, 16 - off % 16))
BEFORE = 4
RING = COLS // 2
NEAR = sorted(
    [(d, f) for d in range(8) for f in range(2) if (d, f) != (3, 0)], key=lambda t: -abs(t[0] - 3)
)
LAST = (((1,), (1,)), ((), ()))


def split(value):
    high = value.astype(jnp.bfloat16)
    low = (value - high.astype(jnp.float32)).astype(jnp.bfloat16)
    return high, low


def kernel(
    basis,
    ids_hbm,
    phase_hbm,
    owner_hbm,
    out,
    raw,
    ids,
    phase,
    owner,
    stage,
    zf,
    zs,
    zb,
    zmx,
    zmy,
    kp,
    kz,
    kx,
    ky,
    kface,
    frame_x,
    frame_y,
    frame_own,
    hx,
    hy,
    hc,
    weights,
    dsum,
    wx,
    wy,
    yb,
    ex,
    ey,
    gx,
    gy,
    gc,
    route,
    mine,
    piece,
    pieces,
    slots,
    owned,
    load_sem,
    ks_send,
    ks_recv,
    z_send,
    z_recv,
    one_send,
    one_recv,
    two_send,
    two_recv,
    local_sem,
):
    f32, bf16 = jnp.float32, jnp.bfloat16
    ax = lax.axis_index("gx")
    ay = lax.axis_index("gy")
    parity = lax.rem(ax, 2)
    parity_f = parity.astype(f32)

    def device(dx, dy):
        return (lax.rem(ax + dx + ROWS, ROWS), lax.rem(ay + dy + COLS, COLS))

    small = [
        pltpu.make_async_copy(ids_hbm, ids, load_sem.at[4]),
        pltpu.make_async_copy(phase_hbm, phase, load_sem.at[5]),
        pltpu.make_async_copy(owner_hbm, owner, load_sem.at[6]),
    ]
    loads = [
        pltpu.make_async_copy(
            basis.at[pl.ds(1024 * g, 1024)], raw.at[pl.ds(1024 * g, 1024)], load_sem.at[g]
        )
        for g in range(4)
    ]
    for copy in small + loads:
        copy.start()

    barrier = pltpu.get_barrier_semaphore()

    for off in FAR:
        pl.semaphore_signal(
            barrier, inc=1, device_id=(ax, lax.rem(ay + off, COLS)), device_id_type=MESH
        )
    for dx, dy in REGIONS:
        if dx != 0:
            pl.semaphore_signal(barrier, inc=1, device_id=device(dx, dy), device_id_type=MESH)

    kp[...] = jnp.zeros_like(kp)
    frame_own[...] = jnp.zeros_like(frame_own)
    frame_x[...] = jnp.zeros_like(frame_x)
    frame_y[...] = jnp.zeros_like(frame_y)
    zero = jnp.zeros((8, K, NZ), f32)
    for edge in (0, CX + 1):
        zf[edge] = zero
        zs[edge] = zero
    zmy[0] = zero[0]
    zmy[CX + 1] = zero[0]
    yb[0] = jnp.zeros((CY, 2 * K, NZ), bf16)

    for copy in small:
        copy.wait()
    table = phase[...].astype(f32)
    for x in range(CX):
        cell = ids[x]
        value = jnp.zeros((CY, NZ), f32)
        for p in range(8):
            value = jnp.where(cell == p, table[0:1, p : p + 1], value)
        kp[x + 1, 8:16, :] = value
    for side, y in ((0, 0), (1, CY - 1)):
        for x in range(CX):
            kface[side, x : x + 1, :] = kp[x + 1, 8 + y : 9 + y, :]

    for g in range(4):
        loads[g].wait()

        def widen(i, carry, g=g):
            at = pl.multiple_of(1024 * g + i * 128, 128)
            to = pl.multiple_of(PITCH * 8 * g + i * PITCH, 8)
            stage[pl.ds(to, 128), :] = raw[pl.ds(at, 128), :].astype(f32)
            return carry

        lax.fori_loop(0, 8, widen, 0)

    def turn(x, carry):
        for y in range(CY):
            r = x * CY + y
            slab = jnp.concatenate(
                [stage[pl.ds(8 * PITCH * g + r, 8, stride=PITCH), :] for g in range(4)], axis=0
            )
            zf[x + 1, y] = slab
            zs[x + 1, y] = pltpu.roll(slab, NZ - 1, 1)
            zb[x, y] = slab.astype(bf16)
        return carry

    lax.fori_loop(0, CX, turn, 0, unroll=4)

    def harmonic(own, near, o):
        coef = 2.0 / (9.0 * (o[0] * o[0] + o[1] * o[1] + o[2] * o[2]))
        return (coef * own) * near / jnp.maximum(own + near, 0.05)

    def below(value):
        lane = lax.broadcasted_iota(jnp.int32, value.shape, 1)
        return jnp.where(lane == 0, 0.0, pltpu.roll(value, 1, 1))

    def above(value):
        lane = lax.broadcasted_iota(jnp.int32, value.shape, 1)
        return jnp.where(lane == NZ - 1, 0.0, pltpu.roll(value, NZ - 1, 1))

    for x in range(CX + 2):
        row = kp[x]
        kz[0, x] = below(row)
        kz[1, x] = row
        kz[2, x] = above(row)

    def weigh(x, carry):
        own = kp[x + 1, 8:16, :]
        total = REACT * own
        for o in OFFSETS:
            near = kz[o[2] + 1, x + 1 + o[0], 8 + o[1] : 16 + o[1], :]
            weight = harmonic(own, near, o)
            if o in HALF:
                weights[HALF.index(o), x] = weight
            total = total + weight
        dsum[x] = 0.5 * total
        return carry

    lax.fori_loop(0, CX, weigh, 0, unroll=2)

    def contract(x, slot):
        left = jnp.concatenate([yb[slot, y] for y in range(CY)], axis=1)
        right = jnp.concatenate([zb[x, y] for y in range(CY)], axis=1)
        return lax.dot_general(left, right, LAST, preferred_element_type=f32)

    def interior(x, acc):
        acc = acc + contract(jnp.maximum(x - 1, 0), x)
        for y in range(CY):
            value = dsum[x, y : y + 1, :] * zf[x + 1, y]
            for i, (ox, oy, oz) in enumerate(HALF):
                if not 0 <= y + oy < CY:
                    continue
                field = zf if oz == 0 else zs
                w = weights[i, x, y : y + 1, :]
                value = value - w * field[x + 1 + ox, y + oy]
            high, low = split(value)
            yb[x + 1, y, 0:K, :] = high
            yb[x + 1, y, K : 2 * K, :] = low
        return acc

    y_edge = 7 * parity

    def lower(x, carry):
        zmy[x + 1] = pltpu.roll(zf[x + 1, y_edge], 1, 1)
        return carry

    lax.fori_loop(0, CX, lower, 0, unroll=4)

    for side in range(2):
        for y in range(CY):
            zmx[side, y] = pltpu.roll(zf[1 if side == 0 else CX, y], 1, 1)
    for side in range(2):
        frame_own[1, side, 8:24, :] = kface[side]
        row = frame_own[1, side]
        frame_own[0, side] = below(row)
        frame_own[2, side] = above(row)

    width = COLS
    own_row = jnp.broadcast_to(owner[...], (width, width))
    i_sub = lax.broadcasted_iota(jnp.int32, (width, width), 0)
    i_lane = lax.broadcasted_iota(jnp.int32, (width, width), 1)
    own_f = own_row.astype(f32)
    own_col = jnp.sum(jnp.where(i_sub == i_lane, own_f, 0.0), axis=1, keepdims=True)
    before = (own_col == own_f) & (i_sub < i_lane)
    rank = jnp.sum(jnp.where(before, 1.0, 0.0), axis=0, keepdims=True)
    code = jnp.broadcast_to(own_f[0:1] * 4.0 + rank, (8, width)).astype(bf16)
    wide_n = 8 * width
    e_sub = lax.broadcasted_iota(jnp.int32, (width, wide_n), 0)
    e_lane = lax.broadcasted_iota(jnp.int32, (width, wide_n), 1)
    step = 2 * parity - 1
    e_from = e_lane // 8 + jnp.where(e_lane % 4 == 3, step, 0)
    expand = jnp.where(e_from == e_sub, 1.0, 0.0).astype(bf16)
    wide = jnp.dot(code, expand, preferred_element_type=f32)[0:1].astype(jnp.int32)
    wide_owner = wide // 4
    wide_rank = wide - wide_owner * 4
    lane1 = lax.broadcasted_iota(jnp.int32, (1, wide_n), 1)
    part = lane1 % 4
    row = jnp.where(part == 2, 6, wide_rank * 2 + jnp.where(part == 3, 1 - parity, part))
    place = (wide_owner % RING - ay % RING + RING + 3) % RING
    target = place * 32 + (wide_owner // RING) * 16 + ((lane1 // 4) % 2) * 8 + row
    end = (lane1 // 8 + step < 0) | (lane1 // 8 + step >= width)
    target = jnp.where((place >= 8) | ((part == 3) & end), -1, target)
    p_sub = lax.broadcasted_iota(jnp.int32, (16 * 16, wide_n), 0)
    route[...] = jnp.where(p_sub == target, 1.0, 0.0).astype(bf16)
    my_rank = jnp.sum(
        jnp.where(lax.broadcasted_iota(jnp.int32, (1, width), 1) == ay, rank, 0.0),
        axis=1,
        keepdims=True,
    )
    quarter = (lax.broadcasted_iota(jnp.int32, (K, NZ), 1) // K).astype(f32)
    mine[...] = jnp.where(quarter == my_rank, 1.0 / (CX * CY * NZ), 0.0)

    acc = lax.fori_loop(0, BEFORE, interior, jnp.zeros((2 * K, K), f32), unroll=4)

    pl.semaphore_wait(barrier, COLS - 1 + 6)

    sends = []
    for i, (dx, dy) in enumerate(REGIONS):
        other = REGIONS.index((-dx, -dy))
        if dx == 0:
            src, dst = kface.at[0 if dy < 0 else 1], ky.at[0 if dy > 0 else 1]
        else:
            src, dst = kp.at[1 if dx < 0 else CX, pl.ds(8, 8), :], kx.at[other]
        sends.append(
            pltpu.make_async_remote_copy(
                src_ref=src,
                dst_ref=dst,
                send_sem=ks_send.at[i],
                recv_sem=ks_recv.at[other],
                device_id=device(dx, dy),
                device_id_type=MESH,
            )
        )
    moves = [
        pltpu.make_async_remote_copy(
            src_ref=zb.at[:, 7 - 7 * parity],
            dst_ref=hy,
            send_sem=z_send.at[0],
            recv_sem=z_recv.at[0],
            device_id=(ax, lax.rem(ay + 1 - 2 * parity + COLS, COLS)),
            device_id_type=MESH,
        )
    ]
    for side, dx in ((0, -1), (1, 1)):
        moves.append(
            pltpu.make_async_remote_copy(
                src_ref=zb.at[0 if dx < 0 else CX - 1],
                dst_ref=hx.at[1 - side],
                send_sem=z_send.at[1 + side],
                recv_sem=z_recv.at[2 - side],
                device_id=device(dx, 0),
                device_id_type=MESH,
            )
        )
    for c, (dx, dy) in enumerate(CORNERS):
        moves.append(
            pltpu.make_async_remote_copy(
                src_ref=zb.at[0 if dx < 0 else CX - 1, 0 if dy < 0 else CY - 1],
                dst_ref=hc.at[3 - c],
                send_sem=z_send.at[3 + c],
                recv_sem=z_recv.at[6 - c],
                device_id=device(dx, dy),
                device_id_type=MESH,
            )
        )
    for copy in sends + moves[3:] + moves[:1] + moves[1:3]:
        copy.start()

    acc = lax.fori_loop(BEFORE, CX, interior, acc, unroll=4)
    acc = acc + contract(CX - 1, CX)

    for copy in sends:
        copy.wait_recv()
    low_x = (ax > 0).astype(f32)
    high_x = (ax < ROWS - 1).astype(f32)
    low_y = (ay > 0).astype(f32)
    high_y = (ay < COLS - 1).astype(f32)
    for side, dx, keep in ((0, -1, low_x), (1, 1, high_x)):
        near = kx[REGIONS.index((dx, 0))] * keep
        frame_x[1, side, 8:16, :] = near
    for side, dy, keep in ((0, -1, low_y), (1, 1, high_y)):
        y = 7 if dy < 0 else 0
        frame_y[1, side, 8:24, :] = ky[side] * keep
        for at, dx, keep_x in ((7, -1, low_x), (24, 1, high_x)):
            corner = kx[REGIONS.index((dx, dy)), y : y + 1, :]
            frame_y[1, side, at : at + 1, :] = corner * (keep * keep_x)
    for frame in (frame_x, frame_y):
        for side in range(2):
            row = frame[1, side]
            frame[0, side] = below(row)
            frame[2, side] = above(row)

    NINE = [(i, j) for i in (-1, 0, 1) for j in (-1, 0, 1)]
    for side, dx in ((0, -1), (1, 1)):
        x = 0 if dx < 0 else CX - 1
        own = kp[x + 1, 8:16, :]
        total = jnp.zeros_like(own)
        for oy, oz in NINE:
            near = frame_x[oz + 1, side, 8 + oy : 16 + oy, :]
            total = total + harmonic(own, near, (dx, oy, oz))
        for y in range(CY):
            high, low = split(total[y : y + 1] * zf[x + 1, y])
            ex[side, y, 0:K, :] = high
            ex[side, y, K : 2 * K, :] = low
    for side, dy in ((0, -1), (1, 1)):
        own = kface[side]
        total = jnp.zeros_like(own)
        for ox, oz in NINE:
            near = frame_y[oz + 1, side, 8 + ox : 24 + ox, :]
            total = total + harmonic(own, near, (ox, dy, oz))
        for x in range(CX):
            high, low = split(total[x : x + 1] * zf[x + 1, 0 if dy < 0 else CY - 1])
            ey[side, x, 0:K, :] = high
            ey[side, x, K : 2 * K, :] = low
    outer = jnp.zeros((2 * K, K), f32)
    for side in range(2):
        x = 0 if side == 0 else CX - 1
        y = 0 if side == 0 else CY - 1
        outer = outer + lax.dot_general(
            jnp.concatenate([ex[side, i] for i in range(CY)], axis=1),
            jnp.concatenate([zb[x, i] for i in range(CY)], axis=1),
            LAST,
            preferred_element_type=f32,
        )
        outer = outer + lax.dot_general(
            jnp.concatenate([ey[side, i] for i in range(CX)], axis=1),
            jnp.concatenate([zb[i, y] for i in range(CX)], axis=1),
            LAST,
            preferred_element_type=f32,
        )
    half = acc[:K] + acc[K:]
    diagonal = half + half.T + outer[:K] + outer[K:]
    piece.reshape(4 * K, NZ)[pl.ds(2, K, stride=4), :] = mine[...] * jnp.concatenate(
        [diagonal] * 4, axis=1
    )

    for side, dx in ((0, -1), (1, 1)):
        x = 0 if dx < 0 else CX - 1
        own = frame_x[1, side, 8:16, :]
        for i, (oy, oz) in enumerate(NINE):
            near = kz[oz + 1, x + 1, 8 + oy : 16 + oy, :]
            wx[side, i] = harmonic(own, near, (dx, oy, oz))
        for y in range(CY):
            value = jnp.zeros((K, NZ), f32)
            for i, (oy, oz) in enumerate(NINE):
                if not 0 <= y + oy < CY:
                    continue
                field = (zmx[side, y + oy], zf[x + 1, y + oy], zs[x + 1, y + oy])[oz + 1]
                value = value - wx[side, i, y : y + 1, :] * field
            high, low = split(value)
            gx[side, y, 0:K, :] = high
            gx[side, y, K : 2 * K, :] = low
    for c, (dx, dy) in enumerate(CORNERS):
        x = 0 if dx < 0 else CX - 1
        y = 0 if dy < 0 else CY - 1
        side = 0 if dx < 0 else 1
        at = 7 if dx < 0 else 24
        own = frame_y[1, 0 if dy < 0 else 1, at : at + 1, :]
        value = jnp.zeros((K, NZ), f32)
        for oz in (-1, 0, 1):
            near = kz[oz + 1, x + 1, 8 + y : 9 + y, :]
            field = (zmx[side, y], zf[x + 1, y], zs[x + 1, y])[oz + 1]
            value = value - harmonic(own, near, (dx, dy, oz)) * field
        high, low = split(value)
        gc[c, 0:K, :] = high
        gc[c, K : 2 * K, :] = low
    own = frame_y[1, parity, 8:24, :]
    for i, (ox, oz) in enumerate(NINE):
        near = frame_own[oz + 1, parity, 8 + ox : 24 + ox, :]
        wy[i] = harmonic(own, near, (ox, 1, oz))

    def face(x, carry):
        value = jnp.zeros((K, NZ), f32)
        for i, (ox, oz) in enumerate(NINE):
            at = x + 1 + ox
            field = (zmy[at], zf[at, y_edge], zs[at, y_edge])[oz + 1]
            value = value - wy[i, pl.ds(x, 1), :] * field
        high, low = split(value)
        gy[x, 0:K, :] = high
        gy[x, K : 2 * K, :] = low
        return carry

    lax.fori_loop(0, CX, face, 0, unroll=CX)

    for copy in moves:
        copy.wait_recv()

    def meet(left, right):
        product = lax.dot_general(left, right, LAST, preferred_element_type=f32)
        return product[:K] + product[K:]

    blocks = {}
    for side, dx in ((0, -1), (1, 1)):
        blocks[(dx, 0)] = meet(
            jnp.concatenate([gx[side, y] for y in range(CY)], axis=1),
            jnp.concatenate([hx[side, y] for y in range(CY)], axis=1),
        )
    for c, region in enumerate(CORNERS):
        blocks[region] = meet(gc[c], hc[c])
    across = meet(
        jnp.concatenate([gy[x] for x in range(CX)], axis=1),
        jnp.concatenate([hy[x] for x in range(CX)], axis=1),
    )
    back = across.T
    none = jnp.zeros_like(back)
    rows = [
        jnp.concatenate(
            [blocks[(-1, -1)], blocks[(-1, 0)], blocks[(-1, 1)], across * (1.0 - parity_f)],
            axis=1,
        ),
        jnp.concatenate(
            [across * parity_f, blocks[(1, -1)], blocks[(1, 0)], blocks[(1, 1)]], axis=1
        ),
        jnp.concatenate([back * (1.0 - parity_f), none, none, back * parity_f], axis=1),
    ]
    for l, value in zip((0, 1, 3), rows):
        piece.reshape(4 * K, NZ)[pl.ds(l, K, stride=4), :] = value

    def pair(to):
        return lax.rem(to, 8) * 2 + to // RING

    for off in FAR:
        to = lax.rem(ay + off, COLS)
        pltpu.make_async_remote_copy(
            src_ref=piece.at[pair(to)],
            dst_ref=pieces.at[ay],
            send_sem=one_send,
            recv_sem=one_recv,
            device_id=(ax, to),
            device_id_type=MESH,
        ).start()
    keep = pltpu.make_async_copy(piece.at[pair(ay)], pieces.at[ay], local_sem.at[0])
    keep.start()
    keep.wait()
    many = pieces.at[pl.ds(0, COLS - 1)]
    pltpu.make_async_copy(many, many, one_recv).wait()

    got = pieces.reshape(8 * COLS, NZ)[...]
    high, low = split(got)
    both = jnp.dot(
        route[...], jnp.concatenate([high, low], axis=1), preferred_element_type=f32
    )
    slots[...] = (both[:, :NZ] + both[:, NZ:]).reshape(16, 16, NZ)

    half_row = ay // RING
    for d, f in NEAR:
        x_half = lax.rem(half_row + f, 2)
        to = x_half * RING + lax.rem(ay + d - 3 + RING, RING)
        pltpu.make_async_remote_copy(
            src_ref=slots.at[2 * d + x_half],
            dst_ref=owned.at[pair(ay)],
            send_sem=two_send,
            recv_sem=two_recv,
            device_id=(ax, to),
            device_id_type=MESH,
        ).start()
    keep = pltpu.make_async_copy(slots.at[6 + half_row], owned.at[pair(ay)], local_sem.at[1])
    keep.start()
    keep.wait()
    for copy in sends + moves:
        copy.wait_send()
    sent = pieces.at[pl.ds(0, COLS - 1)]
    pltpu.make_async_copy(sent, sent, one_send).wait()
    many = owned.at[pl.ds(0, 15)]
    pltpu.make_async_copy(many, many, two_recv).wait()
    keep = pltpu.make_async_copy(owned, out, local_sem.at[2])
    keep.start()
    sent = slots.at[pl.ds(0, 15)]
    pltpu.make_async_copy(sent, sent, two_send).wait()
    keep.wait()


def deal(owned, out_diag, out_coup):
    flat = owned.reshape(8 * K, NZ)
    for c in range(CAP):
        for half_row in range(2):
            value = flat[pl.ds(2 * c + half_row, K, stride=8), :]
            for q in range(4):
                out_coup[c, half_row * 4 + q] = value[:, q * K : (q + 1) * K]
    value = flat[pl.ds(6, K, stride=8), :]
    for c in range(CAP):
        out_diag[c] = value[:, c * K : (c + 1) * K]


def shards(basis, phase_ids, phase_stiffness, owner_map):
    f32, bf16 = jnp.float32, jnp.bfloat16
    vmem = pltpu.VMEM
    dma = pltpu.SemaphoreType.DMA
    whole = pl.BlockSpec(memory_space=pltpu.VMEM)
    owned = pl.pallas_call(
        kernel,
        out_shape=jax.ShapeDtypeStruct((16, 16, NZ), f32),
        in_specs=[pl.BlockSpec(memory_space=pltpu.HBM)] * 4,
        out_specs=pl.BlockSpec(memory_space=pltpu.HBM),
        scratch_shapes=[
            vmem((K * CX * CY, NZ), bf16),
            vmem((CX, CY, NZ), jnp.int32),
            vmem((1, 8), bf16),
            vmem((1, COLS), jnp.int32),
            vmem((K * PITCH, NZ), f32),
            vmem((CX + 2, CY, K, NZ), f32),
            vmem((CX + 2, CY, K, NZ), f32),
            vmem((CX, CY, K, NZ), bf16),
            vmem((2, CY, K, NZ), f32),
            vmem((CX + 2, K, NZ), f32),
            vmem((CX + 2, 24, NZ), f32),
            vmem((3, CX + 2, 24, NZ), f32),
            vmem((8, 8, NZ), f32),
            vmem((2, CX, NZ), f32),
            vmem((2, CX, NZ), f32),
            vmem((3, 2, 24, NZ), f32),
            vmem((3, 2, 32, NZ), f32),
            vmem((3, 2, 32, NZ), f32),
            vmem((2, CY, K, NZ), bf16),
            vmem((CX, K, NZ), bf16),
            vmem((4, K, NZ), bf16),
            vmem((13, CX, CY, NZ), f32),
            vmem((CX, CY, NZ), f32),
            vmem((2, 9, CY, NZ), f32),
            vmem((9, CX, NZ), f32),
            vmem((CX + 1, CY, 2 * K, NZ), bf16),
            vmem((2, CY, 2 * K, NZ), bf16),
            vmem((2, CX, 2 * K, NZ), bf16),
            vmem((2, CY, 2 * K, NZ), bf16),
            vmem((CX, 2 * K, NZ), bf16),
            vmem((4, 2 * K, NZ), bf16),
            vmem((256, 256), bf16),
            vmem((K, NZ), f32),
            vmem((16, 8, NZ), f32),
            vmem((COLS, 8, NZ), f32),
            vmem((16, 16, NZ), f32),
            vmem((16, 16, NZ), f32),
            dma((7,)),
            dma((8,)),
            dma((8,)),
            dma((7,)),
            dma((7,)),
            dma,
            dma,
            dma,
            dma,
            dma((3,)),
        ],
        compiler_params=pltpu.CompilerParams(
            collective_id=0, has_side_effects=True, vmem_limit_bytes=60 * 1024 * 1024
        ),
    )(
        basis.reshape(K * CX * CY, NZ),
        phase_ids,
        phase_stiffness.reshape(1, 8),
        owner_map,
    )
    diag, coup = pl.pallas_call(
        deal,
        out_shape=(
            jax.ShapeDtypeStruct((CAP, K, K), f32),
            jax.ShapeDtypeStruct((CAP, 8, K, K), f32),
        ),
        in_specs=[whole],
        out_specs=(whole, whole),
    )(owned)
    return diag[None], coup[None]


def solution(mesh):
    return jax.shard_map(
        shards,
        mesh=mesh,
        in_specs=(P(None, "gx", "gy", None), P("gx", "gy", None), P(), P("gx", None)),
        out_specs=(P("gx", "gy", None, None), P("gx", "gy", None, None, None)),
        check_vma=False,
    )
```

```python
import functools

import jax
import jax.numpy as jnp
from jax import lax
from jax.experimental import pallas as pl
from jax.experimental.pallas import tpu as pltpu
from jax.sharding import PartitionSpec as P

CAP = 3
REACT = 0.1
REGIONS = ((-1, -1), (-1, 0), (-1, 1), (0, -1), (0, 1), (1, -1), (1, 0), (1, 1))
CORNERS = ((-1, -1), (-1, 1), (1, -1), (1, 1))
OFFSETS = [
    (ox, oy, oz)
    for ox in (-1, 0, 1)
    for oy in (-1, 0, 1)
    for oz in (-1, 0, 1)
    if (ox, oy, oz) != (0, 0, 0)
]
HALF = [o for o in OFFSETS if o[2] == 1] + [(0, 1, 0), (1, -1, 0), (1, 0, 0), (1, 1, 0)]
MESH = pl.DeviceIdType.MESH
K, CX, CY, NZ = 32, 16, 8, 128
ROWS, COLS = 16, 32
PITCH = 136
FAR = sorted(range(1, COLS), key=lambda off: -min(off % 16, 16 - off % 16))
BEFORE = 8
RING = COLS // 2
NEAR = sorted(
    [(d, f) for d in range(8) for f in range(2) if (d, f) != (3, 0)], key=lambda t: -abs(t[0] - 3)
)
LAST = (((1,), (1,)), ((), ()))


def split(value):
    high = value.astype(jnp.bfloat16)
    low = (value - high.astype(jnp.float32)).astype(jnp.bfloat16)
    return high, low


def kernel(
    basis,
    ids_hbm,
    phase_hbm,
    owner_hbm,
    out,
    raw,
    ids,
    phase,
    owner,
    stage,
    zf,
    zs,
    zb,
    zmx,
    zmy,
    kp,
    kz,
    kx,
    ky,
    kface,
    frame_x,
    frame_y,
    frame_own,
    hx,
    hy,
    hc,
    weights,
    dsum,
    wx,
    wy,
    yb,
    ex,
    ey,
    gx,
    gy,
    gc,
    route,
    mine,
    piece,
    pieces,
    slots,
    owned,
    load_sem,
    ks_send,
    ks_recv,
    z_send,
    z_recv,
    one_send,
    one_recv,
    two_send,
    two_recv,
    local_sem,
):
    f32, bf16 = jnp.float32, jnp.bfloat16
    ax = lax.axis_index("gx")
    ay = lax.axis_index("gy")
    parity = lax.rem(ax, 2)
    parity_f = parity.astype(f32)

    def device(dx, dy):
        return (lax.rem(ax + dx + ROWS, ROWS), lax.rem(ay + dy + COLS, COLS))

    small = [
        pltpu.make_async_copy(ids_hbm, ids, load_sem.at[4]),
        pltpu.make_async_copy(phase_hbm, phase, load_sem.at[5]),
        pltpu.make_async_copy(owner_hbm, owner, load_sem.at[6]),
    ]
    loads = [
        pltpu.make_async_copy(
            basis.at[pl.ds(1024 * g, 1024)], raw.at[pl.ds(1024 * g, 1024)], load_sem.at[g]
        )
        for g in range(4)
    ]
    for copy in small + loads:
        copy.start()

    barrier = pltpu.get_barrier_semaphore()

    for off in FAR:
        pl.semaphore_signal(
            barrier, inc=1, device_id=(ax, lax.rem(ay + off, COLS)), device_id_type=MESH
        )
    for dx, dy in REGIONS:
        if dx != 0:
            pl.semaphore_signal(barrier, inc=1, device_id=device(dx, dy), device_id_type=MESH)

    kp[...] = jnp.zeros_like(kp)
    frame_own[...] = jnp.zeros_like(frame_own)
    frame_x[...] = jnp.zeros_like(frame_x)
    frame_y[...] = jnp.zeros_like(frame_y)
    zero = jnp.zeros((8, K, NZ), f32)
    for edge in (0, CX + 1):
        zf[edge] = zero
        zs[edge] = zero
    zmy[0] = zero[0]
    zmy[CX + 1] = zero[0]
    yb[0] = jnp.zeros((CY, 2 * K, NZ), bf16)

    for copy in small:
        copy.wait()
    table = phase[...].astype(f32)
    for x in range(CX):
        cell = ids[x]
        value = jnp.zeros((CY, NZ), f32)
        for p in range(8):
            value = jnp.where(cell == p, table[0:1, p : p + 1], value)
        kp[x + 1, 8:16, :] = value
    for side, y in ((0, 0), (1, CY - 1)):
        for x in range(CX):
            kface[side, x : x + 1, :] = kp[x + 1, 8 + y : 9 + y, :]

    for g in range(4):
        loads[g].wait()

        def widen(i, carry, g=g):
            at = pl.multiple_of(1024 * g + i * 128, 128)
            to = pl.multiple_of(PITCH * 8 * g + i * PITCH, 8)
            stage[pl.ds(to, 128), :] = raw[pl.ds(at, 128), :].astype(f32)
            return carry

        lax.fori_loop(0, 8, widen, 0)

    def turn(x, carry):
        for y in range(CY):
            r = x * CY + y
            slab = jnp.concatenate(
                [stage[pl.ds(8 * PITCH * g + r, 8, stride=PITCH), :] for g in range(4)], axis=0
            )
            zf[x + 1, y] = slab
            zs[x + 1, y] = pltpu.roll(slab, NZ - 1, 1)
            zb[x, y] = slab.astype(bf16)
        return carry

    lax.fori_loop(0, CX, turn, 0, unroll=4)

    def harmonic(own, near, o):
        coef = 2.0 / (9.0 * (o[0] * o[0] + o[1] * o[1] + o[2] * o[2]))
        return (coef * own) * near / jnp.maximum(own + near, 0.05)

    def below(value):
        lane = lax.broadcasted_iota(jnp.int32, value.shape, 1)
        return jnp.where(lane == 0, 0.0, pltpu.roll(value, 1, 1))

    def above(value):
        lane = lax.broadcasted_iota(jnp.int32, value.shape, 1)
        return jnp.where(lane == NZ - 1, 0.0, pltpu.roll(value, NZ - 1, 1))

    for x in range(CX + 2):
        row = kp[x]
        kz[0, x] = below(row)
        kz[1, x] = row
        kz[2, x] = above(row)

    def weigh(x, carry):
        own = kp[x + 1, 8:16, :]
        total = REACT * own
        for o in OFFSETS:
            near = kz[o[2] + 1, x + 1 + o[0], 8 + o[1] : 16 + o[1], :]
            weight = harmonic(own, near, o)
            if o in HALF:
                weights[HALF.index(o), x] = weight
            total = total + weight
        dsum[x] = 0.5 * total
        return carry

    lax.fori_loop(0, CX, weigh, 0, unroll=2)

    def contract(x, slot):
        left = jnp.concatenate([yb[slot, y] for y in range(CY)], axis=1)
        right = jnp.concatenate([zb[x, y] for y in range(CY)], axis=1)
        return lax.dot_general(left, right, LAST, preferred_element_type=f32)

    def interior(x, acc):
        acc = acc + contract(jnp.maximum(x - 1, 0), x)
        for y in range(CY):
            value = dsum[x, y : y + 1, :] * zf[x + 1, y]
            for i, (ox, oy, oz) in enumerate(HALF):
                if not 0 <= y + oy < CY:
                    continue
                field = zf if oz == 0 else zs
                w = weights[i, x, y : y + 1, :]
                value = value - w * field[x + 1 + ox, y + oy]
            high, low = split(value)
            yb[x + 1, y, 0:K, :] = high
            yb[x + 1, y, K : 2 * K, :] = low
        return acc

    y_edge = 7 * parity

    def lower(x, carry):
        zmy[x + 1] = pltpu.roll(zf[x + 1, y_edge], 1, 1)
        return carry

    lax.fori_loop(0, CX, lower, 0, unroll=4)

    for side in range(2):
        for y in range(CY):
            zmx[side, y] = pltpu.roll(zf[1 if side == 0 else CX, y], 1, 1)
    for side in range(2):
        frame_own[1, side, 8:24, :] = kface[side]
        row = frame_own[1, side]
        frame_own[0, side] = below(row)
        frame_own[2, side] = above(row)

    width = COLS
    own_row = jnp.broadcast_to(owner[...], (width, width))
    i_sub = lax.broadcasted_iota(jnp.int32, (width, width), 0)
    i_lane = lax.broadcasted_iota(jnp.int32, (width, width), 1)
    own_f = own_row.astype(f32)
    own_col = jnp.sum(jnp.where(i_sub == i_lane, own_f, 0.0), axis=1, keepdims=True)
    before = (own_col == own_f) & (i_sub < i_lane)
    rank = jnp.sum(jnp.where(before, 1.0, 0.0), axis=0, keepdims=True)
    code = jnp.broadcast_to(own_f[0:1] * 4.0 + rank, (8, width)).astype(bf16)
    wide_n = 8 * width
    e_sub = lax.broadcasted_iota(jnp.int32, (width, wide_n), 0)
    e_lane = lax.broadcasted_iota(jnp.int32, (width, wide_n), 1)
    step = 2 * parity - 1
    e_from = e_lane // 8 + jnp.where(e_lane % 4 == 3, step, 0)
    expand = jnp.where(e_from == e_sub, 1.0, 0.0).astype(bf16)
    wide = jnp.dot(code, expand, preferred_element_type=f32)[0:1].astype(jnp.int32)
    wide_owner = wide // 4
    wide_rank = wide - wide_owner * 4
    lane1 = lax.broadcasted_iota(jnp.int32, (1, wide_n), 1)
    part = lane1 % 4
    row = jnp.where(part == 2, 6, wide_rank * 2 + jnp.where(part == 3, 1 - parity, part))
    place = (wide_owner % RING - ay % RING + RING + 3) % RING
    target = place * 32 + (wide_owner // RING) * 16 + ((lane1 // 4) % 2) * 8 + row
    end = (lane1 // 8 + step < 0) | (lane1 // 8 + step >= width)
    target = jnp.where((place >= 8) | ((part == 3) & end), -1, target)
    p_sub = lax.broadcasted_iota(jnp.int32, (16 * 16, wide_n), 0)
    route[...] = jnp.where(p_sub == target, 1.0, 0.0).astype(bf16)
    my_rank = jnp.sum(
        jnp.where(lax.broadcasted_iota(jnp.int32, (1, width), 1) == ay, rank, 0.0),
        axis=1,
        keepdims=True,
    )
    quarter = (lax.broadcasted_iota(jnp.int32, (K, NZ), 1) // K).astype(f32)
    mine[...] = jnp.where(quarter == my_rank, 1.0 / (CX * CY * NZ), 0.0)

    acc = lax.fori_loop(0, BEFORE, interior, jnp.zeros((2 * K, K), f32), unroll=4)

    pl.semaphore_wait(barrier, COLS - 1 + 6)

    sends = []
    for i, (dx, dy) in enumerate(REGIONS):
        other = REGIONS.index((-dx, -dy))
        if dx == 0:
            src, dst = kface.at[0 if dy < 0 else 1], ky.at[0 if dy > 0 else 1]
        else:
            src, dst = kp.at[1 if dx < 0 else CX, pl.ds(8, 8), :], kx.at[other]
        sends.append(
            pltpu.make_async_remote_copy(
                src_ref=src,
                dst_ref=dst,
                send_sem=ks_send.at[i],
                recv_sem=ks_recv.at[other],
                device_id=device(dx, dy),
                device_id_type=MESH,
            )
        )
    moves = [
        pltpu.make_async_remote_copy(
            src_ref=zb.at[:, 7 - 7 * parity],
            dst_ref=hy,
            send_sem=z_send.at[0],
            recv_sem=z_recv.at[0],
            device_id=(ax, lax.rem(ay + 1 - 2 * parity + COLS, COLS)),
            device_id_type=MESH,
        )
    ]
    for side, dx in ((0, -1), (1, 1)):
        moves.append(
            pltpu.make_async_remote_copy(
                src_ref=zb.at[0 if dx < 0 else CX - 1],
                dst_ref=hx.at[1 - side],
                send_sem=z_send.at[1 + side],
                recv_sem=z_recv.at[2 - side],
                device_id=device(dx, 0),
                device_id_type=MESH,
            )
        )
    for c, (dx, dy) in enumerate(CORNERS):
        moves.append(
            pltpu.make_async_remote_copy(
                src_ref=zb.at[0 if dx < 0 else CX - 1, 0 if dy < 0 else CY - 1],
                dst_ref=hc.at[3 - c],
                send_sem=z_send.at[3 + c],
                recv_sem=z_recv.at[6 - c],
                device_id=device(dx, dy),
                device_id_type=MESH,
            )
        )
    for copy in sends + moves[3:] + moves[1:3] + moves[:1]:
        copy.start()

    acc = lax.fori_loop(BEFORE, CX, interior, acc, unroll=4)
    acc = acc + contract(CX - 1, CX)

    for copy in sends:
        copy.wait_recv()
    low_x = (ax > 0).astype(f32)
    high_x = (ax < ROWS - 1).astype(f32)
    low_y = (ay > 0).astype(f32)
    high_y = (ay < COLS - 1).astype(f32)
    for side, dx, keep in ((0, -1, low_x), (1, 1, high_x)):
        near = kx[REGIONS.index((dx, 0))] * keep
        frame_x[1, side, 8:16, :] = near
    for side, dy, keep in ((0, -1, low_y), (1, 1, high_y)):
        y = 7 if dy < 0 else 0
        frame_y[1, side, 8:24, :] = ky[side] * keep
        for at, dx, keep_x in ((7, -1, low_x), (24, 1, high_x)):
            corner = kx[REGIONS.index((dx, dy)), y : y + 1, :]
            frame_y[1, side, at : at + 1, :] = corner * (keep * keep_x)
    for frame in (frame_x, frame_y):
        for side in range(2):
            row = frame[1, side]
            frame[0, side] = below(row)
            frame[2, side] = above(row)

    NINE = [(i, j) for i in (-1, 0, 1) for j in (-1, 0, 1)]
    for side, dx in ((0, -1), (1, 1)):
        x = 0 if dx < 0 else CX - 1
        own = kp[x + 1, 8:16, :]
        total = jnp.zeros_like(own)
        for oy, oz in NINE:
            near = frame_x[oz + 1, side, 8 + oy : 16 + oy, :]
            total = total + harmonic(own, near, (dx, oy, oz))
        for y in range(CY):
            high, low = split(total[y : y + 1] * zf[x + 1, y])
            ex[side, y, 0:K, :] = high
            ex[side, y, K : 2 * K, :] = low
    for side, dy in ((0, -1), (1, 1)):
        own = kface[side]
        total = jnp.zeros_like(own)
        for ox, oz in NINE:
            near = frame_y[oz + 1, side, 8 + ox : 24 + ox, :]
            total = total + harmonic(own, near, (ox, dy, oz))
        for x in range(CX):
            high, low = split(total[x : x + 1] * zf[x + 1, 0 if dy < 0 else CY - 1])
            ey[side, x, 0:K, :] = high
            ey[side, x, K : 2 * K, :] = low
    outer = jnp.zeros((2 * K, K), f32)
    for side in range(2):
        x = 0 if side == 0 else CX - 1
        y = 0 if side == 0 else CY - 1
        outer = outer + lax.dot_general(
            jnp.concatenate([ex[side, i] for i in range(CY)], axis=1),
            jnp.concatenate([zb[x, i] for i in range(CY)], axis=1),
            LAST,
            preferred_element_type=f32,
        )
        outer = outer + lax.dot_general(
            jnp.concatenate([ey[side, i] for i in range(CX)], axis=1),
            jnp.concatenate([zb[i, y] for i in range(CX)], axis=1),
            LAST,
            preferred_element_type=f32,
        )
    half = acc[:K] + acc[K:]
    diagonal = half + half.T + outer[:K] + outer[K:]
    piece.reshape(4 * K, NZ)[pl.ds(2, K, stride=4), :] = mine[...] * jnp.concatenate(
        [diagonal] * 4, axis=1
    )

    for side, dx in ((0, -1), (1, 1)):
        x = 0 if dx < 0 else CX - 1
        own = frame_x[1, side, 8:16, :]
        for i, (oy, oz) in enumerate(NINE):
            near = kz[oz + 1, x + 1, 8 + oy : 16 + oy, :]
            wx[side, i] = harmonic(own, near, (dx, oy, oz))
        for y in range(CY):
            value = jnp.zeros((K, NZ), f32)
            for i, (oy, oz) in enumerate(NINE):
                if not 0 <= y + oy < CY:
                    continue
                field = (zmx[side, y + oy], zf[x + 1, y + oy], zs[x + 1, y + oy])[oz + 1]
                value = value - wx[side, i, y : y + 1, :] * field
            high, low = split(value)
            gx[side, y, 0:K, :] = high
            gx[side, y, K : 2 * K, :] = low
    for c, (dx, dy) in enumerate(CORNERS):
        x = 0 if dx < 0 else CX - 1
        y = 0 if dy < 0 else CY - 1
        side = 0 if dx < 0 else 1
        at = 7 if dx < 0 else 24
        own = frame_y[1, 0 if dy < 0 else 1, at : at + 1, :]
        value = jnp.zeros((K, NZ), f32)
        for oz in (-1, 0, 1):
            near = kz[oz + 1, x + 1, 8 + y : 9 + y, :]
            field = (zmx[side, y], zf[x + 1, y], zs[x + 1, y])[oz + 1]
            value = value - harmonic(own, near, (dx, dy, oz)) * field
        high, low = split(value)
        gc[c, 0:K, :] = high
        gc[c, K : 2 * K, :] = low
    own = frame_y[1, parity, 8:24, :]
    for i, (ox, oz) in enumerate(NINE):
        near = frame_own[oz + 1, parity, 8 + ox : 24 + ox, :]
        wy[i] = harmonic(own, near, (ox, 1, oz))

    def face(x, carry):
        value = jnp.zeros((K, NZ), f32)
        for i, (ox, oz) in enumerate(NINE):
            at = x + 1 + ox
            field = (zmy[at], zf[at, y_edge], zs[at, y_edge])[oz + 1]
            value = value - wy[i, pl.ds(x, 1), :] * field
        high, low = split(value)
        gy[x, 0:K, :] = high
        gy[x, K : 2 * K, :] = low
        return carry

    lax.fori_loop(0, CX, face, 0, unroll=CX)

    for copy in moves:
        copy.wait_recv()

    def meet(left, right):
        product = lax.dot_general(left, right, LAST, preferred_element_type=f32)
        return product[:K] + product[K:]

    blocks = {}
    for side, dx in ((0, -1), (1, 1)):
        blocks[(dx, 0)] = meet(
            jnp.concatenate([gx[side, y] for y in range(CY)], axis=1),
            jnp.concatenate([hx[side, y] for y in range(CY)], axis=1),
        )
    for c, region in enumerate(CORNERS):
        blocks[region] = meet(gc[c], hc[c])
    across = meet(
        jnp.concatenate([gy[x] for x in range(CX)], axis=1),
        jnp.concatenate([hy[x] for x in range(CX)], axis=1),
    )
    back = across.T
    none = jnp.zeros_like(back)
    rows = [
        jnp.concatenate(
            [blocks[(-1, -1)], blocks[(-1, 0)], blocks[(-1, 1)], across * (1.0 - parity_f)],
            axis=1,
        ),
        jnp.concatenate(
            [across * parity_f, blocks[(1, -1)], blocks[(1, 0)], blocks[(1, 1)]], axis=1
        ),
        jnp.concatenate([back * (1.0 - parity_f), none, none, back * parity_f], axis=1),
    ]
    for l, value in zip((0, 1, 3), rows):
        piece.reshape(4 * K, NZ)[pl.ds(l, K, stride=4), :] = value

    def pair(to):
        return lax.rem(to, 8) * 2 + to // RING

    for off in FAR:
        to = lax.rem(ay + off, COLS)
        pltpu.make_async_remote_copy(
            src_ref=piece.at[pair(to)],
            dst_ref=pieces.at[ay],
            send_sem=one_send,
            recv_sem=one_recv,
            device_id=(ax, to),
            device_id_type=MESH,
        ).start()
    keep = pltpu.make_async_copy(piece.at[pair(ay)], pieces.at[ay], local_sem.at[0])
    keep.start()
    keep.wait()
    many = pieces.at[pl.ds(0, COLS - 1)]
    pltpu.make_async_copy(many, many, one_recv).wait()

    got = pieces.reshape(8 * COLS, NZ)[...]
    high, low = split(got)
    both = jnp.dot(
        route[...], jnp.concatenate([high, low], axis=1), preferred_element_type=f32
    )
    slots[...] = (both[:, :NZ] + both[:, NZ:]).reshape(16, 16, NZ)

    half_row = ay // RING
    for d, f in NEAR:
        x_half = lax.rem(half_row + f, 2)
        to = x_half * RING + lax.rem(ay + d - 3 + RING, RING)
        pltpu.make_async_remote_copy(
            src_ref=slots.at[2 * d + x_half],
            dst_ref=owned.at[pair(ay)],
            send_sem=two_send,
            recv_sem=two_recv,
            device_id=(ax, to),
            device_id_type=MESH,
        ).start()
    keep = pltpu.make_async_copy(slots.at[6 + half_row], owned.at[pair(ay)], local_sem.at[1])
    keep.start()
    keep.wait()
    for copy in sends + moves:
        copy.wait_send()
    sent = pieces.at[pl.ds(0, COLS - 1)]
    pltpu.make_async_copy(sent, sent, one_send).wait()
    many = owned.at[pl.ds(0, 15)]
    pltpu.make_async_copy(many, many, two_recv).wait()
    keep = pltpu.make_async_copy(owned, out, local_sem.at[2])
    keep.start()
    sent = slots.at[pl.ds(0, 15)]
    pltpu.make_async_copy(sent, sent, two_send).wait()
    keep.wait()


def deal(owned, out_diag, out_coup):
    flat = owned.reshape(8 * K, NZ)
    for c in range(CAP):
        for half_row in range(2):
            value = flat[pl.ds(2 * c + half_row, K, stride=8), :]
            for q in range(4):
                out_coup[c, half_row * 4 + q] = value[:, q * K : (q + 1) * K]
    value = flat[pl.ds(6, K, stride=8), :]
    for c in range(CAP):
        out_diag[c] = value[:, c * K : (c + 1) * K]


def shards(basis, phase_ids, phase_stiffness, owner_map):
    f32, bf16 = jnp.float32, jnp.bfloat16
    vmem = pltpu.VMEM
    dma = pltpu.SemaphoreType.DMA
    whole = pl.BlockSpec(memory_space=pltpu.VMEM)
    owned = pl.pallas_call(
        kernel,
        out_shape=jax.ShapeDtypeStruct((16, 16, NZ), f32),
        in_specs=[pl.BlockSpec(memory_space=pltpu.HBM)] * 4,
        out_specs=pl.BlockSpec(memory_space=pltpu.HBM),
        scratch_shapes=[
            vmem((K * CX * CY, NZ), bf16),
            vmem((CX, CY, NZ), jnp.int32),
            vmem((1, 8), bf16),
            vmem((1, COLS), jnp.int32),
            vmem((K * PITCH, NZ), f32),
            vmem((CX + 2, CY, K, NZ), f32),
            vmem((CX + 2, CY, K, NZ), f32),
            vmem((CX, CY, K, NZ), bf16),
            vmem((2, CY, K, NZ), f32),
            vmem((CX + 2, K, NZ), f32),
            vmem((CX + 2, 24, NZ), f32),
            vmem((3, CX + 2, 24, NZ), f32),
            vmem((8, 8, NZ), f32),
            vmem((2, CX, NZ), f32),
            vmem((2, CX, NZ), f32),
            vmem((3, 2, 24, NZ), f32),
            vmem((3, 2, 32, NZ), f32),
            vmem((3, 2, 32, NZ), f32),
            vmem((2, CY, K, NZ), bf16),
            vmem((CX, K, NZ), bf16),
            vmem((4, K, NZ), bf16),
            vmem((13, CX, CY, NZ), f32),
            vmem((CX, CY, NZ), f32),
            vmem((2, 9, CY, NZ), f32),
            vmem((9, CX, NZ), f32),
            vmem((CX + 1, CY, 2 * K, NZ), bf16),
            vmem((2, CY, 2 * K, NZ), bf16),
            vmem((2, CX, 2 * K, NZ), bf16),
            vmem((2, CY, 2 * K, NZ), bf16),
            vmem((CX, 2 * K, NZ), bf16),
            vmem((4, 2 * K, NZ), bf16),
            vmem((256, 256), bf16),
            vmem((K, NZ), f32),
            vmem((16, 8, NZ), f32),
            vmem((COLS, 8, NZ), f32),
            vmem((16, 16, NZ), f32),
            vmem((16, 16, NZ), f32),
            dma((7,)),
            dma((8,)),
            dma((8,)),
            dma((7,)),
            dma((7,)),
            dma,
            dma,
            dma,
            dma,
            dma((3,)),
        ],
        compiler_params=pltpu.CompilerParams(
            collective_id=0, has_side_effects=True, vmem_limit_bytes=60 * 1024 * 1024
        ),
    )(
        basis.reshape(K * CX * CY, NZ),
        phase_ids,
        phase_stiffness.reshape(1, 8),
        owner_map,
    )
    diag, coup = pl.pallas_call(
        deal,
        out_shape=(
            jax.ShapeDtypeStruct((CAP, K, K), f32),
            jax.ShapeDtypeStruct((CAP, 8, K, K), f32),
        ),
        in_specs=[whole],
        out_specs=(whole, whole),
    )(owned)
    return diag[None], coup[None]


def solution(mesh):
    return jax.shard_map(
        shards,
        mesh=mesh,
        in_specs=(P(None, "gx", "gy", None), P("gx", "gy", None), P(), P("gx", None)),
        out_specs=(P("gx", "gy", None, None), P("gx", "gy", None, None, None)),
        check_vma=False,
    )
```
